256 devices in a mesh: tm: 16 (over y, z_hi, core), sx: 4 (over x), sy: 4 (over z_lo).
Axes of the slice: x: 4, y: 4, z: 8 (z_hi: 2, z_lo: 4; z = z_hi * 4 + z_lo), core: 2. Of those that a mesh axis runs over, the one named last changes fastest.
Arguments:
- forcing: float32 [2, 32, 1024, 1024], P(None, 'tm', 'sx', 'sy'), may hold values from -6 to 6
- initial: float32 [2, 1024, 1024], P(None, 'sx', 'sy'), may hold values from -6 to 6
- previous_last: float32 [2, 1024, 1024], P(None, 'sx', 'sy'), may hold values from -16 to 16
- cell_class: int32 [1024, 1024], P('sx', 'sy'), may hold values from 0 to 7
- courant_table: float32 [8], replicated, may hold values from 0.02 to 0.25
Outputs:
- next_iterate: float32 [2, 32, 1024, 1024], P(None, 'tm', 'sx', 'sy')
The draws below stay inside these ranges and needn't reach their ends.
All inputs are finite; a program needn't handle non-finite values.
Results may differ from the reference program's by a relative error of at most 0.00019.
Values sent between devices are 32-bit elements; how exact they have to be, the bound alone decides.
No kernel may reach another device: no remote copies, remote signals or barrier semaphores. Data moves between devices by JAX's collectives and lax.ppermute only.
A program may use at most 64 MiB of HBM per device.

```python
import math
import jax
import jax.numpy as jnp
from jax import lax

STEPS = 32
SWEEPS = 8
CLASSES = 8
NX = 1024
NY = 1024


def touch_ends(drawn, rng, smallest, largest):
    place = [jax.random.randint(jax.random.fold_in(rng, axis), (), 0, length) for axis, length in enumerate(drawn.shape)]
    longest = drawn.shape.index(max(drawn.shape))
    neighbour = place[:longest] + [(place[longest] + 1) % drawn.shape[longest]] + place[longest + 1:]
    return drawn.at[tuple(place)].set(smallest).at[tuple(neighbour)].set(largest)


def levels(rng, shape, pieces, smallest, largest):
    gain, own = 1.0, jax.random.fold_in(rng, 6)
    for dim, parts in pieces:
        heights = jnp.exp(jax.random.uniform(jax.random.fold_in(own, dim), (parts,), jnp.float32, smallest / len(pieces), largest / len(pieces)))
        gain = gain * jnp.repeat(heights, shape[dim] // parts).reshape([-1 if axis == dim else 1 for axis in range(len(shape))])
    return gain


def scatter_about(stream_key, extent, spread, reach, shards=(), kind=jnp.bfloat16):
    gain = levels(stream_key, extent, shards, -0.22, 0.18) if shards else 1.0
    drawn = jax.random.normal(stream_key, extent, jnp.float32) * spread * gain
    return jnp.minimum(jnp.maximum(drawn, -reach), reach).astype(kind)


def setup_inputs(seed: int = 0) -> dict:
    streams_of = jax.random.split(jax.random.key(seed), 6)
    forcing = scatter_about(streams_of[0], (2, STEPS, NX, NY), 1.0, 6.0, ((1, 16), (2, 4), (3, 4)), jnp.float32)
    initial = scatter_about(streams_of[1], (2, NX, NY), 1.0, 6.0, ((1, 4), (2, 4)), jnp.float32)
    previous_last = scatter_about(streams_of[2], (2, NX, NY), 4.0, 16.0, ((1, 4), (2, 4)), jnp.float32)
    cell_class = touch_ends(jax.random.randint(streams_of[3], (NX, NY), 0, CLASSES), jax.random.fold_in(streams_of[3], 1), 0, CLASSES - 1).astype(jnp.int32)
    courant_table = jnp.clip(jnp.exp(jax.random.uniform(streams_of[4], (CLASSES,), jnp.float32, math.log(0.02), math.log(0.25))), 0.02, 0.25)
    return dict(forcing=forcing, initial=initial, previous_last=previous_last, cell_class=cell_class, courant_table=courant_table)


circulant_alpha = 0.1


def reference(forcing, initial, previous_last, cell_class, courant_table):
    right = forcing.at[:, 0].add(initial - circulant_alpha * previous_last)
    decay_log = math.log(circulant_alpha) / STEPS
    steps = jnp.arange(STEPS).astype(jnp.float32)
    weighted = right * jnp.exp(steps * decay_log)[None, :, None, None]
    spectrum = jnp.fft.fft(weighted, axis=1)
    courant = courant_table[cell_class]
    phase = 2.0 * math.pi * steps / STEPS
    factor = math.exp(decay_log)
    lam = (1.0 - factor * jnp.cos(phase)) + 1j * (factor * jnp.sin(phase))

    def solve(item):
        spec_u, spec_w, lam_one = item
        g = spec_w + lam_one * spec_u
        inverse = 1.0 / (lam_one * lam_one + 4.0 * courant)
        field = g * inverse
        for sweep in range(SWEEPS - 1):
            padded = jnp.pad(field, 1)
            beside = padded[2:, 1:-1] + padded[:-2, 1:-1] + padded[1:-1, 2:] + padded[1:-1, :-2]
            field = (g + courant * beside) * inverse
        return field, lam_one * field - spec_u

    fields, velocity = lax.map(solve, (spectrum[0], spectrum[1], lam))
    solved = jnp.stack((fields, velocity))
    back = jnp.real(jnp.fft.ifft(solved, axis=1))
    return back * jnp.exp(-steps * decay_log)[None, :, None, None]
```

```python
import functools
import math

import jax
import jax.numpy as jnp
import numpy as np
from jax import lax
from jax.experimental import pallas as pl
from jax.experimental.pallas import tpu as pltpu
from jax.sharding import PartitionSpec as P

STEPS = 32
SWEEPS = 8
ALPHA = 0.1
DECAY = math.log(ALPHA) / STEPS
FACTOR = math.exp(DECAY)
AXES = ("tm", "sx", "sy")


def flat(tm, sx, sy):
    return (tm * 4 + sx) * 4 + sy


def device_of(row, col):
    row, col = row % 16, col % 16
    sx, upper, core = row // 4, row // 2 % 2, row % 2
    sy, quarter = col // 4, col % 4
    y = quarter ^ (3 * (sy & 1))
    z = upper ^ (sx & 1)
    return flat(y * 4 + z * 2 + core, sx, sy)


def pairs_of(move):
    return [
        (device_of(row, col), device_of(*move(row, col))) for row in range(16) for col in range(16)
    ]


TO_RIGHT = pairs_of(lambda row, col: (row, col + 1))
TO_LEFT = pairs_of(lambda row, col: (row, col - 1))
TO_CORE = pairs_of(lambda row, col: (row ^ 1, col))
TO_CROSS = pairs_of(lambda row, col: (row - 1 if row % 2 == 0 else row + 1, col))


def lanes(rows):
    return lax.broadcasted_iota(jnp.int32, (rows, 128), 1)


def half_turn(value):
    return pltpu.roll(value, 64, 1)


def pack_left(value, low):
    return jnp.where(low, value[:32], half_turn(value[32:]))


def pack_right(value, low):
    return jnp.where(low, half_turn(value[:32]), value[32:])


def slot_of(info, quarter, upper, core):
    return (quarter ^ info[1]) * 4 + (upper ^ info[2]) * 2 + core


def prepare_kernel(info, weight, forcing, initial, last, out):
    block = pl.program_id(0)
    upper, core = block >> 1, block & 1
    low = lanes(32) < 64
    first = weight[3]
    for side in range(2):
        cols = slice(128 * side, 128 * side + 128)
        first_u = forcing[0, 0, :, cols] + first * (initial[0, :, cols] - ALPHA * last[0, :, cols])
        first_w = forcing[1, 0, :, cols] + first * (initial[1, :, cols] - ALPHA * last[1, :, cols])
        second_u = forcing[0, 1, :, cols]
        second_w = forcing[1, 1, :, cols]
        units = (
            weight[0] * (first_w + first_u),
            weight[1] * (second_w + second_u - first_u),
            -weight[2] * second_u,
        )
        left = slot_of(info, 2 * side, upper, core)
        right = slot_of(info, 2 * side + 1, upper, core)
        for k, unit in enumerate(units):
            out[left, 32 * k : 32 * k + 32, :] = pack_left(unit, low)
            out[right, 32 * k : 32 * k + 32, :] = pack_right(unit, low)


def prepare(info, weight, forcing, initial, last):
    return pl.pallas_call(
        prepare_kernel,
        grid=(4,),
        in_specs=[
            pl.BlockSpec(memory_space=pltpu.SMEM),
            pl.BlockSpec(memory_space=pltpu.SMEM),
            pl.BlockSpec((2, 2, 64, 256), lambda i: (0, 0, i, 0)),
            pl.BlockSpec((2, 64, 256), lambda i: (0, i, 0)),
            pl.BlockSpec((2, 64, 256), lambda i: (0, i, 0)),
        ],
        out_specs=pl.BlockSpec((16, 96, 128), lambda i: (0, 0, 0)),
        out_shape=jax.ShapeDtypeStruct((16, 96, 128), jnp.float32),
        name="prepare",
    )(info, weight, forcing, initial, last)


def scaled(factor, value):
    if abs(factor) < 1e-12:
        return None
    if abs(factor - 1.0) < 1e-12:
        return value
    if abs(factor + 1.0) < 1e-12:
        return -value
    return np.float32(factor) * value


def total_of(terms):
    terms = [term for term in terms if term is not None]
    result = terms[0]
    for term in terms[1:]:
        result = result + term
    return result


def angle(index):
    return 2.0 * math.pi * (index % STEPS) / STEPS


def forward(steps):
    even = [steps[0]] + [steps[n] + steps[32 - n] for n in range(1, 16)] + [steps[16]]
    odd = [None] + [steps[n] - steps[32 - n] for n in range(1, 16)]
    planes = [None] * 32
    for j in range(9):
        cos_even = total_of([scaled(math.cos(angle(j * n)), even[n]) for n in range(0, 17, 2)])
        cos_odd = (
            None if j == 8 else total_of([scaled(math.cos(angle(j * n)), even[n]) for n in range(1, 17, 2)])
        )
        high, lowp = (
            (cos_even, None) if cos_odd is None else (cos_even + cos_odd, cos_even - cos_odd)
        )
        if j == 0:
            planes[0], planes[1] = high, lowp
            continue
        planes[2 * j] = high
        if j < 8:
            planes[2 * (16 - j)] = lowp
        sin_odd = total_of([scaled(math.sin(angle(j * n)), odd[n]) for n in range(1, 16, 2)])
        if j == 8:
            planes[2 * j + 1] = -sin_odd
            continue
        sin_even = total_of([scaled(math.sin(angle(j * n)), odd[n]) for n in range(2, 16, 2)])
        planes[2 * j + 1] = -(sin_even + sin_odd)
        planes[2 * (16 - j) + 1] = sin_even - sin_odd
    return planes


def backward(planes):
    real = [planes[0]] + [planes[2 * j] * 2.0 for j in range(1, 16)] + [planes[1]]
    imag = [None] + [planes[2 * j + 1] * 2.0 for j in range(1, 16)]
    steps = [None] * 32

    def put(n, cosine, sine):
        if n in (0, 16):
            steps[n] = cosine
            return
        steps[n] = cosine - sine
        steps[32 - n] = cosine + sine

    for n in range(9):
        cos_even = total_of([scaled(math.cos(angle(j * n)), real[j]) for j in range(0, 17, 2)])
        if n == 8:
            sine = total_of([scaled(math.sin(angle(j * n)), imag[j]) for j in range(1, 16, 2)])
            put(8, cos_even, sine)
            continue
        cos_odd = total_of([scaled(math.cos(angle(j * n)), real[j]) for j in range(1, 17, 2)])
        if n == 0:
            put(0, cos_even + cos_odd, None)
            put(16, cos_even - cos_odd, None)
            continue
        sin_odd = total_of([scaled(math.sin(angle(j * n)), imag[j]) for j in range(1, 16, 2)])
        sin_even = total_of([scaled(math.sin(angle(j * n)), imag[j]) for j in range(2, 16, 2)])
        put(n, cos_even + cos_odd, sin_even + sin_odd)
        put(16 - n, cos_even - cos_odd, sin_odd - sin_even)
    return steps


def transform_kernel(info, table, cell_class, received, planes_out, left_out, right_out, core_out, cross_out):
    upper, core, quarter = info[3], info[4], info[5]
    low8 = lanes(8) < 64
    lane8 = lanes(8) % 64
    row0 = pl.multiple_of((upper * 2 + core) * 64, 64)
    col0 = pl.multiple_of((quarter >> 1) * 128, 128)
    classes = cell_class[pl.ds(row0, 64), pl.ds(col0, 128)]
    courant = jnp.zeros(classes.shape, jnp.float32)
    for k in range(8):
        courant = jnp.where(classes == k, table[k], courant)
    courant = jnp.where((quarter & 1) == 1, half_turn(courant), courant)
    courant = pack_left(courant, lanes(32) < 64)
    planes_out[32] = courant
    for r in range(4):
        rows = slice(8 * r, 8 * r + 8)
        steps = []
        for t in range(16):
            steps.append(received[t, 8 * r : 8 * r + 8, :] + received[(t + 15) % 16, 64 + 8 * r : 72 + 8 * r, :])
            steps.append(received[t, 32 + 8 * r : 40 + 8 * r, :])
        planes = forward(steps)
        for p in range(32):
            planes_out[p, rows, :] = planes[p]
        planes = planes + [courant[rows]]
        for g in range(5):
            left = jnp.zeros((8, 128), jnp.float32)
            right = left
            for m, plane in enumerate(planes[8 * g : 8 * g + 8]):
                here = (lane8 >= 8 * m) & (lane8 < 8 * m + 8)
                left = jnp.where(here, pltpu.roll(plane, 8 * m, 1) if m else plane, left)
                right = jnp.where(here, pltpu.roll(plane, (8 * m - 56) % 128, 1), right)
            left_out[g, rows, :] = left
            right_out[g, rows, :] = right
        planes = planes + [planes[-1]]
        if r == 0:
            for j in range(17):
                top = jnp.where(low8, planes[2 * j], half_turn(planes[2 * j + 1]))

                @pl.when(core == 0)
                def _():
                    cross_out[j] = top

                @pl.when(core == 1)
                def _():
                    core_out[j] = top

        if r == 3:
            for j in range(17):
                bottom = jnp.where(low8, half_turn(planes[2 * j]), planes[2 * j + 1])

                @pl.when(core == 0)
                def _():
                    core_out[j] = bottom

                @pl.when(core == 1)
                def _():
                    cross_out[j] = bottom


def transform(info, table, cell_class, received):
    shapes = ((33, 32, 128), (5, 32, 128), (5, 32, 128), (17, 8, 128), (17, 8, 128))
    return pl.pallas_call(
        transform_kernel,
        in_specs=[
            pl.BlockSpec(memory_space=pltpu.SMEM),
            pl.BlockSpec(memory_space=pltpu.SMEM),
            pl.BlockSpec(memory_space=pltpu.VMEM),
            pl.BlockSpec(memory_space=pltpu.VMEM),
        ],
        out_specs=[pl.BlockSpec(memory_space=pltpu.VMEM)] * 5,
        out_shape=[jax.ShapeDtypeStruct(shape, jnp.float32) for shape in shapes],
        name="transform",
    )(info, table, cell_class, received)


def around(value):
    rows = value.shape[0]
    return (
        pltpu.roll(value, 1, 0)
        + pltpu.roll(value, rows - 1, 0)
        + pltpu.roll(value, 1, 1)
        + pltpu.roll(value, 127, 1)
    )


def solve_kernel(info, lam, planes, from_left, from_right, from_core, from_cross, out, solved):
    core, row0, col0 = info[4], info[6], info[7]
    low = lanes(32) < 64
    lane32 = lanes(32)
    lane8 = lanes(8)
    is_lower = core == 1

    def halo(index):
        return (
            jnp.where(is_lower, from_core[index], from_cross[index]),
            jnp.where(is_lower, from_cross[index], from_core[index]),
        )

    def turn(value, shift):
        return pltpu.roll(value, shift & 127 if isinstance(shift, int) else lax.rem(shift + 256, 128), 1)

    def merged(lane, centre, right, left):
        value = jnp.where(lane < 64, centre, right)
        return jnp.where(lane < 72, value, jnp.where(lane >= 120, left, 0.0))

    def extended(p, pair, odd, group, offset):
        centre = planes[p]
        right, left = from_right[group], from_left[group]
        top_main, bottom_main = halo(pair)
        if odd:
            top_main, bottom_main = half_turn(top_main), half_turn(bottom_main)
        top_left, bottom_left = halo(17 + group)
        top_right, bottom_right = halo(22 + group)
        return jnp.concatenate(
            [
                merged(lane8, top_main, turn(top_right, -offset), turn(top_left, 56 - offset)),
                merged(lane32, centre, turn(right, 64 - offset), turn(left, 120 - offset)),
                merged(lane32, half_turn(centre), turn(right, -offset), turn(left, 56 - offset)),
                merged(lane8, bottom_main, turn(bottom_right, 64 - offset), turn(bottom_left, 120 - offset)),
            ],
            axis=0,
        )

    def packed(value):
        return jnp.where(low, value[8:40], half_turn(value[40:72]))

    rows = lax.broadcasted_iota(jnp.int32, (80, 128), 0) - 8 + row0
    lane80 = lanes(80)
    cols = jnp.where(lane80 >= 120, lane80 - 128, lane80) + col0
    inside = (rows >= 0) & (rows < 1024) & (cols >= 0) & (cols < 1024) & ((lane80 < 72) | (lane80 >= 120))
    courant = jnp.where(inside, extended(32, 16, False, 4, 0), 0.0)
    inner = jnp.where(inside, 1.0, 0.0)

    for p in range(2):
        g = extended(p, 0, p == 1, 0, 8 * p)
        inverse = inner / (lam[0, p] + 4.0 * courant)
        field = g * inverse
        for _ in range(SWEEPS - 1):
            field = (g + courant * around(field)) * inverse
        solved[p] = packed(field)

    def frequency(j, carry):
        group, offset = j >> 2, (j & 3) * 16
        g_re = extended(2 * j, j, False, group, offset)
        g_im = extended(2 * j + 1, j, True, group, offset + 8)
        diag_re = lam[j, 0] + 4.0 * courant
        diag_im = lam[j, 1]
        scale = inner / (diag_re * diag_re + diag_im * diag_im)
        inv_re = diag_re * scale
        inv_im = -diag_im * scale
        re = g_re * inv_re - g_im * inv_im
        im = g_re * inv_im + g_im * inv_re
        for _ in range(SWEEPS - 1):
            all_re = g_re + courant * around(re)
            all_im = g_im + courant * around(im)
            re = all_re * inv_re - all_im * inv_im
            im = all_re * inv_im + all_im * inv_re
        solved[2 * j] = packed(re)
        solved[2 * j + 1] = packed(im)
        return carry

    lax.fori_loop(1, 16, frequency, 0)

    for r in range(4):
        part = slice(8 * r, 8 * r + 8)
        steps = backward([solved[p, part, :] for p in range(32)])
        for n in range(32):
            value = steps[n] * np.float32(math.exp(-n * DECAY) / STEPS)
            t, second = n // 2, n % 2
            out[t, 32 + 32 * second + 8 * r : 40 + 32 * second + 8 * r, :] = value
            if second:
                before = value * np.float32(ALPHA) if n == 31 else value
                out[(t + 1) % 16, part, :] = before


def solve(info, lam, planes, from_left, from_right, from_core, from_cross):
    return pl.pallas_call(
        solve_kernel,
        in_specs=[pl.BlockSpec(memory_space=pltpu.SMEM)] * 2
        + [pl.BlockSpec(memory_space=pltpu.VMEM)] * 5,
        out_specs=pl.BlockSpec(memory_space=pltpu.VMEM),
        out_shape=jax.ShapeDtypeStruct((16, 96, 128), jnp.float32),
        scratch_shapes=[pltpu.VMEM((32, 32, 128), jnp.float32)],
        name="solve",
    )(info, lam, planes, from_left, from_right, from_core, from_cross)


def finish_kernel(info, weight, received, forcing, initial, last, out):
    block = pl.program_id(0)
    upper, core = block >> 1, block & 1
    low = lanes(32) < 64
    first = weight[3]
    for side in range(2):
        cols = slice(128 * side, 128 * side + 128)
        left = slot_of(info, 2 * side, upper, core)
        right = slot_of(info, 2 * side + 1, upper, core)
        for half in range(2):
            rows = slice(32 * half, 32 * half + 32)
            values = []
            for k in range(3):
                one = received[left, 32 * k : 32 * k + 32, :]
                two = received[right, 32 * k : 32 * k + 32, :]
                if half == 0:
                    values.append(jnp.where(low, one, half_turn(two)))
                else:
                    values.append(jnp.where(low, half_turn(one), two))
            before, now, after = values
            start = forcing[0, 0, rows, cols] + first * (
                initial[0, rows, cols] - ALPHA * last[0, rows, cols]
            )
            out[0, 0, rows, cols] = now
            out[0, 1, rows, cols] = after
            out[1, 0, rows, cols] = now - before - start
            out[1, 1, rows, cols] = after - now - forcing[0, 1, rows, cols]


def finish(info, weight, received, forcing, initial, last):
    return pl.pallas_call(
        finish_kernel,
        grid=(4,),
        in_specs=[
            pl.BlockSpec(memory_space=pltpu.SMEM),
            pl.BlockSpec(memory_space=pltpu.SMEM),
            pl.BlockSpec((16, 96, 128), lambda i: (0, 0, 0)),
            pl.BlockSpec((1, 2, 64, 256), lambda i: (0, 0, i, 0)),
            pl.BlockSpec((1, 64, 256), lambda i: (0, i, 0)),
            pl.BlockSpec((1, 64, 256), lambda i: (0, i, 0)),
        ],
        out_specs=pl.BlockSpec((2, 2, 64, 256), lambda i: (0, 0, i, 0)),
        out_shape=jax.ShapeDtypeStruct((2, 2, 256, 256), jnp.float32),
        name="finish",
    )(info, weight, received, forcing, initial, last)


def lam_squares():
    rows = []
    for j in range(16):
        lam = 1.0 - FACTOR * complex(math.cos(angle(j)), -math.sin(angle(j)))
        square = lam * lam
        rows.append((square.real, square.imag))
    rows[0] = ((1.0 - FACTOR) ** 2, (1.0 + FACTOR) ** 2)
    return np.array(rows, np.float32)


def per_device(forcing, initial, previous_last, cell_class, courant_table):
    tm, sx, sy = (lax.axis_index(axis) for axis in AXES)
    flip_y, flip_z = 3 * (sy & 1), sx & 1
    upper, core, quarter = (tm >> 1 & 1) ^ flip_z, tm & 1, (tm >> 2) ^ flip_y
    row0 = sx * 256 + upper * 128 + core * 64
    col0 = sy * 256 + quarter * 64
    info = jnp.stack([tm, flip_y, flip_z, upper, core, quarter, row0, col0]).astype(jnp.int32)
    powers = jnp.asarray(np.exp(DECAY * np.arange(STEPS + 1)), jnp.float32)
    weight = jnp.concatenate(
        [
            lax.dynamic_slice_in_dim(powers, 2 * tm, 3),
            jnp.where(tm == 0, 1.0, 0.0).astype(jnp.float32)[None],
        ]
    )
    lam = jnp.asarray(lam_squares())
    pieces = prepare(info, weight, forcing, initial, previous_last)
    received = lax.all_to_all(pieces, "tm", 0, 0, tiled=True)
    planes, left, right, to_core, to_cross = transform(info, courant_table, cell_class, received)
    from_left = lax.ppermute(right, AXES, TO_RIGHT)
    from_right = lax.ppermute(left, AXES, TO_LEFT)

    def strip(main, start):
        corners = [
            lax.dynamic_slice_in_dim(value, start, 8, axis=1) for value in (from_left, from_right)
        ]
        return jnp.concatenate([main] + corners, axis=0)

    from_core = lax.ppermute(strip(to_core, 24 * (1 - core)), AXES, TO_CORE)
    from_cross = lax.ppermute(strip(to_cross, 24 * core), AXES, TO_CROSS)
    solved = solve(info, lam, planes, from_left, from_right, from_core, from_cross)
    returned = lax.all_to_all(solved, "tm", 0, 0, tiled=True)
    return finish(info, weight, returned, forcing, initial, previous_last)


def solution(mesh):
    in_specs = (
        P(None, "tm", "sx", "sy"),
        P(None, "sx", "sy"),
        P(None, "sx", "sy"),
        P("sx", "sy"),
        P(),
    )
    out_specs = P(None, "tm", "sx", "sy")
    return jax.shard_map(
        per_device, mesh=mesh, in_specs=in_specs, out_specs=out_specs, check_vma=False
    )
```

```python
import math

import jax
import jax.numpy as jnp
import numpy as np
from jax import lax
from jax.experimental import pallas as pl
from jax.experimental.pallas import tpu as pltpu
from jax.sharding import PartitionSpec as P

STEPS = 32
SWEEPS = 8
BATCH = 4
ALPHA = 0.1
DECAY = math.log(ALPHA) / STEPS
FACTOR = math.exp(DECAY)
AXES = ("tm", "sx", "sy")
VMEM = 16 * 2**20


def flat(tm, sx, sy):
    return (tm * 4 + sx) * 4 + sy


def device_of(row, col):
    row, col = row % 16, col % 16
    sx, upper, core = row // 4, row // 2 % 2, row % 2
    sy, quarter = col // 4, col % 4
    y = quarter ^ (3 * (sy & 1))
    z = upper ^ (sx & 1)
    return flat(y * 4 + z * 2 + core, sx, sy)


def pairs_of(move):
    return [
        (device_of(row, col), device_of(*move(row, col))) for row in range(16) for col in range(16)
    ]


TO_RIGHT = pairs_of(lambda row, col: (row, col + 1))
TO_LEFT = pairs_of(lambda row, col: (row, col - 1))
TO_CORE = pairs_of(lambda row, col: (row ^ 1, col))
TO_CROSS = pairs_of(lambda row, col: (row - 1 if row % 2 == 0 else row + 1, col))


def lanes(rows):
    return lax.broadcasted_iota(jnp.int32, (rows, 128), 1)


def half_turn(value):
    return pltpu.roll(value, 64, 1)


def pack_left(value, low):
    return jnp.where(low, value[:32], half_turn(value[32:]))


def pack_right(value, low):
    return jnp.where(low, half_turn(value[:32]), value[32:])


def place():
    tm, sx, sy = (lax.axis_index(axis) for axis in AXES)
    flip_y, flip_z = 3 * (sy & 1), sx & 1
    upper, core, quarter = (tm >> 1 & 1) ^ flip_z, tm & 1, (tm >> 2) ^ flip_y
    row0 = sx * 256 + upper * 128 + core * 64
    col0 = sy * 256 + quarter * 64
    return tm, flip_y, flip_z, upper, core, quarter, row0, col0


def params():
    return pltpu.CompilerParams(vmem_limit_bytes=VMEM)


def prepare_kernel(forcing, initial, last, out):
    tm, flip_y, flip_z = place()[:3]
    low = lanes(32) < 64
    first = jnp.where(tm == 0, 1.0, 0.0).astype(jnp.float32)
    weight = jnp.float32(1.0)
    for bit in range(4):
        weight = weight * jnp.where((tm >> bit & 1) == 1, math.exp(DECAY * 2 ** (bit + 1)), 1.0).astype(jnp.float32)
    weight_two = weight * np.float32(FACTOR)
    weight_three = weight * np.float32(-FACTOR * FACTOR)
    for upper in range(2):
        for side in range(2):
            cols = slice(128 * side, 128 * side + 128)
            first_u = forcing[0, 0, upper, 0, :, cols] + first * (
                initial[0, upper, 0, :, cols] - ALPHA * last[0, upper, 0, :, cols]
            )
            first_w = forcing[1, 0, upper, 0, :, cols] + first * (
                initial[1, upper, 0, :, cols] - ALPHA * last[1, upper, 0, :, cols]
            )
            second_u = forcing[0, 1, upper, 0, :, cols]
            second_w = forcing[1, 1, upper, 0, :, cols]
            units = (
                weight * (first_w + first_u),
                weight_two * (second_w + second_u - first_u),
                weight_three * second_u,
            )
            for k, unit in enumerate(units):
                rows = slice(32 * k, 32 * k + 32)
                out[(2 * side) ^ flip_y, upper ^ flip_z, 0, rows, :] = pack_left(unit, low)
                out[(2 * side + 1) ^ flip_y, upper ^ flip_z, 0, rows, :] = pack_right(unit, low)


def prepare(forcing, initial, last):
    pieces = pl.pallas_call(
        prepare_kernel,
        grid=(2,),
        in_specs=[
            pl.BlockSpec((2, 2, 2, 1, 64, 256), lambda i: (0, 0, 0, i, 0, 0)),
            pl.BlockSpec((2, 2, 1, 64, 256), lambda i: (0, 0, i, 0, 0)),
            pl.BlockSpec((2, 2, 1, 64, 256), lambda i: (0, 0, i, 0, 0)),
        ],
        out_specs=pl.BlockSpec((4, 2, 1, 96, 128), lambda i: (0, 0, i, 0, 0)),
        out_shape=jax.ShapeDtypeStruct((4, 2, 2, 96, 128), jnp.float32),
        compiler_params=params(),
        name="prepare",
    )(
        forcing.reshape(2, 2, 2, 2, 64, 256),
        initial.reshape(2, 2, 2, 64, 256),
        last.reshape(2, 2, 2, 64, 256),
    )
    return pieces.reshape(16, 96, 128)


def scaled(factor, value):
    if abs(factor) < 1e-12:
        return None
    if abs(factor - 1.0) < 1e-12:
        return value
    if abs(factor + 1.0) < 1e-12:
        return -value
    return np.float32(factor) * value


def total_of(terms):
    terms = [term for term in terms if term is not None]
    result = terms[0]
    for term in terms[1:]:
        result = result + term
    return result


def angle(index):
    return 2.0 * math.pi * (index % STEPS) / STEPS


def forward(steps):
    even = [steps[0]] + [steps[n] + steps[32 - n] for n in range(1, 16)] + [steps[16]]
    odd = [None] + [steps[n] - steps[32 - n] for n in range(1, 16)]
    planes = [None] * 32
    for j in range(9):
        cos_even = total_of([scaled(math.cos(angle(j * n)), even[n]) for n in range(0, 17, 2)])
        cos_odd = (
            None if j == 8 else total_of([scaled(math.cos(angle(j * n)), even[n]) for n in range(1, 17, 2)])
        )
        high, lowp = (
            (cos_even, None) if cos_odd is None else (cos_even + cos_odd, cos_even - cos_odd)
        )
        if j == 0:
            planes[0], planes[1] = high, lowp
            continue
        planes[2 * j] = high
        if j < 8:
            planes[2 * (16 - j)] = lowp
        sin_odd = total_of([scaled(math.sin(angle(j * n)), odd[n]) for n in range(1, 16, 2)])
        if j == 8:
            planes[2 * j + 1] = -sin_odd
            continue
        sin_even = total_of([scaled(math.sin(angle(j * n)), odd[n]) for n in range(2, 16, 2)])
        planes[2 * j + 1] = -(sin_even + sin_odd)
        planes[2 * (16 - j) + 1] = sin_even - sin_odd
    return planes


def backward(planes):
    real = [planes[0]] + [planes[2 * j] * 2.0 for j in range(1, 16)] + [planes[1]]
    imag = [None] + [planes[2 * j + 1] * 2.0 for j in range(1, 16)]
    steps = [None] * 32

    def put(n, cosine, sine):
        if n in (0, 16):
            steps[n] = cosine
            return
        steps[n] = cosine - sine
        steps[32 - n] = cosine + sine

    for n in range(9):
        cos_even = total_of([scaled(math.cos(angle(j * n)), real[j]) for j in range(0, 17, 2)])
        if n == 8:
            sine = total_of([scaled(math.sin(angle(j * n)), imag[j]) for j in range(1, 16, 2)])
            put(8, cos_even, sine)
            continue
        cos_odd = total_of([scaled(math.cos(angle(j * n)), real[j]) for j in range(1, 17, 2)])
        if n == 0:
            put(0, cos_even + cos_odd, None)
            put(16, cos_even - cos_odd, None)
            continue
        sin_odd = total_of([scaled(math.sin(angle(j * n)), imag[j]) for j in range(1, 16, 2)])
        sin_even = total_of([scaled(math.sin(angle(j * n)), imag[j]) for j in range(2, 16, 2)])
        put(n, cos_even + cos_odd, sin_even + sin_odd)
        put(16 - n, cos_even - cos_odd, sin_odd - sin_even)
    return steps


def transform_kernel(table, cell_class, received, planes_out, left_out, right_out, core_out, cross_out):
    upper, core, quarter = place()[3:6]
    low8 = lanes(8) < 64
    lane8 = lanes(8) % 64
    row0 = pl.multiple_of((upper * 2 + core) * 64, 64)
    col0 = pl.multiple_of((quarter >> 1) * 128, 128)
    classes = cell_class[pl.ds(row0, 64), pl.ds(col0, 128)]
    courant = jnp.zeros(classes.shape, jnp.float32)
    for k in range(8):
        courant = jnp.where(classes == k, table[k], courant)
    courant = jnp.where((quarter & 1) == 1, half_turn(courant), courant)
    courant = pack_left(courant, lanes(32) < 64)
    planes_out[32] = courant
    for r in range(4):
        rows = slice(8 * r, 8 * r + 8)
        steps = []
        for t in range(16):
            steps.append(received[t, 8 * r : 8 * r + 8, :] + received[(t + 15) % 16, 64 + 8 * r : 72 + 8 * r, :])
            steps.append(received[t, 32 + 8 * r : 40 + 8 * r, :])
        planes = forward(steps)
        for p in range(32):
            planes_out[p, rows, :] = planes[p]
        planes = planes + [courant[rows]]
        for g in range(5):
            left = jnp.zeros((8, 128), jnp.float32)
            right = left
            for m, plane in enumerate(planes[8 * g : 8 * g + 8]):
                here = (lane8 >= 8 * m) & (lane8 < 8 * m + 8)
                left = jnp.where(here, pltpu.roll(plane, 8 * m, 1) if m else plane, left)
                right = jnp.where(here, pltpu.roll(plane, (8 * m - 56) % 128, 1), right)
            left_out[g, rows, :] = left
            right_out[g, rows, :] = right
        planes = planes + [planes[-1]]
        if r == 0:
            for j in range(17):
                top = jnp.where(low8, planes[2 * j], half_turn(planes[2 * j + 1]))

                @pl.when(core == 0)
                def _():
                    cross_out[j] = top

                @pl.when(core == 1)
                def _():
                    core_out[j] = top

        if r == 3:
            for j in range(17):
                bottom = jnp.where(low8, half_turn(planes[2 * j]), planes[2 * j + 1])

                @pl.when(core == 0)
                def _():
                    core_out[j] = bottom

                @pl.when(core == 1)
                def _():
                    cross_out[j] = bottom


def transform(table, cell_class, received):
    shapes = ((33, 32, 128), (5, 32, 128), (5, 32, 128), (17, 8, 128), (17, 8, 128))
    return pl.pallas_call(
        transform_kernel,
        in_specs=[
            pl.BlockSpec(memory_space=pltpu.SMEM),
            pl.BlockSpec(memory_space=pltpu.VMEM),
            pl.BlockSpec(memory_space=pltpu.VMEM),
        ],
        out_specs=[pl.BlockSpec(memory_space=pltpu.VMEM)] * 5,
        out_shape=[jax.ShapeDtypeStruct(shape, jnp.float32) for shape in shapes],
        compiler_params=params(),
        name="transform",
    )(table, cell_class, received)


def around(field):
    first = pltpu.roll(field[9], 1, 0)
    last = pltpu.roll(field[0], 7, 0)
    above = [first] + field[:9]
    below = field[1:] + [last]
    return [
        (up + down) + (pltpu.roll(own, 1, 1) + pltpu.roll(own, 127, 1))
        for up, own, down in zip(above, field, below)
    ]


def solve_kernel(lam, planes, from_left, from_right, from_core, from_cross, out, solved, wide, own):
    core, _, row0, col0 = place()[4:]
    low = lanes(32) < 64
    lane32 = lanes(32)
    lane8 = lanes(8)
    is_lower = core == 1

    def halo(index):
        return (
            jnp.where(is_lower, from_core[index], from_cross[index]),
            jnp.where(is_lower, from_cross[index], from_core[index]),
        )

    def turn(value, shift):
        return pltpu.roll(value, shift & 127 if isinstance(shift, int) else lax.rem(shift + 256, 128), 1)

    def merged(lane, centre, right, left):
        value = jnp.where(lane < 64, centre, right)
        return jnp.where(lane < 72, value, jnp.where(lane >= 120, left, 0.0))

    def extended(p, pair, odd, group, offset):
        centre = planes[p]
        right, left = from_right[group], from_left[group]
        top_main, bottom_main = halo(pair)
        if odd:
            top_main, bottom_main = half_turn(top_main), half_turn(bottom_main)
        top_left, bottom_left = halo(17 + group)
        top_right, bottom_right = halo(22 + group)
        return jnp.concatenate(
            [
                merged(lane8, top_main, turn(top_right, -offset), turn(top_left, 56 - offset)),
                merged(lane32, centre, turn(right, 64 - offset), turn(left, 120 - offset)),
                merged(lane32, half_turn(centre), turn(right, -offset), turn(left, 56 - offset)),
                merged(lane8, bottom_main, turn(bottom_right, 64 - offset), turn(bottom_left, 120 - offset)),
            ],
            axis=0,
        )

    def spread(slot, value):
        wide[slot] = value
        return [wide[slot, pl.ds(v, 8, stride=10), :] for v in range(10)]

    def keep(p, slot, field):
        for v in range(10):
            wide[slot, pl.ds(v, 8, stride=10), :] = field[v]
        solved[p] = jnp.where(low, wide[slot, 8:40, :], half_turn(wide[slot, 40:72, :]))

    rows = lax.broadcasted_iota(jnp.int32, (80, 128), 0) - 8 + row0
    lane80 = lanes(80)
    cols = jnp.where(lane80 >= 120, lane80 - 128, lane80) + col0
    inside = (rows >= 0) & (rows < 1024) & (cols >= 0) & (cols < 1024) & ((lane80 < 72) | (lane80 >= 120))
    courant = spread(0, jnp.where(inside, extended(32, 16, False, 4, 0), 0.0))
    inner = spread(1, jnp.where(inside, 1.0, 0.0))
    for v in range(10):
        own[0, v] = courant[v]
        own[1, v] = inner[v]

    def prepared(j, slot, special, group, offset):
        g_re = spread(2 * slot, extended(2 * j, j, False, group, offset))
        g_im = spread(2 * slot + 1, extended(2 * j + 1, j, True, group, offset + 8))
        start_re, start_im, gain_re, gain_im = [], [], [], []
        for v in range(10):
            speed, kept = own[0, v], own[1, v]
            if special:
                inv_re = kept / (lam[0, 0] + 4.0 * speed)
                inv_im = kept / (lam[0, 1] + 4.0 * speed)
                start_re.append(g_re[v] * inv_re)
                start_im.append(g_im[v] * inv_im)
            else:
                diag_re = lam[j, 0] + 4.0 * speed
                diag_im = lam[j, 1]
                scale = kept / (diag_re * diag_re + diag_im * diag_im)
                inv_re = diag_re * scale
                inv_im = -diag_im * scale
                start_re.append(g_re[v] * inv_re - g_im[v] * inv_im)
                start_im.append(g_re[v] * inv_im + g_im[v] * inv_re)
            gain_re.append(speed * inv_re)
            gain_im.append(speed * inv_im)
        return start_re, start_im, gain_re, gain_im

    def swept(special, start_re, start_im, gain_re, gain_im, re, im):
        all_re, all_im = around(re), around(im)
        if special:
            return (
                [start_re[v] + gain_re[v] * all_re[v] for v in range(10)],
                [start_im[v] + gain_im[v] * all_im[v] for v in range(10)],
            )
        return (
            [start_re[v] + (gain_re[v] * all_re[v] - gain_im[v] * all_im[v]) for v in range(10)],
            [start_im[v] + (gain_re[v] * all_im[v] + gain_im[v] * all_re[v]) for v in range(10)],
        )

    def batch(k, has_special):
        sets, fields = [], []
        for i in range(BATCH):
            special = has_special and i == 0
            j = k * BATCH + i
            sets.append((special,) + prepared(j, i, special, j >> 2, (j & 3) * 16))
            fields.append((sets[i][1], sets[i][2]))
        for _ in range(SWEEPS - 1):
            fields = [swept(*sets[i], *fields[i]) for i in range(BATCH)]
        for i in range(BATCH):
            j = k * BATCH + i
            keep(2 * j, 2 * i, fields[i][0])
            keep(2 * j + 1, 2 * i + 1, fields[i][1])

    def later(k, carry):
        batch(k, False)
        return carry

    batch(0, True)
    lax.fori_loop(1, 16 // BATCH, later, 0)

    for r in range(4):
        part = slice(8 * r, 8 * r + 8)
        steps = backward([solved[p, part, :] for p in range(32)])
        for n in range(32):
            value = steps[n] * np.float32(math.exp(-n * DECAY) / STEPS)
            t, second = n // 2, n % 2
            out[t, 32 + 32 * second + 8 * r : 40 + 32 * second + 8 * r, :] = value
            if second:
                before = value * np.float32(ALPHA) if n == 31 else value
                out[(t + 1) % 16, part, :] = before


def solve(lam, planes, from_left, from_right, from_core, from_cross):
    return pl.pallas_call(
        solve_kernel,
        in_specs=[pl.BlockSpec(memory_space=pltpu.SMEM)]
        + [pl.BlockSpec(memory_space=pltpu.VMEM)] * 5,
        out_specs=pl.BlockSpec(memory_space=pltpu.VMEM),
        out_shape=jax.ShapeDtypeStruct((16, 96, 128), jnp.float32),
        scratch_shapes=[
            pltpu.VMEM((32, 32, 128), jnp.float32),
            pltpu.VMEM((2 * BATCH, 80, 128), jnp.float32),
            pltpu.VMEM((2, 10, 8, 128), jnp.float32),
        ],
        compiler_params=params(),
        name="solve",
    )(lam, planes, from_left, from_right, from_core, from_cross)


def finish_kernel(received, forcing, initial, last, out):
    tm, flip_y, flip_z = place()[:3]
    low = lanes(32) < 64
    first = jnp.where(tm == 0, 1.0, 0.0).astype(jnp.float32)
    for upper in range(2):
        for side in range(2):
            cols = slice(128 * side, 128 * side + 128)
            for half in range(2):
                rows = slice(32 * half, 32 * half + 32)
                values = []
                for k in range(3):
                    unit = slice(32 * k, 32 * k + 32)
                    one = received[(2 * side) ^ flip_y, upper ^ flip_z, 0, unit, :]
                    two = received[(2 * side + 1) ^ flip_y, upper ^ flip_z, 0, unit, :]
                    if half == 0:
                        values.append(jnp.where(low, one, half_turn(two)))
                    else:
                        values.append(jnp.where(low, half_turn(one), two))
                before, now, after = values
                start = forcing[0, 0, upper, 0, rows, cols] + first * (
                    initial[0, upper, 0, rows, cols] - ALPHA * last[0, upper, 0, rows, cols]
                )
                out[0, 0, upper, 0, rows, cols] = now
                out[0, 1, upper, 0, rows, cols] = after
                out[1, 0, upper, 0, rows, cols] = now - before - start
                out[1, 1, upper, 0, rows, cols] = after - now - forcing[0, 1, upper, 0, rows, cols]


def finish(received, forcing, initial, last):
    result = pl.pallas_call(
        finish_kernel,
        grid=(2,),
        in_specs=[
            pl.BlockSpec((4, 2, 1, 96, 128), lambda i: (0, 0, i, 0, 0)),
            pl.BlockSpec((1, 2, 2, 1, 64, 256), lambda i: (0, 0, 0, i, 0, 0)),
            pl.BlockSpec((1, 2, 1, 64, 256), lambda i: (0, 0, i, 0, 0)),
            pl.BlockSpec((1, 2, 1, 64, 256), lambda i: (0, 0, i, 0, 0)),
        ],
        out_specs=pl.BlockSpec((2, 2, 2, 1, 64, 256), lambda i: (0, 0, 0, i, 0, 0)),
        out_shape=jax.ShapeDtypeStruct((2, 2, 2, 2, 64, 256), jnp.float32),
        compiler_params=params(),
        name="finish",
    )(
        received.reshape(4, 2, 2, 96, 128),
        forcing.reshape(2, 2, 2, 2, 64, 256),
        initial.reshape(2, 2, 2, 64, 256),
        last.reshape(2, 2, 2, 64, 256),
    )
    return result.reshape(2, 2, 256, 256)


def lam_squares():
    rows = []
    for j in range(16):
        lam = 1.0 - FACTOR * complex(math.cos(angle(j)), -math.sin(angle(j)))
        square = lam * lam
        rows.append((square.real, square.imag))
    rows[0] = ((1.0 - FACTOR) ** 2, (1.0 + FACTOR) ** 2)
    return np.array(rows, np.float32)


def per_device(forcing, initial, previous_last, cell_class, courant_table):
    core = lax.axis_index("tm") & 1
    lam = jnp.asarray(lam_squares())
    pieces = prepare(forcing, initial, previous_last)
    received = lax.all_to_all(pieces, "tm", 0, 0, tiled=True)
    planes, left, right, to_core, to_cross = transform(courant_table, cell_class, received)
    from_left = lax.ppermute(right, AXES, TO_RIGHT)
    from_right = lax.ppermute(left, AXES, TO_LEFT)

    def strip(main, start):
        corners = [
            lax.dynamic_slice_in_dim(value, start, 8, axis=1) for value in (from_left, from_right)
        ]
        return jnp.concatenate([main] + corners, axis=0)

    from_core = lax.ppermute(strip(to_core, 24 * (1 - core)), AXES, TO_CORE)
    from_cross = lax.ppermute(strip(to_cross, 24 * core), AXES, TO_CROSS)
    solved = solve(lam, planes, from_left, from_right, from_core, from_cross)
    returned = lax.all_to_all(solved, "tm", 0, 0, tiled=True)
    return finish(returned, forcing, initial, previous_last)


def solution(mesh):
    in_specs = (
        P(None, "tm", "sx", "sy"),
        P(None, "sx", "sy"),
        P(None, "sx", "sy"),
        P("sx", "sy"),
        P(),
    )
    out_specs = P(None, "tm", "sx", "sy")
    return jax.shard_map(
        per_device, mesh=mesh, in_specs=in_specs, out_specs=out_specs, check_vma=False
    )
```

```python
import math

import jax
import jax.numpy as jnp
import numpy as np
from jax import lax
from jax.experimental import pallas as pl
from jax.experimental.pallas import tpu as pltpu
from jax.sharding import PartitionSpec as P

STEPS = 32
SWEEPS = 8
BATCH = 4
ALPHA = 0.1
DECAY = math.log(ALPHA) / STEPS
FACTOR = math.exp(DECAY)
AXES = ("tm", "sx", "sy")
VMEM = 16 * 2**20


def chip_of(half, upper, inner, odd_x, odd_y):
    half_y, upper_y = half ^ odd_y, upper ^ odd_x
    return (2 * half_y + (upper_y ^ half_y)) * 2 + (inner ^ half)


def device_of(row, col):
    row, col = row % 16, col % 16
    sx, upper, core = row // 4, row // 2 % 2, row % 2
    sy, half, inner = col // 4, col // 2 % 2, col % 2
    tm = chip_of(half, upper, inner, sx & 1, sy & 1) * 2 + core
    return (tm * 4 + sx) * 4 + sy


def pairs_of(move):
    return [
        (device_of(row, col), device_of(*move(row, col))) for row in range(16) for col in range(16)
    ]


def away(index):
    return index - 1 if index % 2 == 0 else index + 1


TO_SIDE = pairs_of(lambda row, col: (row, away(col)))
TO_CORE = pairs_of(lambda row, col: (row ^ 1, col))
TO_CROSS = pairs_of(lambda row, col: (away(row), col))
CHIPS = [[chip * 2 + core for chip in range(8)] for core in range(2)]
CORES = [(tm, tm ^ 1) for tm in range(16)]


def lanes(rows):
    return lax.broadcasted_iota(jnp.int32, (rows, 128), 1)


def half_turn(value):
    return pltpu.roll(value, 64, 1)


def pack_left(value, low):
    return jnp.where(low, value[:32], half_turn(value[32:]))


def pack_right(value, low):
    return jnp.where(low, half_turn(value[:32]), value[32:])


def place():
    tm, sx, sy = (lax.axis_index(axis) for axis in AXES)
    odd_x, odd_y = sx & 1, sy & 1
    y, z, core = tm >> 2, tm >> 1 & 1, tm & 1
    half_y = y >> 1
    upper_y = (y & 1) ^ half_y
    half, upper = half_y ^ odd_y, upper_y ^ odd_x
    inner = z ^ half
    row0 = sx * 256 + upper * 128 + core * 64
    col0 = sy * 256 + half * 128 + inner * 64
    return tm, odd_x, odd_y, core, upper, half, inner, row0, col0


def params():
    return pltpu.CompilerParams(vmem_limit_bytes=VMEM)


def turn(value, shift):
    if isinstance(shift, int):
        return pltpu.roll(value, shift % 128, 1) if shift % 128 else value
    return pltpu.roll(value, lax.rem(shift + 256, 128), 1)


def prepare_kernel(forcing, mine, theirs):
    tm, odd_x, odd_y, own_core = place()[:4]
    low = lanes(32) < 64
    weight = jnp.float32(1.0)
    for bit in range(4):
        step = math.exp(DECAY * 2 ** (bit + 1))
        weight = weight * jnp.where((tm >> bit & 1) == 1, step, 1.0).astype(jnp.float32)
    weight_two = weight * np.float32(FACTOR)
    weight_three = weight * np.float32(-FACTOR * FACTOR)
    for out, core in ((mine, own_core), (theirs, 1 - own_core)):
        for upper in range(2):
            for half in range(2):
                cols = slice(128 * half, 128 * half + 128)
                first_u, second_u = forcing[0, 0, upper, core, :, cols], forcing[0, 1, upper, core, :, cols]
                first_w, second_w = forcing[1, 0, upper, core, :, cols], forcing[1, 1, upper, core, :, cols]
                units = (
                    weight * (first_w + first_u),
                    weight_two * (second_w + second_u - first_u),
                    weight_three * second_u,
                )
                left = chip_of(half, upper, 0, odd_x, odd_y)
                right = chip_of(half, upper, 1, odd_x, odd_y)
                for k, unit in enumerate(units):
                    rows = slice(32 * k, 32 * k + 32)
                    out[left, rows, :] = pack_left(unit, low)
                    out[right, rows, :] = pack_right(unit, low)


def prepare(forcing):
    return pl.pallas_call(
        prepare_kernel,
        in_specs=[pl.BlockSpec(memory_space=pltpu.VMEM)],
        out_specs=[pl.BlockSpec(memory_space=pltpu.VMEM)] * 2,
        out_shape=[jax.ShapeDtypeStruct((8, 96, 128), jnp.float32)] * 2,
        compiler_params=params(),
        name="prepare",
    )(forcing.reshape(2, 2, 2, 2, 64, 256))


def merge_kernel(mine, received, out):
    _, odd_x, odd_y, core = place()[:4]
    is_first = core == 0
    lane8 = lanes(8) % 64
    for chip in range(8):
        for k in range(3):
            rows = slice(32 * k, 32 * k + 32)
            own, other = mine[chip, rows, :], received[chip, rows, :]
            early, late = jnp.where(is_first, own, other), jnp.where(is_first, other, own)
            if k < 2:
                out[chip, 32 * k : 32 * k + 32, :] = early
                kept = late if k == 0 else kept
                if k == 1:
                    out[chip, 96:128, :] = late
            else:
                out[chip, 64:96, :] = kept + early
                out[chip, 128:160, :] = late
    for chip in range(8):
        inner = (chip & 1) ^ (chip >> 2) ^ odd_y
        for tile in range(3):
            value = jnp.zeros((8, 128), jnp.float32)
            for m in range(8):
                k, r = (8 * tile + m) // 4, m % 4
                if k == 5:
                    break
                beside = out[chip ^ 1, 32 * k + 8 * r : 32 * k + 8 * r + 8, :]
                here = (lane8 >= 8 * m) & (lane8 < 8 * m + 8)
                value = jnp.where(here, turn(beside, 8 * m - 56 * inner), value)
            out[chip, 160 + 8 * tile : 168 + 8 * tile, :] = value


def merge(mine, received):
    return pl.pallas_call(
        merge_kernel,
        in_specs=[pl.BlockSpec(memory_space=pltpu.VMEM)] * 2,
        out_specs=pl.BlockSpec(memory_space=pltpu.VMEM),
        out_shape=jax.ShapeDtypeStruct((8, 184, 128), jnp.float32),
        compiler_params=params(),
        name="merge",
    )(mine, received)


def scaled(factor, value):
    if abs(factor) < 1e-12:
        return None
    if abs(factor - 1.0) < 1e-12:
        return value
    if abs(factor + 1.0) < 1e-12:
        return -value
    return np.float32(factor) * value


def total_of(terms):
    terms = [term for term in terms if term is not None]
    result = terms[0]
    for term in terms[1:]:
        result = result + term
    return result


def angle(index):
    return 2.0 * math.pi * (index % STEPS) / STEPS


def forward(steps):
    even = [steps[0]] + [steps[n] + steps[32 - n] for n in range(1, 16)] + [steps[16]]
    odd = [None] + [steps[n] - steps[32 - n] for n in range(1, 16)]
    planes = [None] * 32
    for j in range(9):
        cos_even = total_of([scaled(math.cos(angle(j * n)), even[n]) for n in range(0, 17, 2)])
        cos_odd = (
            None if j == 8 else total_of([scaled(math.cos(angle(j * n)), even[n]) for n in range(1, 17, 2)])
        )
        high, lowp = (
            (cos_even, None) if cos_odd is None else (cos_even + cos_odd, cos_even - cos_odd)
        )
        if j == 0:
            planes[0], planes[1] = high, lowp
            continue
        planes[2 * j] = high
        if j < 8:
            planes[2 * (16 - j)] = lowp
        sin_odd = total_of([scaled(math.sin(angle(j * n)), odd[n]) for n in range(1, 16, 2)])
        if j == 8:
            planes[2 * j + 1] = -sin_odd
            continue
        sin_even = total_of([scaled(math.sin(angle(j * n)), odd[n]) for n in range(2, 16, 2)])
        planes[2 * j + 1] = -(sin_even + sin_odd)
        planes[2 * (16 - j) + 1] = sin_even - sin_odd
    return planes


def backward(planes):
    real = [planes[0]] + [planes[2 * j] * 2.0 for j in range(1, 16)] + [planes[1]]
    imag = [None] + [planes[2 * j + 1] * 2.0 for j in range(1, 16)]
    steps = [None] * 32

    def put(n, cosine, sine):
        if n in (0, 16):
            steps[n] = cosine
            return
        steps[n] = cosine - sine
        steps[32 - n] = cosine + sine

    for n in range(9):
        cos_even = total_of([scaled(math.cos(angle(j * n)), real[j]) for j in range(0, 17, 2)])
        if n == 8:
            sine = total_of([scaled(math.sin(angle(j * n)), imag[j]) for j in range(1, 16, 2)])
            put(8, cos_even, sine)
            continue
        cos_odd = total_of([scaled(math.cos(angle(j * n)), real[j]) for j in range(1, 17, 2)])
        if n == 0:
            put(0, cos_even + cos_odd, None)
            put(16, cos_even - cos_odd, None)
            continue
        sin_odd = total_of([scaled(math.sin(angle(j * n)), imag[j]) for j in range(1, 16, 2)])
        sin_even = total_of([scaled(math.sin(angle(j * n)), imag[j]) for j in range(2, 16, 2)])
        put(n, cos_even + cos_odd, sin_even + sin_odd)
        put(16 - n, cos_even - cos_odd, sin_odd - sin_even)
    return steps


def transform_kernel(
    table, cell_class, initial, last, received, planes_out, beside_out, side_out, core_out, cross_out
):
    _, _, _, core, upper, half, inner = place()[:7]
    low8, low32 = lanes(8) < 64, lanes(32) < 64
    lane8 = lanes(8) % 64
    rows = pl.ds(pl.multiple_of((upper * 2 + core) * 64, 64), 64)
    cols = pl.ds(pl.multiple_of(half * 128, 128), 128)
    is_right = inner == 1

    def slots(m):
        return (lane8 >= 8 * m) & (lane8 < 8 * m + 8)

    def own_and_beside(value):
        turned = half_turn(value)
        own = pack_left(jnp.where(is_right, turned, value), low32)
        other = pack_left(jnp.where(is_right, value, turned), low32)
        beside = jnp.zeros((8, 128), jnp.float32)
        for r in range(4):
            beside = jnp.where(slots(r), turn(other[8 * r : 8 * r + 8], 8 * r - 56 * inner), beside)
        return [own[8 * r : 8 * r + 8] for r in range(4)] + [beside]

    classes = cell_class[rows, cols]
    courant = jnp.zeros(classes.shape, jnp.float32)
    for k in range(8):
        courant = jnp.where(classes == k, table[k], courant)
    courant = own_and_beside(courant)
    start_u, start_w = (
        own_and_beside(initial[c, rows, cols] - ALPHA * last[c, rows, cols]) for c in range(2)
    )

    for r in range(5):
        steps = []
        for t in range(8):
            before = (t + 7) % 8
            if r < 4:
                part = [received[t, 32 * k + 8 * r : 32 * k + 8 * r + 8, :] for k in range(4)]
                part[0] = part[0] + received[before, 128 + 8 * r : 136 + 8 * r, :]
            else:
                one, two = received[t, 160:168, :], received[t, 168:176, :]
                part = [one + received[before, 176:184, :], turn(one, -32), two, turn(two, -32)]
            steps.extend(part)
        steps[0] = steps[0] + (start_w[r] + start_u[r])
        steps[1] = steps[1] - np.float32(FACTOR) * start_u[r]
        planes = forward(steps) + [courant[r]]
        if r == 4:
            for p in range(33):
                beside_out[p] = planes[p]
        else:
            for p in range(33):
                planes_out[p, 8 * r : 8 * r + 8, :] = planes[p]
            for g in range(5):
                value = jnp.zeros((8, 128), jnp.float32)
                for m, plane in enumerate(planes[8 * g : 8 * g + 8]):
                    value = jnp.where(slots(m), turn(plane, 8 * m - 56 * inner), value)
                side_out[g, 8 * r : 8 * r + 8, :] = value
        if r == 0:
            pairs = planes + [planes[32]]
            top = [jnp.where(low8, pairs[2 * j], half_turn(pairs[2 * j + 1])) for j in range(17)]
        if r == 3:
            pairs = planes + [planes[32]]
            bottom = [jnp.where(low8, half_turn(pairs[2 * j]), pairs[2 * j + 1]) for j in range(17)]
        if r == 4:
            for strip, start in ((top, 0), (bottom, 88)):
                for g in range(5):
                    value = jnp.zeros((8, 128), jnp.float32)
                    for m, plane in enumerate(planes[8 * g : 8 * g + 8]):
                        value = jnp.where(slots(m), turn(plane, 8 * m - start), value)
                    strip.append(value)
    for i in range(22):
        core_out[i] = jnp.where(core == 0, bottom[i], top[i])
        cross_out[i] = jnp.where(core == 0, top[i], bottom[i])


def transform(table, cell_class, initial, last, received):
    shapes = ((33, 32, 128), (33, 8, 128), (5, 32, 128), (22, 8, 128), (22, 8, 128))
    return pl.pallas_call(
        transform_kernel,
        in_specs=[pl.BlockSpec(memory_space=pltpu.SMEM)] + [pl.BlockSpec(memory_space=pltpu.VMEM)] * 4,
        out_specs=[pl.BlockSpec(memory_space=pltpu.VMEM)] * 5,
        out_shape=[jax.ShapeDtypeStruct(shape, jnp.float32) for shape in shapes],
        compiler_params=params(),
        name="transform",
    )(table, cell_class, initial, last, received)


def around(field):
    first = pltpu.roll(field[9], 1, 0)
    last = pltpu.roll(field[0], 7, 0)
    above = [first] + field[:9]
    below = field[1:] + [last]
    return [
        (up + down) + (pltpu.roll(own, 1, 1) + pltpu.roll(own, 127, 1))
        for up, own, down in zip(above, field, below)
    ]


def solve_kernel(lam, planes, beside, from_side, from_core, from_cross, out, solved, wide, own):
    core, _, _, inner, row0, col0 = place()[3:]
    low = lanes(32) < 64
    is_lower = core == 1
    side_base = 120 - 56 * inner
    beside_base = 64 + 56 * inner

    def within(lane, base):
        return (lane >= base) & (lane < base + 8)

    side_lanes, beside_lanes = within(lanes(8), side_base), within(lanes(8), beside_base)
    low8 = lanes(8) < 64

    def halo(index):
        return (
            jnp.where(is_lower, from_core[index], from_cross[index]),
            jnp.where(is_lower, from_cross[index], from_core[index]),
        )

    def merged(centre, side, other):
        value = jnp.where(low8, centre, 0.0)
        value = jnp.where(side_lanes, side, value)
        return jnp.where(beside_lanes, other, value)

    def extended(p, pair, odd, group, offset):
        edge = beside[p]
        top_main, bottom_main = halo(pair)
        if odd:
            top_main, bottom_main = half_turn(top_main), half_turn(bottom_main)
        top_beside, bottom_beside = halo(17 + group)
        top_side, bottom_side = halo(22 + group)
        parts = [
            merged(
                top_main,
                turn(top_side, side_base - 64 - offset),
                turn(top_beside, beside_base - offset),
            )
        ]
        for r in range(8):
            part = slice(8 * (r % 4), 8 * (r % 4) + 8)
            centre, shift = planes[p, part, :], 0 if r < 4 else 64
            parts.append(
                merged(
                    turn(centre, shift),
                    turn(from_side[group, part, :], side_base - shift - offset),
                    turn(edge, beside_base - shift - 8 * (r % 4)),
                )
            )
        parts.append(
            merged(
                bottom_main,
                turn(bottom_side, side_base - offset),
                turn(bottom_beside, beside_base - offset),
            )
        )
        return jnp.concatenate(parts, axis=0)

    def spread(slot, value):
        wide[slot] = value
        return [wide[slot, pl.ds(v, 8, stride=10), :] for v in range(10)]

    def keep(p, slot, field):
        for v in range(10):
            wide[slot, pl.ds(v, 8, stride=10), :] = field[v]
        solved[p] = jnp.where(low, wide[slot, 8:40, :], half_turn(wide[slot, 40:72, :]))

    rows = lax.broadcasted_iota(jnp.int32, (80, 128), 0) - 8 + row0
    lane80 = lanes(80)
    cols = jnp.where(lane80 >= 120, lane80 - 128, lane80) + col0
    inside = (rows >= 0) & (rows < 1024) & (cols >= 0) & (cols < 1024) & ((lane80 < 72) | (lane80 >= 120))
    courant = spread(0, jnp.where(inside, extended(32, 16, False, 4, 0), 0.0))
    inner = spread(1, jnp.where(inside, 1.0, 0.0))
    for v in range(10):
        own[0, v] = courant[v]
        own[1, v] = inner[v]

    def prepared(j, slot, special, group, offset):
        g_re = spread(2 * slot, extended(2 * j, j, False, group, offset))
        g_im = spread(2 * slot + 1, extended(2 * j + 1, j, True, group, offset + 8))
        start_re, start_im, gain_re, gain_im = [], [], [], []
        for v in range(10):
            speed, kept = own[0, v], own[1, v]
            if special:
                inv_re = kept / (lam[0, 0] + 4.0 * speed)
                inv_im = kept / (lam[0, 1] + 4.0 * speed)
                start_re.append(g_re[v] * inv_re)
                start_im.append(g_im[v] * inv_im)
            else:
                diag_re = lam[j, 0] + 4.0 * speed
                diag_im = lam[j, 1]
                scale = kept / (diag_re * diag_re + diag_im * diag_im)
                inv_re = diag_re * scale
                inv_im = -diag_im * scale
                start_re.append(g_re[v] * inv_re - g_im[v] * inv_im)
                start_im.append(g_re[v] * inv_im + g_im[v] * inv_re)
            gain_re.append(speed * inv_re)
            gain_im.append(speed * inv_im)
        return start_re, start_im, gain_re, gain_im

    def swept(special, start_re, start_im, gain_re, gain_im, re, im):
        all_re, all_im = around(re), around(im)
        if special:
            return (
                [start_re[v] + gain_re[v] * all_re[v] for v in range(10)],
                [start_im[v] + gain_im[v] * all_im[v] for v in range(10)],
            )
        return (
            [start_re[v] + (gain_re[v] * all_re[v] - gain_im[v] * all_im[v]) for v in range(10)],
            [start_im[v] + (gain_re[v] * all_im[v] + gain_im[v] * all_re[v]) for v in range(10)],
        )

    def batch(k, has_special):
        sets, fields = [], []
        for i in range(BATCH):
            special = has_special and i == 0
            j = k * BATCH + i
            sets.append((special,) + prepared(j, i, special, j >> 2, (j & 3) * 16))
            fields.append((sets[i][1], sets[i][2]))
        for _ in range(SWEEPS - 1):
            fields = [swept(*sets[i], *fields[i]) for i in range(BATCH)]
        for i in range(BATCH):
            j = k * BATCH + i
            keep(2 * j, 2 * i, fields[i][0])
            keep(2 * j + 1, 2 * i + 1, fields[i][1])

    def later(k, carry):
        batch(k, False)
        return carry

    batch(0, True)
    lax.fori_loop(1, 16 // BATCH, later, 0)

    for r in range(4):
        part = slice(8 * r, 8 * r + 8)
        steps = backward([solved[p, part, :] for p in range(32)])
        for n in range(32):
            value = steps[n] * np.float32(math.exp(-n * DECAY) / STEPS)
            t, k = n // 4, n % 4
            out[t, 32 * k + 32 + 8 * r : 32 * k + 40 + 8 * r, :] = value
            if k == 3:
                out[(t + 1) % 8, part, :] = value * np.float32(ALPHA) if n == 31 else value


def solve(lam, planes, beside, from_side, from_core, from_cross):
    return pl.pallas_call(
        solve_kernel,
        in_specs=[pl.BlockSpec(memory_space=pltpu.SMEM)] + [pl.BlockSpec(memory_space=pltpu.VMEM)] * 5,
        out_specs=pl.BlockSpec(memory_space=pltpu.VMEM),
        out_shape=jax.ShapeDtypeStruct((8, 160, 128), jnp.float32),
        scratch_shapes=[
            pltpu.VMEM((32, 32, 128), jnp.float32),
            pltpu.VMEM((2 * BATCH, 80, 128), jnp.float32),
            pltpu.VMEM((2, 10, 8, 128), jnp.float32),
        ],
        compiler_params=params(),
        name="solve",
    )(lam, planes, beside, from_side, from_core, from_cross)


def finish_kernel(returned, received, forcing, initial, last, out):
    tm, odd_x, odd_y, core = place()[:4]
    is_own = pl.program_id(0) == core
    low = lanes(32) < 64
    first = jnp.where(tm == 0, 1.0, 0.0).astype(jnp.float32)

    def unit(chip, k):
        start = pl.multiple_of(64 * core + 32 * k, 32)
        return jnp.where(is_own, returned[chip, pl.ds(start, 32), :], received[chip, 32 * k : 32 * k + 32, :])

    for upper in range(2):
        for half in range(2):
            cols = slice(128 * half, 128 * half + 128)
            left = chip_of(half, upper, 0, odd_x, odd_y)
            right = chip_of(half, upper, 1, odd_x, odd_y)
            ones, twos = ([unit(chip, k) for k in range(3)] for chip in (left, right))
            for part in range(2):
                rows = slice(32 * part, 32 * part + 32)
                if part == 0:
                    values = [jnp.where(low, one, half_turn(two)) for one, two in zip(ones, twos)]
                else:
                    values = [jnp.where(low, half_turn(one), two) for one, two in zip(ones, twos)]
                before, now, after = values
                start = forcing[0, 0, upper, 0, rows, cols] + first * (
                    initial[0, upper, 0, rows, cols] - ALPHA * last[0, upper, 0, rows, cols]
                )
                out[0, 0, upper, 0, rows, cols] = now
                out[0, 1, upper, 0, rows, cols] = after
                out[1, 0, upper, 0, rows, cols] = now - before - start
                out[1, 1, upper, 0, rows, cols] = after - now - forcing[0, 1, upper, 0, rows, cols]


def finish(returned, received, forcing, initial, last):
    result = pl.pallas_call(
        finish_kernel,
        grid=(2,),
        in_specs=[
            pl.BlockSpec((8, 160, 128), lambda i: (0, 0, 0)),
            pl.BlockSpec((8, 96, 128), lambda i: (0, 0, 0)),
            pl.BlockSpec((1, 2, 2, 1, 64, 256), lambda i: (0, 0, 0, i, 0, 0)),
            pl.BlockSpec((1, 2, 1, 64, 256), lambda i: (0, 0, i, 0, 0)),
            pl.BlockSpec((1, 2, 1, 64, 256), lambda i: (0, 0, i, 0, 0)),
        ],
        out_specs=pl.BlockSpec((2, 2, 2, 1, 64, 256), lambda i: (0, 0, 0, i, 0, 0)),
        out_shape=jax.ShapeDtypeStruct((2, 2, 2, 2, 64, 256), jnp.float32),
        compiler_params=params(),
        name="finish",
    )(
        returned,
        received,
        forcing.reshape(2, 2, 2, 2, 64, 256),
        initial.reshape(2, 2, 2, 64, 256),
        last.reshape(2, 2, 2, 64, 256),
    )
    return result.reshape(2, 2, 256, 256)


def lam_squares():
    rows = []
    for j in range(16):
        lam = 1.0 - FACTOR * complex(math.cos(angle(j)), -math.sin(angle(j)))
        square = lam * lam
        rows.append((square.real, square.imag))
    rows[0] = ((1.0 - FACTOR) ** 2, (1.0 + FACTOR) ** 2)
    return np.array(rows, np.float32)


def chips_exchange(pieces):
    return lax.all_to_all(pieces, "tm", 0, 0, axis_index_groups=CHIPS, tiled=True)


def per_device(forcing, initial, previous_last, cell_class, courant_table):
    core = lax.axis_index("tm") & 1
    lam = jnp.asarray(lam_squares())
    mine, theirs = prepare(forcing)
    received = chips_exchange(merge(mine, lax.ppermute(theirs, "tm", CORES)))
    planes, beside, side, to_core, to_cross = transform(
        courant_table, cell_class, initial, previous_last, received
    )
    from_side = lax.ppermute(side, AXES, TO_SIDE)

    def strip(main, start):
        return jnp.concatenate([main, lax.dynamic_slice_in_dim(from_side, start, 8, axis=1)], axis=0)

    from_core = lax.ppermute(strip(to_core, 24 * (1 - core)), AXES, TO_CORE)
    from_cross = lax.ppermute(strip(to_cross, 24 * core), AXES, TO_CROSS)
    returned = chips_exchange(solve(lam, planes, beside, from_side, from_core, from_cross))
    wanted = lax.dynamic_slice_in_dim(returned, 64 * (1 - core), 96, axis=1)
    other = lax.ppermute(wanted, "tm", CORES)
    return finish(returned, other, forcing, initial, previous_last)


def solution(mesh):
    in_specs = (
        P(None, "tm", "sx", "sy"),
        P(None, "sx", "sy"),
        P(None, "sx", "sy"),
        P("sx", "sy"),
        P(),
    )
    out_specs = P(None, "tm", "sx", "sy")
    return jax.shard_map(
        per_device, mesh=mesh, in_specs=in_specs, out_specs=out_specs, check_vma=False
    )
```

```python
import functools
import math

import jax
import jax.numpy as jnp
import numpy as np
from jax import lax
from jax.experimental import pallas as pl
from jax.experimental.pallas import tpu as pltpu
from jax.sharding import PartitionSpec as P

STEPS = 32
SWEEPS = 8
BATCH = 8
ALPHA = 0.1
DECAY = math.log(ALPHA) / STEPS
FACTOR = math.exp(DECAY)
AXES = ("tm", "sx", "sy")
VMEM = 16 * 2**20


def chip_of(half, upper, inner, odd_x, odd_y):
    half_y, upper_y = half ^ odd_y, upper ^ odd_x
    return (2 * half_y + (upper_y ^ half_y)) * 2 + (inner ^ half)


def device_of(row, col):
    row, col = row % 16, col % 16
    sx, upper, core = row // 4, row // 2 % 2, row % 2
    sy, half, inner = col // 4, col // 2 % 2, col % 2
    tm = chip_of(half, upper, inner, sx & 1, sy & 1) * 2 + core
    return (tm * 4 + sx) * 4 + sy


def pairs_of(move):
    return [
        (device_of(row, col), device_of(*move(row, col))) for row in range(16) for col in range(16)
    ]


def away(index):
    return index - 1 if index % 2 == 0 else index + 1


def side_of(row, col):
    return (row, away(col)) if 0 < col < 15 else (row ^ 1, col)


TO_SIDE = pairs_of(side_of)
TO_CORE = pairs_of(lambda row, col: (row ^ 1, col))
TO_CROSS = pairs_of(lambda row, col: (away(row), col))
CHIPS = [[chip * 2 + core for chip in range(8)] for core in range(2)]
CORES = [(tm, tm ^ 1) for tm in range(16)]


def lanes(rows):
    return lax.broadcasted_iota(jnp.int32, (rows, 128), 1)


def half_turn(value):
    return pltpu.roll(value, 64, 1)


def pack_left(value, low):
    return jnp.where(low, value[:32], half_turn(value[32:]))


def pack_right(value, low):
    return jnp.where(low, half_turn(value[:32]), value[32:])


def place():
    tm, sx, sy = (lax.axis_index(axis) for axis in AXES)
    odd_x, odd_y = sx & 1, sy & 1
    y, z, core = tm >> 2, tm >> 1 & 1, tm & 1
    half_y = y >> 1
    upper_y = (y & 1) ^ half_y
    half, upper = half_y ^ odd_y, upper_y ^ odd_x
    inner = z ^ half
    row0 = sx * 256 + upper * 128 + core * 64
    col0 = sy * 256 + half * 128 + inner * 64
    return tm, odd_x, odd_y, core, upper, half, inner, row0, col0


def params():
    return pltpu.CompilerParams(vmem_limit_bytes=VMEM)


def cost(size):
    return pl.CostEstimate(flops=size, bytes_accessed=size, transcendentals=0)


def turn(value, shift):
    if isinstance(shift, int):
        return pltpu.roll(value, shift % 128, 1) if shift % 128 else value
    return pltpu.roll(value, lax.rem(shift + 256, 128), 1)


def prepare_kernel(other, forcing, out, held, arrived):
    tm, odd_x, odd_y, core = place()[:4]
    core = core ^ other
    copies = []
    for upper in range(2):
        copies.append(
            pltpu.make_async_copy(forcing.at[:, :, upper, core], held.at[upper], arrived.at[upper])
        )
        copies[upper].start()
    low = lanes(32) < 64
    weight = jnp.float32(1.0)
    for bit in range(4):
        step = math.exp(DECAY * 2 ** (bit + 1))
        weight = weight * jnp.where((tm >> bit & 1) == 1, step, 1.0).astype(jnp.float32)
    weight_two = weight * np.float32(FACTOR)
    weight_three = weight * np.float32(-FACTOR * FACTOR)
    for upper in range(2):
        copies[upper].wait()
        for half in range(2):
            cols = slice(128 * half, 128 * half + 128)
            first_u, second_u = held[upper, 0, 0, :, cols], held[upper, 0, 1, :, cols]
            first_w, second_w = held[upper, 1, 0, :, cols], held[upper, 1, 1, :, cols]
            units = (
                weight * (first_w + first_u),
                weight_two * (second_w + second_u - first_u),
                weight_three * second_u,
            )
            left = chip_of(half, upper, 0, odd_x, odd_y)
            right = chip_of(half, upper, 1, odd_x, odd_y)
            for k, unit in enumerate(units):
                rows = slice(32 * k, 32 * k + 32)
                out[left, rows, :] = pack_left(unit, low)
                out[right, rows, :] = pack_right(unit, low)


def prepare(forcing, other):
    return pl.pallas_call(
        functools.partial(prepare_kernel, other),
        in_specs=[pl.BlockSpec(memory_space=pltpu.HBM)],
        out_specs=pl.BlockSpec(memory_space=pltpu.VMEM),
        out_shape=jax.ShapeDtypeStruct((8, 96, 128), jnp.float32),
        scratch_shapes=[pltpu.VMEM((2, 2, 2, 64, 256), jnp.float32), pltpu.SemaphoreType.DMA((2,))],
        compiler_params=params(),
        cost_estimate=cost(2**20),
        name="prepare_other" if other else "prepare_own",
    )(forcing.reshape(2, 2, 2, 2, 64, 256))


def merge_kernel(mine, received, out):
    _, odd_x, odd_y, core = place()[:4]
    is_first = core == 0
    lane8 = lanes(8) % 64
    for chip in range(8):
        for k in range(3):
            rows = slice(32 * k, 32 * k + 32)
            own, other = mine[chip, rows, :], received[chip, rows, :]
            early, late = jnp.where(is_first, own, other), jnp.where(is_first, other, own)
            if k < 2:
                out[chip, 32 * k : 32 * k + 32, :] = early
                kept = late if k == 0 else kept
                if k == 1:
                    out[chip, 96:128, :] = late
            else:
                out[chip, 64:96, :] = kept + early
                out[chip, 128:160, :] = late
    for chip in range(8):
        inner = (chip & 1) ^ (chip >> 2) ^ odd_y
        for tile in range(3):
            value = jnp.zeros((8, 128), jnp.float32)
            for m in range(8):
                k, r = (8 * tile + m) // 4, m % 4
                if k == 5:
                    break
                beside = out[chip ^ 1, 32 * k + 8 * r : 32 * k + 8 * r + 8, :]
                here = (lane8 >= 8 * m) & (lane8 < 8 * m + 8)
                value = jnp.where(here, turn(beside, 8 * m - 56 * inner), value)
            out[chip, 160 + 8 * tile : 168 + 8 * tile, :] = value


def merge(mine, received):
    return pl.pallas_call(
        merge_kernel,
        in_specs=[pl.BlockSpec(memory_space=pltpu.VMEM)] * 2,
        out_specs=pl.BlockSpec(memory_space=pltpu.VMEM),
        out_shape=jax.ShapeDtypeStruct((8, 184, 128), jnp.float32),
        compiler_params=params(),
        name="merge",
    )(mine, received)


def scaled(factor, value):
    if abs(factor) < 1e-12:
        return None
    if abs(factor - 1.0) < 1e-12:
        return value
    if abs(factor + 1.0) < 1e-12:
        return -value
    return np.float32(factor) * value


def total_of(terms):
    terms = [term for term in terms if term is not None]
    result = terms[0]
    for term in terms[1:]:
        result = result + term
    return result


def angle(index):
    return 2.0 * math.pi * (index % STEPS) / STEPS


def forward(steps):
    even = [steps[0]] + [steps[n] + steps[32 - n] for n in range(1, 16)] + [steps[16]]
    odd = [None] + [steps[n] - steps[32 - n] for n in range(1, 16)]
    planes = [None] * 32
    for j in range(9):
        cos_even = total_of([scaled(math.cos(angle(j * n)), even[n]) for n in range(0, 17, 2)])
        cos_odd = (
            None if j == 8 else total_of([scaled(math.cos(angle(j * n)), even[n]) for n in range(1, 17, 2)])
        )
        high, lowp = (
            (cos_even, None) if cos_odd is None else (cos_even + cos_odd, cos_even - cos_odd)
        )
        if j == 0:
            planes[0], planes[1] = high, lowp
            continue
        planes[2 * j] = high
        if j < 8:
            planes[2 * (16 - j)] = lowp
        sin_odd = total_of([scaled(math.sin(angle(j * n)), odd[n]) for n in range(1, 16, 2)])
        if j == 8:
            planes[2 * j + 1] = -sin_odd
            continue
        sin_even = total_of([scaled(math.sin(angle(j * n)), odd[n]) for n in range(2, 16, 2)])
        planes[2 * j + 1] = -(sin_even + sin_odd)
        planes[2 * (16 - j) + 1] = sin_even - sin_odd
    return planes


def backward(planes):
    real = [planes[0]] + [planes[2 * j] * 2.0 for j in range(1, 16)] + [planes[1]]
    imag = [None] + [planes[2 * j + 1] * 2.0 for j in range(1, 16)]
    steps = [None] * 32

    def put(n, cosine, sine):
        if n in (0, 16):
            steps[n] = cosine
            return
        steps[n] = cosine - sine
        steps[32 - n] = cosine + sine

    for n in range(9):
        cos_even = total_of([scaled(math.cos(angle(j * n)), real[j]) for j in range(0, 17, 2)])
        if n == 8:
            sine = total_of([scaled(math.sin(angle(j * n)), imag[j]) for j in range(1, 16, 2)])
            put(8, cos_even, sine)
            continue
        cos_odd = total_of([scaled(math.cos(angle(j * n)), real[j]) for j in range(1, 17, 2)])
        if n == 0:
            put(0, cos_even + cos_odd, None)
            put(16, cos_even - cos_odd, None)
            continue
        sin_odd = total_of([scaled(math.sin(angle(j * n)), imag[j]) for j in range(1, 16, 2)])
        sin_even = total_of([scaled(math.sin(angle(j * n)), imag[j]) for j in range(2, 16, 2)])
        put(n, cos_even + cos_odd, sin_even + sin_odd)
        put(16 - n, cos_even - cos_odd, sin_odd - sin_even)
    return steps


def transform_kernel(
    table, cell_class, initial, last, received, planes_out, beside_out, side_out, core_out, cross_out
):
    _, _, _, core, upper, half, inner = place()[:7]
    low8, low32 = lanes(8) < 64, lanes(32) < 64
    lane8 = lanes(8) % 64
    rows = pl.ds(pl.multiple_of((upper * 2 + core) * 64, 64), 64)
    cols = pl.ds(pl.multiple_of(half * 128, 128), 128)
    is_right = inner == 1

    def slots(m):
        return (lane8 >= 8 * m) & (lane8 < 8 * m + 8)

    def own_and_beside(value):
        turned = half_turn(value)
        own = pack_left(jnp.where(is_right, turned, value), low32)
        other = pack_left(jnp.where(is_right, value, turned), low32)
        beside = jnp.zeros((8, 128), jnp.float32)
        for r in range(4):
            beside = jnp.where(slots(r), turn(other[8 * r : 8 * r + 8], 8 * r - 56 * inner), beside)
        return [own[8 * r : 8 * r + 8] for r in range(4)] + [beside]

    classes = cell_class[rows, cols]
    courant = jnp.zeros(classes.shape, jnp.float32)
    for k in range(8):
        courant = jnp.where(classes == k, table[k], courant)
    courant = own_and_beside(courant)
    start_u, start_w = (
        own_and_beside(initial[c, rows, cols] - ALPHA * last[c, rows, cols]) for c in range(2)
    )

    for r in range(5):
        steps = []
        for t in range(8):
            before = (t + 7) % 8
            if r < 4:
                part = [received[t, 32 * k + 8 * r : 32 * k + 8 * r + 8, :] for k in range(4)]
                part[0] = part[0] + received[before, 128 + 8 * r : 136 + 8 * r, :]
            else:
                one, two = received[t, 160:168, :], received[t, 168:176, :]
                part = [one + received[before, 176:184, :], turn(one, -32), two, turn(two, -32)]
            steps.extend(part)
        steps[0] = steps[0] + (start_w[r] + start_u[r])
        steps[1] = steps[1] - np.float32(FACTOR) * start_u[r]
        planes = forward(steps) + [courant[r]]
        if r == 4:
            for p in range(33):
                beside_out[p] = planes[p]
        else:
            for p in range(33):
                planes_out[p, 8 * r : 8 * r + 8, :] = planes[p]
            for g in range(5):
                value = jnp.zeros((8, 128), jnp.float32)
                for m, plane in enumerate(planes[8 * g : 8 * g + 8]):
                    value = jnp.where(slots(m), turn(plane, 8 * m - 56 * inner), value)
                side_out[g, 8 * r : 8 * r + 8, :] = value
        if r == 0:
            pairs = planes + [planes[32]]
            top = [jnp.where(low8, pairs[2 * j], half_turn(pairs[2 * j + 1])) for j in range(17)]
        if r == 3:
            pairs = planes + [planes[32]]
            bottom = [jnp.where(low8, half_turn(pairs[2 * j]), pairs[2 * j + 1]) for j in range(17)]
        if r == 4:
            for strip, start in ((top, 0), (bottom, 88)):
                for g in range(5):
                    value = jnp.zeros((8, 128), jnp.float32)
                    for m, plane in enumerate(planes[8 * g : 8 * g + 8]):
                        value = jnp.where(slots(m), turn(plane, 8 * m - start), value)
                    strip.append(value)
    for i in range(22):
        core_out[i] = jnp.where(core == 0, bottom[i], top[i])
        cross_out[i] = jnp.where(core == 0, top[i], bottom[i])


def transform(table, cell_class, initial, last, received):
    shapes = ((33, 32, 128), (33, 8, 128), (5, 32, 128), (22, 8, 128), (22, 8, 128))
    return pl.pallas_call(
        transform_kernel,
        in_specs=[pl.BlockSpec(memory_space=pltpu.SMEM)] + [pl.BlockSpec(memory_space=pltpu.VMEM)] * 4,
        out_specs=[pl.BlockSpec(memory_space=pltpu.VMEM)] * 5,
        out_shape=[jax.ShapeDtypeStruct(shape, jnp.float32) for shape in shapes],
        compiler_params=params(),
        name="transform",
    )(table, cell_class, initial, last, received)


def around(field):
    first = pltpu.roll(field[9], 1, 0)
    last = pltpu.roll(field[0], 7, 0)
    above = [first] + field[:9]
    below = field[1:] + [last]
    return [
        (up + down) + (pltpu.roll(own, 1, 1) + pltpu.roll(own, 127, 1))
        for up, own, down in zip(above, field, below)
    ]


def solve_kernel(lam, planes, beside, from_side, from_core, from_cross, out, solved, wide, own):
    core, _, _, inner, row0, col0 = place()[3:]
    low = lanes(32) < 64
    is_lower = core == 1
    side_base = 120 - 56 * inner
    beside_base = 64 + 56 * inner

    def within(lane, base):
        return (lane >= base) & (lane < base + 8)

    side_lanes, beside_lanes = within(lanes(8), side_base), within(lanes(8), beside_base)
    low8 = lanes(8) < 64

    def halo(index):
        return (
            jnp.where(is_lower, from_core[index], from_cross[index]),
            jnp.where(is_lower, from_cross[index], from_core[index]),
        )

    def merged(centre, side, other):
        value = jnp.where(low8, centre, 0.0)
        value = jnp.where(side_lanes, side, value)
        return jnp.where(beside_lanes, other, value)

    def extended(p, pair, odd, group, offset):
        edge = beside[p]
        top_main, bottom_main = halo(pair)
        if odd:
            top_main, bottom_main = half_turn(top_main), half_turn(bottom_main)
        top_beside, bottom_beside = halo(17 + group)
        top_side, bottom_side = halo(22 + group)
        parts = [
            merged(
                top_main,
                turn(top_side, side_base - 64 - offset),
                turn(top_beside, beside_base - offset),
            )
        ]
        for r in range(8):
            part = slice(8 * (r % 4), 8 * (r % 4) + 8)
            centre, shift = planes[p, part, :], 0 if r < 4 else 64
            parts.append(
                merged(
                    turn(centre, shift),
                    turn(from_side[group, part, :], side_base - shift - offset),
                    turn(edge, beside_base - shift - 8 * (r % 4)),
                )
            )
        parts.append(
            merged(
                bottom_main,
                turn(bottom_side, side_base - offset),
                turn(bottom_beside, beside_base - offset),
            )
        )
        return jnp.concatenate(parts, axis=0)

    def spread(slot, value):
        wide[slot] = value
        return [wide[slot, pl.ds(v, 8, stride=10), :] for v in range(10)]

    def keep(p, slot, field):
        for v in range(10):
            wide[slot, pl.ds(v, 8, stride=10), :] = field[v]
        solved[p] = jnp.where(low, wide[slot, 8:40, :], half_turn(wide[slot, 40:72, :]))

    rows = lax.broadcasted_iota(jnp.int32, (80, 128), 0) - 8 + row0
    lane80 = lanes(80)
    cols = jnp.where(lane80 >= 120, lane80 - 128, lane80) + col0
    inside = (rows >= 0) & (rows < 1024) & (cols >= 0) & (cols < 1024) & ((lane80 < 72) | (lane80 >= 120))
    courant = spread(0, jnp.where(inside, extended(32, 16, False, 4, 0), 0.0))
    inner = spread(1, jnp.where(inside, 1.0, 0.0))
    for v in range(10):
        own[0, v] = courant[v]
        own[1, v] = inner[v]

    def prepared(j, slot, special, group, offset):
        g_re = spread(2 * slot, extended(2 * j, j, False, group, offset))
        g_im = spread(2 * slot + 1, extended(2 * j + 1, j, True, group, offset + 8))
        start_re, start_im, gain_re, gain_im = [], [], [], []
        for v in range(10):
            speed, kept = own[0, v], own[1, v]
            if special:
                inv_re = kept / (lam[0, 0] + 4.0 * speed)
                inv_im = kept / (lam[0, 1] + 4.0 * speed)
                start_re.append(g_re[v] * inv_re)
                start_im.append(g_im[v] * inv_im)
            else:
                diag_re = lam[j, 0] + 4.0 * speed
                diag_im = lam[j, 1]
                scale = kept / (diag_re * diag_re + diag_im * diag_im)
                inv_re = diag_re * scale
                inv_im = -diag_im * scale
                start_re.append(g_re[v] * inv_re - g_im[v] * inv_im)
                start_im.append(g_re[v] * inv_im + g_im[v] * inv_re)
            gain_re.append(speed * inv_re)
            gain_im.append(speed * inv_im)
        return start_re, start_im, gain_re, gain_im

    def swept(special, start_re, start_im, gain_re, gain_im, re, im):
        all_re, all_im = around(re), around(im)
        if special:
            return (
                [start_re[v] + gain_re[v] * all_re[v] for v in range(10)],
                [start_im[v] + gain_im[v] * all_im[v] for v in range(10)],
            )
        return (
            [start_re[v] + (gain_re[v] * all_re[v] - gain_im[v] * all_im[v]) for v in range(10)],
            [start_im[v] + (gain_re[v] * all_im[v] + gain_im[v] * all_re[v]) for v in range(10)],
        )

    def batch(k, has_special):
        sets, fields = [], []
        for i in range(BATCH):
            special = has_special and i == 0
            j = k * BATCH + i
            sets.append((special,) + prepared(j, i, special, j >> 2, (j & 3) * 16))
            fields.append((sets[i][1], sets[i][2]))
        for _ in range(SWEEPS - 1):
            fields = [swept(*sets[i], *fields[i]) for i in range(BATCH)]
        for i in range(BATCH):
            j = k * BATCH + i
            keep(2 * j, 2 * i, fields[i][0])
            keep(2 * j + 1, 2 * i + 1, fields[i][1])

    def later(k, carry):
        batch(k, False)
        return carry

    batch(0, True)
    lax.fori_loop(1, 16 // BATCH, later, 0)

    for r in range(4):
        part = slice(8 * r, 8 * r + 8)
        steps = backward([solved[p, part, :] for p in range(32)])
        for n in range(32):
            value = steps[n] * np.float32(math.exp(-n * DECAY) / STEPS)
            t, k = n // 4, n % 4
            out[t, 32 * k + 32 + 8 * r : 32 * k + 40 + 8 * r, :] = value
            if k == 3:
                out[(t + 1) % 8, part, :] = value * np.float32(ALPHA) if n == 31 else value


def solve(lam, planes, beside, from_side, from_core, from_cross):
    return pl.pallas_call(
        solve_kernel,
        in_specs=[pl.BlockSpec(memory_space=pltpu.SMEM)] + [pl.BlockSpec(memory_space=pltpu.VMEM)] * 5,
        out_specs=pl.BlockSpec(memory_space=pltpu.VMEM),
        out_shape=jax.ShapeDtypeStruct((8, 160, 128), jnp.float32),
        scratch_shapes=[
            pltpu.VMEM((32, 32, 128), jnp.float32),
            pltpu.VMEM((2 * BATCH, 80, 128), jnp.float32),
            pltpu.VMEM((2, 10, 8, 128), jnp.float32),
        ],
        compiler_params=params(),
        name="solve",
    )(lam, planes, beside, from_side, from_core, from_cross)


def finish_kernel(other, units, forcing, initial, last, *refs):
    out, held, sent = refs[-3:]
    tm, odd_x, odd_y, core = place()[:4]
    low = lanes(32) < 64
    first = jnp.where(tm == 0, 1.0, 0.0).astype(jnp.float32)
    begin = 0 if other else pl.multiple_of(64 * core, 64)
    core = core ^ other
    copies = []
    for upper in range(2):
        for half in range(2):
            cols = slice(128 * half, 128 * half + 128)
            ones, twos = (
                [units[chip, pl.ds(begin + 32 * k, 32), :] for k in range(3)]
                for chip in (chip_of(half, upper, inner, odd_x, odd_y) for inner in range(2))
            )
            for part in range(2):
                rows = slice(32 * part, 32 * part + 32)
                if part == 0:
                    values = [jnp.where(low, one, half_turn(two)) for one, two in zip(ones, twos)]
                else:
                    values = [jnp.where(low, half_turn(one), two) for one, two in zip(ones, twos)]
                before, now, after = values
                start = forcing[0, 0, upper, core, rows, cols] + first * (
                    initial[0, upper, core, rows, cols] - ALPHA * last[0, upper, core, rows, cols]
                )
                held[upper, 0, 0, rows, cols] = now
                held[upper, 0, 1, rows, cols] = after
                held[upper, 1, 0, rows, cols] = now - before - start
                held[upper, 1, 1, rows, cols] = after - now - forcing[0, 1, upper, core, rows, cols]
        copies.append(pltpu.make_async_copy(held.at[upper], out.at[:, :, upper, core], sent.at[upper]))
        copies[upper].start()
    for upper in range(2):
        copies[upper].wait()


def finish(units, forcing, initial, last, result=None):
    other = result is not None
    return pl.pallas_call(
        functools.partial(finish_kernel, int(other)),
        in_specs=[pl.BlockSpec(memory_space=pltpu.VMEM)] * 4
        + [pl.BlockSpec(memory_space=pltpu.HBM)] * other,
        out_specs=pl.BlockSpec(memory_space=pltpu.HBM),
        out_shape=jax.ShapeDtypeStruct((2, 2, 2, 2, 64, 256), jnp.float32),
        scratch_shapes=[pltpu.VMEM((2, 2, 2, 64, 256), jnp.float32), pltpu.SemaphoreType.DMA((2,))],
        input_output_aliases={4: 0} if other else {},
        compiler_params=params(),
        cost_estimate=cost(2**20),
        name="finish_other" if other else "finish_own",
    )(
        units,
        forcing.reshape(2, 2, 2, 2, 64, 256),
        initial.reshape(2, 2, 2, 64, 256),
        last.reshape(2, 2, 2, 64, 256),
        *([result] if other else []),
    )


def lam_squares():
    rows = []
    for j in range(16):
        lam = 1.0 - FACTOR * complex(math.cos(angle(j)), -math.sin(angle(j)))
        square = lam * lam
        rows.append((square.real, square.imag))
    rows[0] = ((1.0 - FACTOR) ** 2, (1.0 + FACTOR) ** 2)
    return np.array(rows, np.float32)


def chips_exchange(pieces):
    return lax.all_to_all(pieces, "tm", 0, 0, axis_index_groups=CHIPS, tiled=True)


def per_device(forcing, initial, previous_last, cell_class, courant_table):
    core = lax.axis_index("tm") & 1
    lam = jnp.asarray(lam_squares())
    theirs = lax.ppermute(prepare(forcing, 1), "tm", CORES)
    received = chips_exchange(merge(prepare(forcing, 0), theirs))
    planes, beside, side, to_core, to_cross = transform(
        courant_table, cell_class, initial, previous_last, received
    )
    from_side = lax.ppermute(side, AXES, TO_SIDE)

    def strip(main, start):
        return jnp.concatenate([main, lax.dynamic_slice_in_dim(from_side, start, 8, axis=1)], axis=0)

    from_core = lax.ppermute(strip(to_core, 24 * (1 - core)), AXES, TO_CORE)
    from_cross = lax.ppermute(strip(to_cross, 24 * core), AXES, TO_CROSS)
    returned = chips_exchange(solve(lam, planes, beside, from_side, from_core, from_cross))
    wanted = lax.dynamic_slice_in_dim(returned, 64 * (1 - core), 96, axis=1)
    other = lax.ppermute(wanted, "tm", CORES)
    result = finish(returned, forcing, initial, previous_last)
    result = finish(other, forcing, initial, previous_last, result)
    return result.reshape(2, 2, 256, 256)


def solution(mesh):
    in_specs = (
        P(None, "tm", "sx", "sy"),
        P(None, "sx", "sy"),
        P(None, "sx", "sy"),
        P("sx", "sy"),
        P(),
    )
    out_specs = P(None, "tm", "sx", "sy")
    return jax.shard_map(
        per_device, mesh=mesh, in_specs=in_specs, out_specs=out_specs, check_vma=False
    )
```

```python
import functools
import math

import jax
import jax.numpy as jnp
import numpy as np
from jax import lax
from jax.experimental import pallas as pl
from jax.experimental.pallas import tpu as pltpu
from jax.sharding import PartitionSpec as P

STEPS = 32
SWEEPS = 8
BATCH = 8
ALPHA = 0.1
DECAY = math.log(ALPHA) / STEPS
FACTOR = math.exp(DECAY)
AXES = ("tm", "sx", "sy")
VMEM = 16 * 2**20


def chip_of(half, upper, inner, odd_x, odd_y):
    half_y, upper_y = half ^ odd_y, upper ^ odd_x
    return (2 * half_y + (upper_y ^ half_y)) * 2 + (inner ^ half)


def device_of(row, col):
    row, col = row % 16, col % 16
    sx, upper, core = row // 4, row // 2 % 2, row % 2
    sy, half, inner = col // 4, col // 2 % 2, col % 2
    tm = chip_of(half, upper, inner, sx & 1, sy & 1) * 2 + core
    return (tm * 4 + sx) * 4 + sy


def pairs_of(move):
    return [
        (device_of(row, col), device_of(*move(row, col))) for row in range(16) for col in range(16)
    ]


def away(index):
    return index - 1 if index % 2 == 0 else index + 1


def side_of(row, col):
    return (row, away(col)) if 0 < col < 15 else (row ^ 1, col)


TO_SIDE = pairs_of(side_of)
TO_CORE = pairs_of(lambda row, col: (row ^ 1, col))
TO_CROSS = pairs_of(lambda row, col: (away(row), col))
CHIPS = [[chip * 2 + core for chip in range(8)] for core in range(2)]
CORES = [(tm, tm ^ 1) for tm in range(16)]


def lanes(rows):
    return lax.broadcasted_iota(jnp.int32, (rows, 128), 1)


def half_turn(value):
    return pltpu.roll(value, 64, 1)


def pack_left(value, low):
    return jnp.where(low, value[:32], half_turn(value[32:]))


def pack_right(value, low):
    return jnp.where(low, half_turn(value[:32]), value[32:])


def place():
    tm, sx, sy = (lax.axis_index(axis) for axis in AXES)
    odd_x, odd_y = sx & 1, sy & 1
    y, z, core = tm >> 2, tm >> 1 & 1, tm & 1
    half_y = y >> 1
    upper_y = (y & 1) ^ half_y
    half, upper = half_y ^ odd_y, upper_y ^ odd_x
    inner = z ^ half
    row0 = sx * 256 + upper * 128 + core * 64
    col0 = sy * 256 + half * 128 + inner * 64
    return tm, odd_x, odd_y, core, upper, half, inner, row0, col0


def params():
    return pltpu.CompilerParams(vmem_limit_bytes=VMEM)


def cost(size):
    return pl.CostEstimate(flops=size, bytes_accessed=size, transcendentals=0)


def turn(value, shift):
    if isinstance(shift, int):
        return pltpu.roll(value, shift % 128, 1) if shift % 128 else value
    return pltpu.roll(value, lax.rem(shift + 256, 128), 1)


def prepare_kernel(other, forcing, out, held, arrived):
    tm, odd_x, odd_y, core = place()[:4]
    core = core ^ other
    copies = []
    for upper in range(2):
        copies.append(
            pltpu.make_async_copy(forcing.at[:, :, upper, core], held.at[upper], arrived.at[upper])
        )
        copies[upper].start()
    low = lanes(32) < 64
    weight = jnp.float32(1.0)
    for bit in range(4):
        step = math.exp(DECAY * 2 ** (bit + 1))
        weight = weight * jnp.where((tm >> bit & 1) == 1, step, 1.0).astype(jnp.float32)
    weight_two = weight * np.float32(FACTOR)
    weight_three = weight * np.float32(-FACTOR * FACTOR)
    for upper in range(2):
        copies[upper].wait()
        for half in range(2):
            cols = slice(128 * half, 128 * half + 128)
            first_u, second_u = held[upper, 0, 0, :, cols], held[upper, 0, 1, :, cols]
            first_w, second_w = held[upper, 1, 0, :, cols], held[upper, 1, 1, :, cols]
            units = (
                weight * (first_w + first_u),
                weight_two * (second_w + second_u - first_u),
                weight_three * second_u,
            )
            left = chip_of(half, upper, 0, odd_x, odd_y)
            right = chip_of(half, upper, 1, odd_x, odd_y)
            for k, unit in enumerate(units):
                rows = slice(32 * k, 32 * k + 32)
                out[left, rows, :] = pack_left(unit, low)
                out[right, rows, :] = pack_right(unit, low)


def prepare(forcing, other):
    return pl.pallas_call(
        functools.partial(prepare_kernel, other),
        in_specs=[pl.BlockSpec(memory_space=pltpu.HBM)],
        out_specs=pl.BlockSpec(memory_space=pltpu.VMEM),
        out_shape=jax.ShapeDtypeStruct((8, 96, 128), jnp.float32),
        scratch_shapes=[pltpu.VMEM((2, 2, 2, 64, 256), jnp.float32), pltpu.SemaphoreType.DMA((2,))],
        compiler_params=params(),
        cost_estimate=cost(2**20),
        name="prepare_other" if other else "prepare_own",
    )(forcing.reshape(2, 2, 2, 2, 64, 256))


def merge_kernel(mine, received, out):
    _, odd_x, odd_y, core = place()[:4]
    is_first = core == 0
    lane8 = lanes(8) % 64
    for chip in range(8):
        for k in range(3):
            rows = slice(32 * k, 32 * k + 32)
            own, other = mine[chip, rows, :], received[chip, rows, :]
            early, late = jnp.where(is_first, own, other), jnp.where(is_first, other, own)
            if k < 2:
                out[chip, 32 * k : 32 * k + 32, :] = early
                kept = late if k == 0 else kept
                if k == 1:
                    out[chip, 96:128, :] = late
            else:
                out[chip, 64:96, :] = kept + early
                out[chip, 128:160, :] = late
    for chip in range(8):
        inner = (chip & 1) ^ (chip >> 2) ^ odd_y
        for tile in range(3):
            value = jnp.zeros((8, 128), jnp.float32)
            for m in range(8):
                k, r = (8 * tile + m) // 4, m % 4
                if k == 5:
                    break
                beside = out[chip ^ 1, 32 * k + 8 * r : 32 * k + 8 * r + 8, :]
                here = (lane8 >= 8 * m) & (lane8 < 8 * m + 8)
                value = jnp.where(here, turn(beside, 8 * m - 56 * inner), value)
            out[chip, 160 + 8 * tile : 168 + 8 * tile, :] = value


def merge(mine, received):
    return pl.pallas_call(
        merge_kernel,
        in_specs=[pl.BlockSpec(memory_space=pltpu.VMEM)] * 2,
        out_specs=pl.BlockSpec(memory_space=pltpu.VMEM),
        out_shape=jax.ShapeDtypeStruct((8, 184, 128), jnp.float32),
        compiler_params=params(),
        name="merge",
    )(mine, received)


def scaled(factor, value):
    if abs(factor) < 1e-12:
        return None
    if abs(factor - 1.0) < 1e-12:
        return value
    if abs(factor + 1.0) < 1e-12:
        return -value
    return np.float32(factor) * value


def total_of(terms):
    terms = [term for term in terms if term is not None]
    result = terms[0]
    for term in terms[1:]:
        result = result + term
    return result


def angle(index):
    return 2.0 * math.pi * (index % STEPS) / STEPS


def forward(steps):
    even = [steps[0]] + [steps[n] + steps[32 - n] for n in range(1, 16)] + [steps[16]]
    odd = [None] + [steps[n] - steps[32 - n] for n in range(1, 16)]
    planes = [None] * 32
    for j in range(9):
        cos_even = total_of([scaled(math.cos(angle(j * n)), even[n]) for n in range(0, 17, 2)])
        cos_odd = (
            None if j == 8 else total_of([scaled(math.cos(angle(j * n)), even[n]) for n in range(1, 17, 2)])
        )
        high, lowp = (
            (cos_even, None) if cos_odd is None else (cos_even + cos_odd, cos_even - cos_odd)
        )
        if j == 0:
            planes[0], planes[1] = high, lowp
            continue
        planes[2 * j] = high
        if j < 8:
            planes[2 * (16 - j)] = lowp
        sin_odd = total_of([scaled(math.sin(angle(j * n)), odd[n]) for n in range(1, 16, 2)])
        if j == 8:
            planes[2 * j + 1] = -sin_odd
            continue
        sin_even = total_of([scaled(math.sin(angle(j * n)), odd[n]) for n in range(2, 16, 2)])
        planes[2 * j + 1] = -(sin_even + sin_odd)
        planes[2 * (16 - j) + 1] = sin_even - sin_odd
    return planes


def backward(planes):
    real = [planes[0]] + [planes[2 * j] * 2.0 for j in range(1, 16)] + [planes[1]]
    imag = [None] + [planes[2 * j + 1] * 2.0 for j in range(1, 16)]
    steps = [None] * 32

    def put(n, cosine, sine):
        if n in (0, 16):
            steps[n] = cosine
            return
        steps[n] = cosine - sine
        steps[32 - n] = cosine + sine

    for n in range(9):
        cos_even = total_of([scaled(math.cos(angle(j * n)), real[j]) for j in range(0, 17, 2)])
        if n == 8:
            sine = total_of([scaled(math.sin(angle(j * n)), imag[j]) for j in range(1, 16, 2)])
            put(8, cos_even, sine)
            continue
        cos_odd = total_of([scaled(math.cos(angle(j * n)), real[j]) for j in range(1, 17, 2)])
        if n == 0:
            put(0, cos_even + cos_odd, None)
            put(16, cos_even - cos_odd, None)
            continue
        sin_odd = total_of([scaled(math.sin(angle(j * n)), imag[j]) for j in range(1, 16, 2)])
        sin_even = total_of([scaled(math.sin(angle(j * n)), imag[j]) for j in range(2, 16, 2)])
        put(n, cos_even + cos_odd, sin_even + sin_odd)
        put(16 - n, cos_even - cos_odd, sin_odd - sin_even)
    return steps


def slots(m):
    lane = lanes(8) % 64
    return (lane >= 8 * m) & (lane < 8 * m + 8)


def in_slots(planes, start):
    groups = []
    for g in range(5):
        value = jnp.zeros((8, 128), jnp.float32)
        for m, plane in enumerate(planes[8 * g : 8 * g + 8]):
            value = jnp.where(slots(m), turn(plane, 8 * m - start), value)
        groups.append(value)
    return groups


def block_of(value, inner):
    return pack_left(jnp.where(inner == 1, half_turn(value), value), lanes(32) < 64)


def beside_of(value, inner):
    other = block_of(value, 1 - inner)
    beside = jnp.zeros((8, 128), jnp.float32)
    for r in range(4):
        beside = jnp.where(slots(r), turn(other[8 * r : 8 * r + 8], 8 * r - 56 * inner), beside)
    return beside


def pair_fields(table, cell_class, initial, last):
    core, upper, half = place()[3:6]
    rows = pl.ds(pl.multiple_of((upper * 2 + core) * 64, 64), 64)
    cols = pl.ds(pl.multiple_of(half * 128, 128), 128)
    classes = cell_class[rows, cols]
    courant = jnp.zeros(classes.shape, jnp.float32)
    for k in range(8):
        courant = jnp.where(classes == k, table[k], courant)
    return [courant] + [initial[c, rows, cols] - ALPHA * last[c, rows, cols] for c in range(2)]


def with_start(steps, start_u, start_w):
    return [steps[0] + (start_w + start_u), steps[1] - np.float32(FACTOR) * start_u] + steps[2:]


def transform_kernel(table, cell_class, initial, last, received, planes_out, side_out):
    inner = place()[6]
    courant, start_u, start_w = (
        block_of(value, inner) for value in pair_fields(table, cell_class, initial, last)
    )
    for r in range(4):
        rows = slice(8 * r, 8 * r + 8)
        steps = []
        for t in range(8):
            part = [received[t, 32 * k + 8 * r : 32 * k + 8 * r + 8, :] for k in range(4)]
            part[0] = part[0] + received[(t + 7) % 8, 128 + 8 * r : 136 + 8 * r, :]
            steps.extend(part)
        planes = forward(with_start(steps, start_u[rows], start_w[rows])) + [courant[rows]]
        for p in range(33):
            planes_out[p, rows, :] = planes[p]
        for g, value in enumerate(in_slots(planes, 56 * inner)):
            side_out[g, rows, :] = value


def transform(table, cell_class, initial, last, received):
    shapes = ((33, 32, 128), (5, 32, 128))
    return pl.pallas_call(
        transform_kernel,
        in_specs=[pl.BlockSpec(memory_space=pltpu.SMEM)] + [pl.BlockSpec(memory_space=pltpu.VMEM)] * 4,
        out_specs=[pl.BlockSpec(memory_space=pltpu.VMEM)] * 2,
        out_shape=[jax.ShapeDtypeStruct(shape, jnp.float32) for shape in shapes],
        compiler_params=params(),
        name="transform",
    )(table, cell_class, initial, last, received)


def strips_kernel(
    table, cell_class, initial, last, received, planes, beside_out, core_out, cross_out
):
    core, _, _, inner = place()[3:7]
    low = lanes(8) < 64
    courant, start_u, start_w = (
        beside_of(value, inner) for value in pair_fields(table, cell_class, initial, last)
    )
    steps = []
    for t in range(8):
        one, two = received[t, 160:168, :], received[t, 168:176, :]
        first = one + received[(t + 7) % 8, 176:184, :]
        steps.extend([first, turn(one, -32), two, turn(two, -32)])
    beside = forward(with_start(steps, start_u, start_w)) + [courant]
    for p in range(33):
        beside_out[p] = beside[p]
    top, bottom = [], []
    for j in range(17):
        one, two = 2 * j, min(2 * j + 1, 32)
        top.append(jnp.where(low, planes[one, 0:8, :], half_turn(planes[two, 0:8, :])))
        bottom.append(jnp.where(low, half_turn(planes[one, 24:32, :]), planes[two, 24:32, :]))
    top.extend(in_slots(beside, 0))
    bottom.extend(in_slots(beside, 88))
    for i in range(22):
        core_out[i] = jnp.where(core == 0, bottom[i], top[i])
        cross_out[i] = jnp.where(core == 0, top[i], bottom[i])


def strips(table, cell_class, initial, last, received, planes):
    shapes = ((33, 8, 128), (22, 8, 128), (22, 8, 128))
    return pl.pallas_call(
        strips_kernel,
        in_specs=[pl.BlockSpec(memory_space=pltpu.SMEM)] + [pl.BlockSpec(memory_space=pltpu.VMEM)] * 5,
        out_specs=[pl.BlockSpec(memory_space=pltpu.VMEM)] * 3,
        out_shape=[jax.ShapeDtypeStruct(shape, jnp.float32) for shape in shapes],
        compiler_params=params(),
        cost_estimate=cost(2**20),
        name="strips",
    )(table, cell_class, initial, last, received, planes)


def side_matrix():
    rows = lax.broadcasted_iota(jnp.int32, (256, 128), 0) % 128
    gap = (rows - lax.broadcasted_iota(jnp.int32, (256, 128), 1)) % 128
    return jnp.where((gap == 1) | (gap == 127), 1.0, 0.0).astype(jnp.bfloat16)


def sides_by_matrix(field, matrix):
    value = jnp.concatenate(field, axis=0)
    high = value.astype(jnp.bfloat16)
    low = (value - high.astype(jnp.float32)).astype(jnp.bfloat16)
    result = jnp.dot(jnp.concatenate([high, low], axis=1), matrix, preferred_element_type=jnp.float32)
    return [result[8 * v : 8 * v + 8] for v in range(10)]


def sides_by_rotation(field):
    return [pltpu.roll(own, 1, 1) + pltpu.roll(own, 127, 1) for own in field]


def around(field, sides):
    first = pltpu.roll(field[9], 1, 0)
    last = pltpu.roll(field[0], 7, 0)
    above = [first] + field[:9]
    below = field[1:] + [last]
    return [(up + down) + side for up, side, down in zip(above, sides, below)]


def bases(inner):
    return 120 - 56 * inner, 64 + 56 * inner


def merged(centre, side, other, bases):
    lane = lanes(8)
    value = jnp.where(lane < 64, centre, 0.0)
    for base, edge in zip(bases, (side, other)):
        value = jnp.where((lane >= base) & (lane < base + 8), edge, value)
    return value


def in_grid(first_row, count, col0):
    rows = lax.broadcasted_iota(jnp.int32, (count, 128), 0) + first_row
    lane = lanes(count)
    cols = jnp.where(lane >= 120, lane - 128, lane) + col0
    used = (lane < 72) | (lane >= 120)
    return used & (rows >= 0) & (rows < 1024) & (cols >= 0) & (cols < 1024)


def coefficients(lam, j, special, g_re, g_im, courant, inside):
    if special:
        inv_re = inside / (lam[0, 0] + 4.0 * courant)
        inv_im = inside / (lam[0, 1] + 4.0 * courant)
        return g_re * inv_re, g_im * inv_im, courant * inv_re, courant * inv_im
    diag_re = lam[j, 0] + 4.0 * courant
    diag_im = lam[j, 1]
    scale = inside / (diag_re * diag_re + diag_im * diag_im)
    inv_re = diag_re * scale
    inv_im = -diag_im * scale
    return (
        g_re * inv_re - g_im * inv_im,
        g_re * inv_im + g_im * inv_re,
        courant * inv_re,
        courant * inv_im,
    )


def over_frequencies(work):
    for j in range(4):
        work(j, j == 0, 0, 16 * j)

    def group(k, carry):
        for i in range(4):
            work(4 * k + i, False, k, 16 * i)
        return carry

    lax.fori_loop(1, 4, group, 0)


def widen_kernel(lam, planes, beside, from_side, out):
    inner, _, col0 = place()[6:]
    both = bases(inner)

    def extended(p, group, offset):
        edge = beside[p]
        parts = []
        for r in range(8):
            part = slice(8 * (r % 4), 8 * (r % 4) + 8)
            shift = 0 if r < 4 else 64
            parts.append(
                merged(
                    turn(planes[p, part, :], shift),
                    turn(from_side[group, part, :], both[0] - shift - offset),
                    turn(edge, both[1] - shift - 8 * (r % 4)),
                    both,
                )
            )
        return jnp.concatenate(parts, axis=0)

    mask = in_grid(0, 64, col0)
    courant = jnp.where(mask, extended(32, 4, 0), 0.0)
    inside = jnp.where(mask, 1.0, 0.0)

    def work(j, special, group, offset):
        g_re, g_im = extended(2 * j, group, offset), extended(2 * j + 1, group, offset + 8)
        for i, value in enumerate(coefficients(lam, j, special, g_re, g_im, courant, inside)):
            out[j, i, 8:72, :] = value

    over_frequencies(work)


def widen(lam, planes, beside, from_side):
    return pl.pallas_call(
        widen_kernel,
        in_specs=[pl.BlockSpec(memory_space=pltpu.SMEM)] + [pl.BlockSpec(memory_space=pltpu.VMEM)] * 3,
        out_specs=pl.BlockSpec(memory_space=pltpu.VMEM),
        out_shape=jax.ShapeDtypeStruct((16, 4, 80, 128), jnp.float32),
        compiler_params=params(),
        cost_estimate=cost(2**21),
        name="widen",
    )(lam, planes, beside, from_side)


def solve_kernel(lam, middle, from_core, from_cross, out, full, solved, wide):
    core, _, _, inner, row0, col0 = place()[3:]
    both = bases(inner)
    low = lanes(32) < 64
    matrix = side_matrix()

    def halo(index):
        one, two = from_core[index], from_cross[index]
        return jnp.where(core == 1, one, two), jnp.where(core == 1, two, one)

    def extended(pair, odd, group, offset):
        centre, edge, side = halo(pair), halo(17 + group), halo(22 + group)
        return jnp.concatenate(
            [
                merged(
                    half_turn(centre[i]) if odd else centre[i],
                    turn(side[i], both[0] - offset - (0 if i else 64)),
                    turn(edge[i], both[1] - offset),
                    both,
                )
                for i in range(2)
            ],
            axis=0,
        )

    mask = jnp.concatenate([in_grid(row0 - 8, 8, col0), in_grid(row0 + 64, 8, col0)], axis=0)
    courant = jnp.where(mask, extended(16, False, 4, 0), 0.0)
    inside = jnp.where(mask, 1.0, 0.0)

    def work(j, special, group, offset):
        g_re, g_im = extended(j, False, group, offset), extended(j, True, group, offset + 8)
        for i, value in enumerate(coefficients(lam, j, special, g_re, g_im, courant, inside)):
            full[j, i, 0:8, :] = value[:8]
            full[j, i, 72:80, :] = value[8:]

    over_frequencies(work)

    def keep(p, slot, field):
        for v in range(10):
            wide[slot, pl.ds(v, 8, stride=10), :] = field[v]
        solved[p] = jnp.where(low, wide[slot, 8:40, :], half_turn(wide[slot, 40:72, :]))

    def swept(special, start_re, start_im, gain_re, gain_im, re, im):
        all_re = around(re, sides_by_rotation(re))
        all_im = around(im, sides_by_matrix(im, matrix))
        if special:
            return (
                [start_re[v] + gain_re[v] * all_re[v] for v in range(10)],
                [start_im[v] + gain_im[v] * all_im[v] for v in range(10)],
            )
        return (
            [start_re[v] + (gain_re[v] * all_re[v] - gain_im[v] * all_im[v]) for v in range(10)],
            [start_im[v] + (gain_re[v] * all_im[v] + gain_im[v] * all_re[v]) for v in range(10)],
        )

    def batch(k, has_special):
        sets, fields = [], []
        for i in range(BATCH):
            j = k * BATCH + i
            parts = [[full[j, a, pl.ds(v, 8, stride=10), :] for v in range(10)] for a in range(4)]
            sets.append((has_special and i == 0, *parts))
            fields.append((parts[0], parts[1]))
        for _ in range(SWEEPS - 1):
            fields = [swept(*sets[i], *fields[i]) for i in range(BATCH)]
        for i in range(BATCH):
            j = k * BATCH + i
            keep(2 * j, 2 * i, fields[i][0])
            keep(2 * j + 1, 2 * i + 1, fields[i][1])

    def later(k, carry):
        batch(k, False)
        return carry

    batch(0, True)
    lax.fori_loop(1, 16 // BATCH, later, 0)

    for r in range(4):
        part = slice(8 * r, 8 * r + 8)
        steps = backward([solved[p, part, :] for p in range(32)])
        for n in range(32):
            value = steps[n] * np.float32(math.exp(-n * DECAY) / STEPS)
            t, k = n // 4, n % 4
            out[t, 32 * k + 32 + 8 * r : 32 * k + 40 + 8 * r, :] = value
            if k == 3:
                out[(t + 1) % 8, part, :] = value * np.float32(ALPHA) if n == 31 else value


def solve(lam, middle, from_core, from_cross):
    return pl.pallas_call(
        solve_kernel,
        in_specs=[pl.BlockSpec(memory_space=pltpu.SMEM)] + [pl.BlockSpec(memory_space=pltpu.VMEM)] * 3,
        out_specs=[pl.BlockSpec(memory_space=pltpu.VMEM)] * 2,
        out_shape=[
            jax.ShapeDtypeStruct((8, 160, 128), jnp.float32),
            jax.ShapeDtypeStruct((16, 4, 80, 128), jnp.float32),
        ],
        input_output_aliases={1: 1},
        scratch_shapes=[
            pltpu.VMEM((32, 32, 128), jnp.float32),
            pltpu.VMEM((2 * BATCH, 80, 128), jnp.float32),
        ],
        compiler_params=params(),
        name="solve",
    )(lam, middle, from_core, from_cross)[0]


def finish_kernel(other, units, forcing, initial, last, *refs):
    out, held, sent = refs[-3:]
    tm, odd_x, odd_y, core = place()[:4]
    low = lanes(32) < 64
    first = jnp.where(tm == 0, 1.0, 0.0).astype(jnp.float32)
    begin = 0 if other else pl.multiple_of(64 * core, 64)
    core = core ^ other
    copies = []
    for upper in range(2):
        for half in range(2):
            cols = slice(128 * half, 128 * half + 128)
            ones, twos = (
                [units[chip, pl.ds(begin + 32 * k, 32), :] for k in range(3)]
                for chip in (chip_of(half, upper, inner, odd_x, odd_y) for inner in range(2))
            )
            for part in range(2):
                rows = slice(32 * part, 32 * part + 32)
                if part == 0:
                    values = [jnp.where(low, one, half_turn(two)) for one, two in zip(ones, twos)]
                else:
                    values = [jnp.where(low, half_turn(one), two) for one, two in zip(ones, twos)]
                before, now, after = values
                start = forcing[0, 0, upper, core, rows, cols] + first * (
                    initial[0, upper, core, rows, cols] - ALPHA * last[0, upper, core, rows, cols]
                )
                held[upper, 0, 0, rows, cols] = now
                held[upper, 0, 1, rows, cols] = after
                held[upper, 1, 0, rows, cols] = now - before - start
                held[upper, 1, 1, rows, cols] = after - now - forcing[0, 1, upper, core, rows, cols]
        copies.append(pltpu.make_async_copy(held.at[upper], out.at[:, :, upper, core], sent.at[upper]))
        copies[upper].start()
    for upper in range(2):
        copies[upper].wait()


def finish(units, forcing, initial, last, result=None):
    other = result is not None
    return pl.pallas_call(
        functools.partial(finish_kernel, int(other)),
        in_specs=[pl.BlockSpec(memory_space=pltpu.VMEM)] * 4
        + [pl.BlockSpec(memory_space=pltpu.HBM)] * other,
        out_specs=pl.BlockSpec(memory_space=pltpu.HBM),
        out_shape=jax.ShapeDtypeStruct((2, 2, 2, 2, 64, 256), jnp.float32),
        scratch_shapes=[pltpu.VMEM((2, 2, 2, 64, 256), jnp.float32), pltpu.SemaphoreType.DMA((2,))],
        input_output_aliases={4: 0} if other else {},
        compiler_params=params(),
        cost_estimate=cost(2**20),
        name="finish_other" if other else "finish_own",
    )(
        units,
        forcing.reshape(2, 2, 2, 2, 64, 256),
        initial.reshape(2, 2, 2, 64, 256),
        last.reshape(2, 2, 2, 64, 256),
        *([result] if other else []),
    )


def lam_squares():
    rows = []
    for j in range(16):
        lam = 1.0 - FACTOR * complex(math.cos(angle(j)), -math.sin(angle(j)))
        square = lam * lam
        rows.append((square.real, square.imag))
    rows[0] = ((1.0 - FACTOR) ** 2, (1.0 + FACTOR) ** 2)
    return np.array(rows, np.float32)


def chips_exchange(pieces):
    return lax.all_to_all(pieces, "tm", 0, 0, axis_index_groups=CHIPS, tiled=True)


def per_device(forcing, initial, previous_last, cell_class, courant_table):
    core = lax.axis_index("tm") & 1
    lam = jnp.asarray(lam_squares())
    theirs = lax.ppermute(prepare(forcing, 1), "tm", CORES)
    received = chips_exchange(merge(prepare(forcing, 0), theirs))
    fields = (courant_table, cell_class, initial, previous_last, received)
    planes, side = transform(*fields)
    from_side = lax.ppermute(side, AXES, TO_SIDE)
    beside, to_core, to_cross = strips(*fields, planes)

    def strip(main, start):
        return jnp.concatenate([main, lax.dynamic_slice_in_dim(from_side, start, 8, axis=1)], axis=0)

    from_cross = lax.ppermute(strip(to_cross, 24 * core), AXES, TO_CROSS)
    from_core = lax.ppermute(strip(to_core, 24 * (1 - core)), AXES, TO_CORE)
    middle = widen(lam, planes, beside, from_side)
    returned = chips_exchange(solve(lam, middle, from_core, from_cross))
    wanted = lax.dynamic_slice_in_dim(returned, 64 * (1 - core), 96, axis=1)
    other = lax.ppermute(wanted, "tm", CORES)
    result = finish(returned, forcing, initial, previous_last)
    result = finish(other, forcing, initial, previous_last, result)
    return result.reshape(2, 2, 256, 256)


def solution(mesh):
    in_specs = (
        P(None, "tm", "sx", "sy"),
        P(None, "sx", "sy"),
        P(None, "sx", "sy"),
        P("sx", "sy"),
        P(),
    )
    out_specs = P(None, "tm", "sx", "sy")
    return jax.shard_map(
        per_device, mesh=mesh, in_specs=in_specs, out_specs=out_specs, check_vma=False
    )
```

```python
import functools
import math

import jax
import jax.numpy as jnp
import numpy as np
from jax import lax
from jax.experimental import pallas as pl
from jax.experimental.pallas import tpu as pltpu
from jax.sharding import PartitionSpec as P

STEPS = 32
SWEEPS = 8
BATCH = 8
ALPHA = 0.1
DECAY = math.log(ALPHA) / STEPS
FACTOR = math.exp(DECAY)
AXES = ("tm", "sx", "sy")
VMEM = 16 * 2**20


def chip_of(half, upper, inner, odd_x, odd_y):
    half_y, upper_y = half ^ odd_y, upper ^ odd_x
    return (2 * half_y + (upper_y ^ half_y)) * 2 + (inner ^ half)


def device_of(row, col):
    row, col = row % 16, col % 16
    sx, upper, core = row // 4, row // 2 % 2, row % 2
    sy, half, inner = col // 4, col // 2 % 2, col % 2
    tm = chip_of(half, upper, inner, sx & 1, sy & 1) * 2 + core
    return (tm * 4 + sx) * 4 + sy


def pairs_of(move):
    return [
        (device_of(row, col), device_of(*move(row, col))) for row in range(16) for col in range(16)
    ]


def away(index):
    return index - 1 if index % 2 == 0 else index + 1


def side_of(row, col):
    return (row, away(col)) if 0 < col < 15 else (row ^ 1, col)


TO_SIDE = pairs_of(side_of)
TO_CORE = pairs_of(lambda row, col: (row ^ 1, col))
TO_CROSS = pairs_of(lambda row, col: (away(row), col))
CHIPS = [[chip * 2 + core for chip in range(8)] for core in range(2)]
CORES = [(tm, tm ^ 1) for tm in range(16)]


def lanes(rows):
    return lax.broadcasted_iota(jnp.int32, (rows, 128), 1)


def half_turn(value):
    return pltpu.roll(value, 64, 1)


def pack_left(value, low):
    return jnp.where(low, value[:32], half_turn(value[32:]))


def pack_right(value, low):
    return jnp.where(low, half_turn(value[:32]), value[32:])


def place():
    tm, sx, sy = (lax.axis_index(axis) for axis in AXES)
    odd_x, odd_y = sx & 1, sy & 1
    y, z, core = tm >> 2, tm >> 1 & 1, tm & 1
    half_y = y >> 1
    upper_y = (y & 1) ^ half_y
    half, upper = half_y ^ odd_y, upper_y ^ odd_x
    inner = z ^ half
    row0 = sx * 256 + upper * 128 + core * 64
    col0 = sy * 256 + half * 128 + inner * 64
    return tm, odd_x, odd_y, core, upper, half, inner, row0, col0


def params():
    return pltpu.CompilerParams(vmem_limit_bytes=VMEM)


def cost(size):
    return pl.CostEstimate(flops=size, bytes_accessed=size, transcendentals=0)


def turn(value, shift):
    if isinstance(shift, int):
        return pltpu.roll(value, shift % 128, 1) if shift % 128 else value
    return pltpu.roll(value, lax.rem(shift + 256, 128), 1)


def prepare_kernel(forcing, out):
    tm, odd_x, odd_y = place()[:3]
    low = lanes(32) < 64
    weight = jnp.float32(1.0)
    for bit in range(4):
        step = math.exp(DECAY * 2 ** (bit + 1))
        weight = weight * jnp.where((tm >> bit & 1) == 1, step, 1.0).astype(jnp.float32)
    weight_two = weight * np.float32(FACTOR)
    weight_three = weight * np.float32(-FACTOR * FACTOR)
    for upper in range(2):
        for half in range(2):
            cols = slice(128 * half, 128 * half + 128)
            first_u, second_u = forcing[0, 0, upper, :, cols], forcing[0, 1, upper, :, cols]
            first_w, second_w = forcing[1, 0, upper, :, cols], forcing[1, 1, upper, :, cols]
            units = (
                weight * (first_w + first_u),
                weight_two * (second_w + second_u - first_u),
                weight_three * second_u,
            )
            left = chip_of(half, upper, 0, odd_x, odd_y)
            right = chip_of(half, upper, 1, odd_x, odd_y)
            for k, unit in enumerate(units):
                rows = slice(32 * k, 32 * k + 32)
                out[left, rows, :] = pack_left(unit, low)
                out[right, rows, :] = pack_right(unit, low)


def prepare(forcing, core, name):
    rows = lax.dynamic_index_in_dim(forcing.reshape(2, 2, 2, 2, 64, 256), core, 3, keepdims=False)
    return pl.pallas_call(
        prepare_kernel,
        in_specs=[pl.BlockSpec(memory_space=pltpu.VMEM)],
        out_specs=pl.BlockSpec(memory_space=pltpu.VMEM),
        out_shape=jax.ShapeDtypeStruct((8, 96, 128), jnp.float32),
        compiler_params=params(),
        cost_estimate=cost(2**20),
        name=name,
    )(rows)


def merge_kernel(mine, received, out):
    _, odd_x, odd_y, core = place()[:4]
    is_first = core == 0
    lane8 = lanes(8) % 64
    for chip in range(8):
        for k in range(3):
            rows = slice(32 * k, 32 * k + 32)
            own, other = mine[chip, rows, :], received[chip, rows, :]
            early, late = jnp.where(is_first, own, other), jnp.where(is_first, other, own)
            if k < 2:
                out[chip, 32 * k : 32 * k + 32, :] = early
                kept = late if k == 0 else kept
                if k == 1:
                    out[chip, 96:128, :] = late
            else:
                out[chip, 64:96, :] = kept + early
                out[chip, 128:160, :] = late
    for chip in range(8):
        inner = (chip & 1) ^ (chip >> 2) ^ odd_y
        for tile in range(3):
            value = jnp.zeros((8, 128), jnp.float32)
            for m in range(8):
                k, r = (8 * tile + m) // 4, m % 4
                if k == 5:
                    break
                beside = out[chip ^ 1, 32 * k + 8 * r : 32 * k + 8 * r + 8, :]
                here = (lane8 >= 8 * m) & (lane8 < 8 * m + 8)
                value = jnp.where(here, turn(beside, 8 * m - 56 * inner), value)
            out[chip, 160 + 8 * tile : 168 + 8 * tile, :] = value


def merge(mine, received):
    return pl.pallas_call(
        merge_kernel,
        in_specs=[pl.BlockSpec(memory_space=pltpu.VMEM)] * 2,
        out_specs=pl.BlockSpec(memory_space=pltpu.VMEM),
        out_shape=jax.ShapeDtypeStruct((8, 184, 128), jnp.float32),
        compiler_params=params(),
        name="merge",
    )(mine, received)


def scaled(factor, value):
    if abs(factor) < 1e-12:
        return None
    if abs(factor - 1.0) < 1e-12:
        return value
    if abs(factor + 1.0) < 1e-12:
        return -value
    return np.float32(factor) * value


def total_of(terms):
    terms = [term for term in terms if term is not None]
    result = terms[0]
    for term in terms[1:]:
        result = result + term
    return result


def angle(index):
    return 2.0 * math.pi * (index % STEPS) / STEPS


def forward(steps):
    even = [steps[0]] + [steps[n] + steps[32 - n] for n in range(1, 16)] + [steps[16]]
    odd = [None] + [steps[n] - steps[32 - n] for n in range(1, 16)]
    planes = [None] * 32
    for j in range(9):
        cos_even = total_of([scaled(math.cos(angle(j * n)), even[n]) for n in range(0, 17, 2)])
        cos_odd = (
            None if j == 8 else total_of([scaled(math.cos(angle(j * n)), even[n]) for n in range(1, 17, 2)])
        )
        high, lowp = (
            (cos_even, None) if cos_odd is None else (cos_even + cos_odd, cos_even - cos_odd)
        )
        if j == 0:
            planes[0], planes[1] = high, lowp
            continue
        planes[2 * j] = high
        if j < 8:
            planes[2 * (16 - j)] = lowp
        sin_odd = total_of([scaled(math.sin(angle(j * n)), odd[n]) for n in range(1, 16, 2)])
        if j == 8:
            planes[2 * j + 1] = -sin_odd
            continue
        sin_even = total_of([scaled(math.sin(angle(j * n)), odd[n]) for n in range(2, 16, 2)])
        planes[2 * j + 1] = -(sin_even + sin_odd)
        planes[2 * (16 - j) + 1] = sin_even - sin_odd
    return planes


def backward(planes):
    real = [planes[0]] + [planes[2 * j] * 2.0 for j in range(1, 16)] + [planes[1]]
    imag = [None] + [planes[2 * j + 1] * 2.0 for j in range(1, 16)]
    steps = [None] * 32

    def put(n, cosine, sine):
        if n in (0, 16):
            steps[n] = cosine
            return
        steps[n] = cosine - sine
        steps[32 - n] = cosine + sine

    for n in range(9):
        cos_even = total_of([scaled(math.cos(angle(j * n)), real[j]) for j in range(0, 17, 2)])
        if n == 8:
            sine = total_of([scaled(math.sin(angle(j * n)), imag[j]) for j in range(1, 16, 2)])
            put(8, cos_even, sine)
            continue
        cos_odd = total_of([scaled(math.cos(angle(j * n)), real[j]) for j in range(1, 17, 2)])
        if n == 0:
            put(0, cos_even + cos_odd, None)
            put(16, cos_even - cos_odd, None)
            continue
        sin_odd = total_of([scaled(math.sin(angle(j * n)), imag[j]) for j in range(1, 16, 2)])
        sin_even = total_of([scaled(math.sin(angle(j * n)), imag[j]) for j in range(2, 16, 2)])
        put(n, cos_even + cos_odd, sin_even + sin_odd)
        put(16 - n, cos_even - cos_odd, sin_odd - sin_even)
    return steps


def slots(m):
    lane = lanes(8) % 64
    return (lane >= 8 * m) & (lane < 8 * m + 8)


def in_slots(planes, start):
    groups = []
    for g in range(5):
        value = jnp.zeros((8, 128), jnp.float32)
        for m, plane in enumerate(planes[8 * g : 8 * g + 8]):
            value = jnp.where(slots(m), turn(plane, 8 * m - start), value)
        groups.append(value)
    return groups


def block_of(value, inner):
    return pack_left(jnp.where(inner == 1, half_turn(value), value), lanes(32) < 64)


def beside_of(value, inner):
    other = block_of(value, 1 - inner)
    beside = jnp.zeros((8, 128), jnp.float32)
    for r in range(4):
        beside = jnp.where(slots(r), turn(other[8 * r : 8 * r + 8], 8 * r - 56 * inner), beside)
    return beside


def pair_fields(table, cell_class, initial, last):
    core, upper, half = place()[3:6]
    rows = pl.ds(pl.multiple_of((upper * 2 + core) * 64, 64), 64)
    cols = pl.ds(pl.multiple_of(half * 128, 128), 128)
    classes = cell_class[rows, cols]
    courant = jnp.zeros(classes.shape, jnp.float32)
    for k in range(8):
        courant = jnp.where(classes == k, table[k], courant)
    return [courant] + [initial[c, rows, cols] - ALPHA * last[c, rows, cols] for c in range(2)]


def with_start(steps, start_u, start_w):
    return [steps[0] + (start_w + start_u), steps[1] - np.float32(FACTOR) * start_u] + steps[2:]


def transform_kernel(table, cell_class, initial, last, received, planes_out, side_out):
    inner = place()[6]
    courant, start_u, start_w = (
        block_of(value, inner) for value in pair_fields(table, cell_class, initial, last)
    )
    for r in range(4):
        rows = slice(8 * r, 8 * r + 8)
        steps = []
        for t in range(8):
            part = [received[t, 32 * k + 8 * r : 32 * k + 8 * r + 8, :] for k in range(4)]
            part[0] = part[0] + received[(t + 7) % 8, 128 + 8 * r : 136 + 8 * r, :]
            steps.extend(part)
        planes = forward(with_start(steps, start_u[rows], start_w[rows])) + [courant[rows]]
        for p in range(33):
            planes_out[p, rows, :] = planes[p]
        for g, value in enumerate(in_slots(planes, 56 * inner)):
            side_out[g, rows, :] = value


def transform(table, cell_class, initial, last, received):
    shapes = ((33, 32, 128), (5, 32, 128))
    return pl.pallas_call(
        transform_kernel,
        in_specs=[pl.BlockSpec(memory_space=pltpu.SMEM)] + [pl.BlockSpec(memory_space=pltpu.VMEM)] * 4,
        out_specs=[pl.BlockSpec(memory_space=pltpu.VMEM)] * 2,
        out_shape=[jax.ShapeDtypeStruct(shape, jnp.float32) for shape in shapes],
        compiler_params=params(),
        name="transform",
    )(table, cell_class, initial, last, received)


def strips_kernel(
    table, cell_class, initial, last, received, planes, beside_out, core_out, cross_out
):
    core, _, _, inner = place()[3:7]
    low = lanes(8) < 64
    courant, start_u, start_w = (
        beside_of(value, inner) for value in pair_fields(table, cell_class, initial, last)
    )
    steps = []
    for t in range(8):
        one, two = received[t, 160:168, :], received[t, 168:176, :]
        first = one + received[(t + 7) % 8, 176:184, :]
        steps.extend([first, turn(one, -32), two, turn(two, -32)])
    beside = forward(with_start(steps, start_u, start_w)) + [courant]
    for p in range(33):
        beside_out[p] = beside[p]
    top, bottom = [], []
    for j in range(17):
        one, two = 2 * j, min(2 * j + 1, 32)
        top.append(jnp.where(low, planes[one, 0:8, :], half_turn(planes[two, 0:8, :])))
        bottom.append(jnp.where(low, half_turn(planes[one, 24:32, :]), planes[two, 24:32, :]))
    top.extend(in_slots(beside, 0))
    bottom.extend(in_slots(beside, 88))
    for i in range(22):
        core_out[i] = jnp.where(core == 0, bottom[i], top[i])
        cross_out[i] = jnp.where(core == 0, top[i], bottom[i])


def strips(table, cell_class, initial, last, received, planes):
    shapes = ((33, 8, 128), (22, 8, 128), (22, 8, 128))
    return pl.pallas_call(
        strips_kernel,
        in_specs=[pl.BlockSpec(memory_space=pltpu.SMEM)] + [pl.BlockSpec(memory_space=pltpu.VMEM)] * 5,
        out_specs=[pl.BlockSpec(memory_space=pltpu.VMEM)] * 3,
        out_shape=[jax.ShapeDtypeStruct(shape, jnp.float32) for shape in shapes],
        compiler_params=params(),
        cost_estimate=cost(2**20),
        name="strips",
    )(table, cell_class, initial, last, received, planes)


def side_matrix():
    rows = lax.broadcasted_iota(jnp.int32, (256, 128), 0) % 128
    gap = (rows - lax.broadcasted_iota(jnp.int32, (256, 128), 1)) % 128
    return jnp.where((gap == 1) | (gap == 127), 1.0, 0.0).astype(jnp.bfloat16)


def sides_by_matrix(field, matrix):
    value = jnp.concatenate(field, axis=0)
    high = value.astype(jnp.bfloat16)
    low = (value - high.astype(jnp.float32)).astype(jnp.bfloat16)
    result = jnp.dot(jnp.concatenate([high, low], axis=1), matrix, preferred_element_type=jnp.float32)
    return [result[8 * v : 8 * v + 8] for v in range(10)]


def sides_by_rotation(field):
    return [pltpu.roll(own, 1, 1) + pltpu.roll(own, 127, 1) for own in field]


def around(field, sides):
    first = pltpu.roll(field[9], 1, 0)
    last = pltpu.roll(field[0], 7, 0)
    above = [first] + field[:9]
    below = field[1:] + [last]
    return [(up + down) + side for up, side, down in zip(above, sides, below)]


def bases(inner):
    return 120 - 56 * inner, 64 + 56 * inner


def merged(centre, side, other, bases):
    lane = lanes(8)
    value = jnp.where(lane < 64, centre, 0.0)
    for base, edge in zip(bases, (side, other)):
        value = jnp.where((lane >= base) & (lane < base + 8), edge, value)
    return value


def in_grid(first_row, count, col0):
    rows = lax.broadcasted_iota(jnp.int32, (count, 128), 0) + first_row
    lane = lanes(count)
    cols = jnp.where(lane >= 120, lane - 128, lane) + col0
    used = (lane < 72) | (lane >= 120)
    return used & (rows >= 0) & (rows < 1024) & (cols >= 0) & (cols < 1024)


def coefficients(lam, j, special, g_re, g_im, courant, inside):
    if special:
        inv_re = inside / (lam[0, 0] + 4.0 * courant)
        inv_im = inside / (lam[0, 1] + 4.0 * courant)
        return g_re * inv_re, g_im * inv_im, courant * inv_re, courant * inv_im
    diag_re = lam[j, 0] + 4.0 * courant
    diag_im = lam[j, 1]
    scale = inside / (diag_re * diag_re + diag_im * diag_im)
    inv_re = diag_re * scale
    inv_im = -diag_im * scale
    return (
        g_re * inv_re - g_im * inv_im,
        g_re * inv_im + g_im * inv_re,
        courant * inv_re,
        courant * inv_im,
    )


def over_frequencies(work):
    for j in range(4):
        work(j, j == 0, 0, 16 * j)

    def group(k, carry):
        for i in range(4):
            work(4 * k + i, False, k, 16 * i)
        return carry

    lax.fori_loop(1, 4, group, 0)


def widen_kernel(lam, planes, beside, from_side, out):
    inner, _, col0 = place()[6:]
    both = bases(inner)

    def extended(p, group, offset):
        edge = beside[p]
        parts = []
        for r in range(8):
            part = slice(8 * (r % 4), 8 * (r % 4) + 8)
            shift = 0 if r < 4 else 64
            parts.append(
                merged(
                    turn(planes[p, part, :], shift),
                    turn(from_side[group, part, :], both[0] - shift - offset),
                    turn(edge, both[1] - shift - 8 * (r % 4)),
                    both,
                )
            )
        return jnp.concatenate(parts, axis=0)

    mask = in_grid(0, 64, col0)
    courant = jnp.where(mask, extended(32, 4, 0), 0.0)
    inside = jnp.where(mask, 1.0, 0.0)

    def work(j, special, group, offset):
        g_re, g_im = extended(2 * j, group, offset), extended(2 * j + 1, group, offset + 8)
        for i, value in enumerate(coefficients(lam, j, special, g_re, g_im, courant, inside)):
            out[j, i, 8:72, :] = value

    over_frequencies(work)


def widen(lam, planes, beside, from_side):
    return pl.pallas_call(
        widen_kernel,
        in_specs=[pl.BlockSpec(memory_space=pltpu.SMEM)] + [pl.BlockSpec(memory_space=pltpu.VMEM)] * 3,
        out_specs=pl.BlockSpec(memory_space=pltpu.VMEM),
        out_shape=jax.ShapeDtypeStruct((16, 4, 80, 128), jnp.float32),
        compiler_params=params(),
        cost_estimate=cost(2**21),
        name="widen",
    )(lam, planes, beside, from_side)


def solve_kernel(lam, middle, from_core, from_cross, out, full, solved, wide):
    core, _, _, inner, row0, col0 = place()[3:]
    both = bases(inner)
    low = lanes(32) < 64
    matrix = side_matrix()

    def halo(index):
        one, two = from_core[index], from_cross[index]
        return jnp.where(core == 1, one, two), jnp.where(core == 1, two, one)

    def extended(pair, odd, group, offset):
        centre, edge, side = halo(pair), halo(17 + group), halo(22 + group)
        return jnp.concatenate(
            [
                merged(
                    half_turn(centre[i]) if odd else centre[i],
                    turn(side[i], both[0] - offset - (0 if i else 64)),
                    turn(edge[i], both[1] - offset),
                    both,
                )
                for i in range(2)
            ],
            axis=0,
        )

    mask = jnp.concatenate([in_grid(row0 - 8, 8, col0), in_grid(row0 + 64, 8, col0)], axis=0)
    courant = jnp.where(mask, extended(16, False, 4, 0), 0.0)
    inside = jnp.where(mask, 1.0, 0.0)

    def work(j, special, group, offset):
        g_re, g_im = extended(j, False, group, offset), extended(j, True, group, offset + 8)
        for i, value in enumerate(coefficients(lam, j, special, g_re, g_im, courant, inside)):
            full[j, i, 0:8, :] = value[:8]
            full[j, i, 72:80, :] = value[8:]

    over_frequencies(work)

    def keep(p, slot, field):
        for v in range(10):
            wide[slot, pl.ds(v, 8, stride=10), :] = field[v]
        solved[p] = jnp.where(low, wide[slot, 8:40, :], half_turn(wide[slot, 40:72, :]))

    def swept(special, start_re, start_im, gain_re, gain_im, re, im):
        all_re = around(re, sides_by_rotation(re))
        all_im = around(im, sides_by_matrix(im, matrix))
        if special:
            return (
                [start_re[v] + gain_re[v] * all_re[v] for v in range(10)],
                [start_im[v] + gain_im[v] * all_im[v] for v in range(10)],
            )
        return (
            [start_re[v] + (gain_re[v] * all_re[v] - gain_im[v] * all_im[v]) for v in range(10)],
            [start_im[v] + (gain_re[v] * all_im[v] + gain_im[v] * all_re[v]) for v in range(10)],
        )

    def batch(k, has_special):
        sets, fields = [], []
        for i in range(BATCH):
            j = k * BATCH + i
            parts = [[full[j, a, pl.ds(v, 8, stride=10), :] for v in range(10)] for a in range(4)]
            sets.append((has_special and i == 0, *parts))
            fields.append((parts[0], parts[1]))
        for _ in range(SWEEPS - 1):
            fields = [swept(*sets[i], *fields[i]) for i in range(BATCH)]
        for i in range(BATCH):
            j = k * BATCH + i
            keep(2 * j, 2 * i, fields[i][0])
            keep(2 * j + 1, 2 * i + 1, fields[i][1])

    def later(k, carry):
        batch(k, False)
        return carry

    batch(0, True)
    lax.fori_loop(1, 16 // BATCH, later, 0)

    for r in range(4):
        part = slice(8 * r, 8 * r + 8)
        steps = backward([solved[p, part, :] for p in range(32)])
        for n in range(32):
            value = steps[n] * np.float32(math.exp(-n * DECAY) / STEPS)
            t, k = n // 4, n % 4
            out[t, 32 * k + 32 + 8 * r : 32 * k + 40 + 8 * r, :] = value
            if k == 3:
                out[(t + 1) % 8, part, :] = value * np.float32(ALPHA) if n == 31 else value


def solve(lam, middle, from_core, from_cross):
    return pl.pallas_call(
        solve_kernel,
        in_specs=[pl.BlockSpec(memory_space=pltpu.SMEM)] + [pl.BlockSpec(memory_space=pltpu.VMEM)] * 3,
        out_specs=[pl.BlockSpec(memory_space=pltpu.VMEM)] * 2,
        out_shape=[
            jax.ShapeDtypeStruct((8, 160, 128), jnp.float32),
            jax.ShapeDtypeStruct((16, 4, 80, 128), jnp.float32),
        ],
        input_output_aliases={1: 1},
        scratch_shapes=[
            pltpu.VMEM((32, 32, 128), jnp.float32),
            pltpu.VMEM((2 * BATCH, 80, 128), jnp.float32),
        ],
        compiler_params=params(),
        name="solve",
    )(lam, middle, from_core, from_cross)[0]


def finish_kernel(other, units, forcing, initial, last, *refs):
    out, held, sent = refs[-3:]
    tm, odd_x, odd_y, core = place()[:4]
    low = lanes(32) < 64
    first = jnp.where(tm == 0, 1.0, 0.0).astype(jnp.float32)
    begin = 0 if other else pl.multiple_of(64 * core, 64)
    core = core ^ other
    copies = []
    for upper in range(2):
        for half in range(2):
            cols = slice(128 * half, 128 * half + 128)
            ones, twos = (
                [units[chip, pl.ds(begin + 32 * k, 32), :] for k in range(3)]
                for chip in (chip_of(half, upper, inner, odd_x, odd_y) for inner in range(2))
            )
            for part in range(2):
                rows = slice(32 * part, 32 * part + 32)
                if part == 0:
                    values = [jnp.where(low, one, half_turn(two)) for one, two in zip(ones, twos)]
                else:
                    values = [jnp.where(low, half_turn(one), two) for one, two in zip(ones, twos)]
                before, now, after = values
                start = forcing[0, 0, upper, core, rows, cols] + first * (
                    initial[0, upper, core, rows, cols] - ALPHA * last[0, upper, core, rows, cols]
                )
                held[upper, 0, 0, rows, cols] = now
                held[upper, 0, 1, rows, cols] = after
                held[upper, 1, 0, rows, cols] = now - before - start
                held[upper, 1, 1, rows, cols] = after - now - forcing[0, 1, upper, core, rows, cols]
        copies.append(pltpu.make_async_copy(held.at[upper], out.at[:, :, upper, core], sent.at[upper]))
        copies[upper].start()
    for upper in range(2):
        copies[upper].wait()


def finish(units, forcing, initial, last, result=None):
    other = result is not None
    return pl.pallas_call(
        functools.partial(finish_kernel, int(other)),
        in_specs=[pl.BlockSpec(memory_space=pltpu.VMEM)] * 4
        + [pl.BlockSpec(memory_space=pltpu.HBM)] * other,
        out_specs=pl.BlockSpec(memory_space=pltpu.HBM),
        out_shape=jax.ShapeDtypeStruct((2, 2, 2, 2, 64, 256), jnp.float32),
        scratch_shapes=[pltpu.VMEM((2, 2, 2, 64, 256), jnp.float32), pltpu.SemaphoreType.DMA((2,))],
        input_output_aliases={4: 0} if other else {},
        compiler_params=params(),
        cost_estimate=cost(2**20),
        name="finish_other" if other else "finish_own",
    )(
        units,
        forcing.reshape(2, 2, 2, 2, 64, 256),
        initial.reshape(2, 2, 2, 64, 256),
        last.reshape(2, 2, 2, 64, 256),
        *([result] if other else []),
    )


def lam_squares():
    rows = []
    for j in range(16):
        lam = 1.0 - FACTOR * complex(math.cos(angle(j)), -math.sin(angle(j)))
        square = lam * lam
        rows.append((square.real, square.imag))
    rows[0] = ((1.0 - FACTOR) ** 2, (1.0 + FACTOR) ** 2)
    return np.array(rows, np.float32)


def chips_exchange(pieces):
    return lax.all_to_all(pieces, "tm", 0, 0, axis_index_groups=CHIPS, tiled=True)


def per_device(forcing, initial, previous_last, cell_class, courant_table):
    core = lax.axis_index("tm") & 1
    lam = jnp.asarray(lam_squares())
    theirs = prepare(forcing, 1 - core, "prepare_other")
    theirs, rest = lax.optimization_barrier((theirs, forcing))
    theirs = lax.ppermute(theirs, "tm", CORES)
    received = chips_exchange(merge(prepare(rest, core, "prepare_own"), theirs))
    fields = (courant_table, cell_class, initial, previous_last, received)
    planes, side = transform(*fields)
    from_side = lax.ppermute(side, AXES, TO_SIDE)
    beside, to_core, to_cross = strips(*fields, planes)

    def strip(main, start):
        return jnp.concatenate([main, lax.dynamic_slice_in_dim(from_side, start, 8, axis=1)], axis=0)

    from_cross = lax.ppermute(strip(to_cross, 24 * core), AXES, TO_CROSS)
    from_core = lax.ppermute(strip(to_core, 24 * (1 - core)), AXES, TO_CORE)
    middle = widen(lam, planes, beside, from_side)
    solved, is_first = lax.optimization_barrier((solve(lam, middle, from_core, from_cross), core == 0))
    returned = chips_exchange(solved)
    wanted = jnp.where(is_first, returned[:, 64:160], returned[:, 0:96])
    other = lax.ppermute(wanted, "tm", CORES)
    result = finish(returned, forcing, initial, previous_last)
    result = finish(other, forcing, initial, previous_last, result)
    return result.reshape(2, 2, 256, 256)


def solution(mesh):
    in_specs = (
        P(None, "tm", "sx", "sy"),
        P(None, "sx", "sy"),
        P(None, "sx", "sy"),
        P("sx", "sy"),
        P(),
    )
    out_specs = P(None, "tm", "sx", "sy")
    return jax.shard_map(
        per_device, mesh=mesh, in_specs=in_specs, out_specs=out_specs, check_vma=False
    )
```

```python
import functools
import math

import jax
import jax.numpy as jnp
import numpy as np
from jax import lax
from jax.experimental import pallas as pl
from jax.experimental.pallas import tpu as pltpu
from jax.sharding import PartitionSpec as P

STEPS = 32
SWEEPS = 8
BATCH = 8
ALPHA = 0.1
DECAY = math.log(ALPHA) / STEPS
FACTOR = math.exp(DECAY)
AXES = ("tm", "sx", "sy")
VMEM = 16 * 2**20


def chip_of(half, upper, inner, odd_x, odd_y):
    half_y, upper_y = half ^ odd_y, upper ^ odd_x
    return (2 * half_y + (upper_y ^ half_y)) * 2 + (inner ^ half)


def device_of(row, col):
    row, col = row % 16, col % 16
    sx, upper, core = row // 4, row // 2 % 2, row % 2
    sy, half, inner = col // 4, col // 2 % 2, col % 2
    tm = chip_of(half, upper, inner, sx & 1, sy & 1) * 2 + core
    return (tm * 4 + sx) * 4 + sy


def pairs_of(move):
    return [
        (device_of(row, col), device_of(*move(row, col))) for row in range(16) for col in range(16)
    ]


def away(index):
    return index - 1 if index % 2 == 0 else index + 1


def side_of(row, col):
    return (row, away(col)) if 0 < col < 15 else (row ^ 1, col)


TO_SIDE = pairs_of(side_of)
TO_CORE = pairs_of(lambda row, col: (row ^ 1, col))
TO_CROSS = pairs_of(lambda row, col: (away(row), col))
CHIPS = [[chip * 2 + core for chip in range(8)] for core in range(2)]
CORES = [(tm, tm ^ 1) for tm in range(16)]


def lanes(rows):
    return lax.broadcasted_iota(jnp.int32, (rows, 128), 1)


def half_turn(value):
    return pltpu.roll(value, 64, 1)


def pack_left(value, low):
    return jnp.where(low, value[:32], half_turn(value[32:]))


def pack_right(value, low):
    return jnp.where(low, half_turn(value[:32]), value[32:])


def place():
    tm, sx, sy = (lax.axis_index(axis) for axis in AXES)
    odd_x, odd_y = sx & 1, sy & 1
    y, z, core = tm >> 2, tm >> 1 & 1, tm & 1
    half_y = y >> 1
    upper_y = (y & 1) ^ half_y
    half, upper = half_y ^ odd_y, upper_y ^ odd_x
    inner = z ^ half
    row0 = sx * 256 + upper * 128 + core * 64
    col0 = sy * 256 + half * 128 + inner * 64
    return tm, odd_x, odd_y, core, upper, half, inner, row0, col0


def params():
    return pltpu.CompilerParams(vmem_limit_bytes=VMEM)


def cost(size):
    return pl.CostEstimate(flops=size, bytes_accessed=size, transcendentals=0)


def turn(value, shift):
    if isinstance(shift, int):
        return pltpu.roll(value, shift % 128, 1) if shift % 128 else value
    return pltpu.roll(value, lax.rem(shift + 256, 128), 1)


def prepare_kernel(forcing, out):
    tm, odd_x, odd_y = place()[:3]
    low = lanes(32) < 64
    weight = jnp.float32(1.0)
    for bit in range(4):
        step = math.exp(DECAY * 2 ** (bit + 1))
        weight = weight * jnp.where((tm >> bit & 1) == 1, step, 1.0).astype(jnp.float32)
    weight_two = weight * np.float32(FACTOR)
    weight_three = weight * np.float32(-FACTOR * FACTOR)
    for upper in range(2):
        for half in range(2):
            cols = slice(128 * half, 128 * half + 128)
            first_u, second_u = forcing[0, 0, upper, :, cols], forcing[0, 1, upper, :, cols]
            first_w, second_w = forcing[1, 0, upper, :, cols], forcing[1, 1, upper, :, cols]
            units = (
                weight * (first_w + first_u),
                weight_two * (second_w + second_u - first_u),
                weight_three * second_u,
            )
            left = chip_of(half, upper, 0, odd_x, odd_y)
            right = chip_of(half, upper, 1, odd_x, odd_y)
            for k, unit in enumerate(units):
                rows = slice(32 * k, 32 * k + 32)
                out[left, rows, :] = pack_left(unit, low)
                out[right, rows, :] = pack_right(unit, low)


def prepare(forcing, core, name):
    rows = lax.dynamic_index_in_dim(forcing.reshape(2, 2, 2, 2, 64, 256), core, 3, keepdims=False)
    return pl.pallas_call(
        prepare_kernel,
        in_specs=[pl.BlockSpec(memory_space=pltpu.VMEM)],
        out_specs=pl.BlockSpec(memory_space=pltpu.VMEM),
        out_shape=jax.ShapeDtypeStruct((8, 96, 128), jnp.float32),
        compiler_params=params(),
        cost_estimate=cost(2**20),
        name=name,
    )(rows)


def merge_kernel(mine, received, out):
    _, odd_x, odd_y, core = place()[:4]
    is_first = core == 0
    lane8 = lanes(8) % 64
    for chip in range(8):
        for k in range(3):
            rows = slice(32 * k, 32 * k + 32)
            own, other = mine[chip, rows, :], received[chip, rows, :]
            early, late = jnp.where(is_first, own, other), jnp.where(is_first, other, own)
            if k < 2:
                out[chip, 32 * k : 32 * k + 32, :] = early
                kept = late if k == 0 else kept
                if k == 1:
                    out[chip, 96:128, :] = late
            else:
                out[chip, 64:96, :] = kept + early
                out[chip, 128:160, :] = late
    for chip in range(8):
        inner = (chip & 1) ^ (chip >> 2) ^ odd_y
        for tile in range(3):
            value = jnp.zeros((8, 128), jnp.float32)
            for m in range(8):
                k, r = (8 * tile + m) // 4, m % 4
                if k == 5:
                    break
                beside = out[chip ^ 1, 32 * k + 8 * r : 32 * k + 8 * r + 8, :]
                here = (lane8 >= 8 * m) & (lane8 < 8 * m + 8)
                value = jnp.where(here, turn(beside, 8 * m - 56 * inner), value)
            out[chip, 160 + 8 * tile : 168 + 8 * tile, :] = value


def merge(mine, received):
    return pl.pallas_call(
        merge_kernel,
        in_specs=[pl.BlockSpec(memory_space=pltpu.VMEM)] * 2,
        out_specs=pl.BlockSpec(memory_space=pltpu.VMEM),
        out_shape=jax.ShapeDtypeStruct((8, 184, 128), jnp.float32),
        compiler_params=params(),
        name="merge",
    )(mine, received)


def scaled(factor, value):
    if abs(factor) < 1e-12:
        return None
    if abs(factor - 1.0) < 1e-12:
        return value
    if abs(factor + 1.0) < 1e-12:
        return -value
    return np.float32(factor) * value


def total_of(terms):
    terms = [term for term in terms if term is not None]
    result = terms[0]
    for term in terms[1:]:
        result = result + term
    return result


def angle(index):
    return 2.0 * math.pi * (index % STEPS) / STEPS


def forward(steps):
    even = [steps[0]] + [steps[n] + steps[32 - n] for n in range(1, 16)] + [steps[16]]
    odd = [None] + [steps[n] - steps[32 - n] for n in range(1, 16)]
    planes = [None] * 32
    for j in range(9):
        cos_even = total_of([scaled(math.cos(angle(j * n)), even[n]) for n in range(0, 17, 2)])
        cos_odd = (
            None if j == 8 else total_of([scaled(math.cos(angle(j * n)), even[n]) for n in range(1, 17, 2)])
        )
        high, lowp = (
            (cos_even, None) if cos_odd is None else (cos_even + cos_odd, cos_even - cos_odd)
        )
        if j == 0:
            planes[0], planes[1] = high, lowp
            continue
        planes[2 * j] = high
        if j < 8:
            planes[2 * (16 - j)] = lowp
        sin_odd = total_of([scaled(math.sin(angle(j * n)), odd[n]) for n in range(1, 16, 2)])
        if j == 8:
            planes[2 * j + 1] = -sin_odd
            continue
        sin_even = total_of([scaled(math.sin(angle(j * n)), odd[n]) for n in range(2, 16, 2)])
        planes[2 * j + 1] = -(sin_even + sin_odd)
        planes[2 * (16 - j) + 1] = sin_even - sin_odd
    return planes


def backward(planes):
    real = [planes[0]] + [planes[2 * j] * 2.0 for j in range(1, 16)] + [planes[1]]
    imag = [None] + [planes[2 * j + 1] * 2.0 for j in range(1, 16)]
    steps = [None] * 32

    def put(n, cosine, sine):
        if n in (0, 16):
            steps[n] = cosine
            return
        steps[n] = cosine - sine
        steps[32 - n] = cosine + sine

    for n in range(9):
        cos_even = total_of([scaled(math.cos(angle(j * n)), real[j]) for j in range(0, 17, 2)])
        if n == 8:
            sine = total_of([scaled(math.sin(angle(j * n)), imag[j]) for j in range(1, 16, 2)])
            put(8, cos_even, sine)
            continue
        cos_odd = total_of([scaled(math.cos(angle(j * n)), real[j]) for j in range(1, 17, 2)])
        if n == 0:
            put(0, cos_even + cos_odd, None)
            put(16, cos_even - cos_odd, None)
            continue
        sin_odd = total_of([scaled(math.sin(angle(j * n)), imag[j]) for j in range(1, 16, 2)])
        sin_even = total_of([scaled(math.sin(angle(j * n)), imag[j]) for j in range(2, 16, 2)])
        put(n, cos_even + cos_odd, sin_even + sin_odd)
        put(16 - n, cos_even - cos_odd, sin_odd - sin_even)
    return steps


def slots(m):
    lane = lanes(8) % 64
    return (lane >= 8 * m) & (lane < 8 * m + 8)


def in_slots(planes, start):
    groups = []
    for g in range((len(planes) + 7) // 8):
        value = jnp.zeros((8, 128), jnp.float32)
        for m, plane in enumerate(planes[8 * g : 8 * g + 8]):
            value = jnp.where(slots(m), turn(plane, 8 * m - start), value)
        groups.append(value)
    return groups


def block_of(value, inner):
    return pack_left(jnp.where(inner == 1, half_turn(value), value), lanes(32) < 64)


def columns_in_slots(block, inner):
    result = jnp.zeros((8, 128), jnp.float32)
    for r in range(4):
        result = jnp.where(slots(r), turn(block[8 * r : 8 * r + 8], 8 * r - 56 * inner), result)
    return result


def beside_of(value, inner):
    return columns_in_slots(block_of(value, 1 - inner), inner)


def pair_fields(table, cell_class, initial, last):
    core, upper, half = place()[3:6]
    rows = pl.ds(pl.multiple_of((upper * 2 + core) * 64, 64), 64)
    cols = pl.ds(pl.multiple_of(half * 128, 128), 128)
    classes = cell_class[rows, cols]
    courant = jnp.zeros(classes.shape, jnp.float32)
    for k in range(8):
        courant = jnp.where(classes == k, table[k], courant)
    return [courant] + [initial[c, rows, cols] - ALPHA * last[c, rows, cols] for c in range(2)]


def with_start(steps, start_u, start_w):
    return [steps[0] + (start_w + start_u), steps[1] - np.float32(FACTOR) * start_u] + steps[2:]


def transform_kernel(table, cell_class, initial, last, received, planes_out, side_out):
    inner = place()[6]
    courant, start_u, start_w = (
        block_of(value, inner) for value in pair_fields(table, cell_class, initial, last)
    )
    for r in range(4):
        rows = slice(8 * r, 8 * r + 8)
        steps = []
        for t in range(8):
            part = [received[t, 32 * k + 8 * r : 32 * k + 8 * r + 8, :] for k in range(4)]
            part[0] = part[0] + received[(t + 7) % 8, 128 + 8 * r : 136 + 8 * r, :]
            steps.extend(part)
        planes = forward(with_start(steps, start_u[rows], start_w[rows]))
        for p in range(32):
            planes_out[p, rows, :] = planes[p]
        for g, value in enumerate(in_slots(planes, 56 * inner)):
            side_out[4 * g + r] = value
    planes_out[32] = courant
    side_out[16] = columns_in_slots(courant, inner)


def transform(table, cell_class, initial, last, received):
    shapes = ((33, 32, 128), (17, 8, 128))
    return pl.pallas_call(
        transform_kernel,
        in_specs=[pl.BlockSpec(memory_space=pltpu.SMEM)] + [pl.BlockSpec(memory_space=pltpu.VMEM)] * 4,
        out_specs=[pl.BlockSpec(memory_space=pltpu.VMEM)] * 2,
        out_shape=[jax.ShapeDtypeStruct(shape, jnp.float32) for shape in shapes],
        compiler_params=params(),
        name="transform",
    )(table, cell_class, initial, last, received)


def strips_kernel(
    table, cell_class, initial, last, received, planes, beside_out, core_out, cross_out
):
    core, _, _, inner = place()[3:7]
    low = lanes(8) < 64
    courant, start_u, start_w = (
        beside_of(value, inner) for value in pair_fields(table, cell_class, initial, last)
    )
    steps = []
    for t in range(8):
        one, two = received[t, 160:168, :], received[t, 168:176, :]
        first = one + received[(t + 7) % 8, 176:184, :]
        steps.extend([first, turn(one, -32), two, turn(two, -32)])
    beside = forward(with_start(steps, start_u, start_w)) + [courant]
    for p in range(33):
        beside_out[p] = beside[p]
    top, bottom = [], []
    for j in range(17):
        one, two = 2 * j, min(2 * j + 1, 32)
        top.append(jnp.where(low, planes[one, 0:8, :], half_turn(planes[two, 0:8, :])))
        bottom.append(jnp.where(low, half_turn(planes[one, 24:32, :]), planes[two, 24:32, :]))
    top.extend(in_slots(beside, -64))
    bottom.extend(in_slots(beside, 88))
    for i in range(22):
        core_out[i] = jnp.where(core == 0, bottom[i], top[i])
        cross_out[i] = jnp.where(core == 0, top[i], bottom[i])


def strips(table, cell_class, initial, last, received, planes):
    shapes = ((33, 8, 128), (22, 8, 128), (22, 8, 128))
    return pl.pallas_call(
        strips_kernel,
        in_specs=[pl.BlockSpec(memory_space=pltpu.SMEM)] + [pl.BlockSpec(memory_space=pltpu.VMEM)] * 5,
        out_specs=[pl.BlockSpec(memory_space=pltpu.VMEM)] * 3,
        out_shape=[jax.ShapeDtypeStruct(shape, jnp.float32) for shape in shapes],
        compiler_params=params(),
        cost_estimate=cost(2**20),
        name="strips",
    )(table, cell_class, initial, last, received, planes)


def side_matrix():
    rows = lax.broadcasted_iota(jnp.int32, (256, 128), 0) % 128
    gap = (rows - lax.broadcasted_iota(jnp.int32, (256, 128), 1)) % 128
    return jnp.where((gap == 1) | (gap == 127), 1.0, 0.0).astype(jnp.bfloat16)


def sides_by_matrix(field, matrix):
    value = jnp.concatenate(field, axis=0)
    high = value.astype(jnp.bfloat16)
    low = (value - high.astype(jnp.float32)).astype(jnp.bfloat16)
    result = jnp.dot(jnp.concatenate([high, low], axis=1), matrix, preferred_element_type=jnp.float32)
    return [result[8 * v : 8 * v + 8] for v in range(10)]


def sides_by_rotation(field):
    return [pltpu.roll(own, 1, 1) + pltpu.roll(own, 127, 1) for own in field]


def around(field, sides):
    first = pltpu.roll(field[9], 1, 0)
    last = pltpu.roll(field[0], 7, 0)
    above = [first] + field[:9]
    below = field[1:] + [last]
    return [(up + down) + side for up, side, down in zip(above, sides, below)]


def bases(inner):
    return 120 - 56 * inner, 64 + 56 * inner


def merged(centre, side, other, bases):
    lane = lanes(8)
    value = jnp.where(lane < 64, centre, 0.0)
    for base, edge in zip(bases, (side, other)):
        value = jnp.where((lane >= base) & (lane < base + 8), edge, value)
    return value


def in_grid(first_row, count, col0):
    rows = lax.broadcasted_iota(jnp.int32, (count, 128), 0) + first_row
    lane = lanes(count)
    cols = jnp.where(lane >= 120, lane - 128, lane) + col0
    used = (lane < 72) | (lane >= 120)
    return used & (rows >= 0) & (rows < 1024) & (cols >= 0) & (cols < 1024)


def coefficients(lam, j, special, g_re, g_im, courant, inside):
    if special:
        inv_re = inside / (lam[0, 0] + 4.0 * courant)
        inv_im = inside / (lam[0, 1] + 4.0 * courant)
        return g_re * inv_re, g_im * inv_im, courant * inv_re, courant * inv_im
    diag_re = lam[j, 0] + 4.0 * courant
    diag_im = lam[j, 1]
    scale = inside / (diag_re * diag_re + diag_im * diag_im)
    inv_re = diag_re * scale
    inv_im = -diag_im * scale
    return (
        g_re * inv_re - g_im * inv_im,
        g_re * inv_im + g_im * inv_re,
        courant * inv_re,
        courant * inv_im,
    )


def over_frequencies(work):
    for j in range(4):
        work(j, j == 0, 0, 16 * j)

    def group(k, carry):
        for i in range(4):
            work(4 * k + i, False, k, 16 * i)
        return carry

    lax.fori_loop(1, 4, group, 0)


def widen_kernel(lam, planes, beside, from_side, out):
    inner, _, col0 = place()[6:]
    both = bases(inner)

    def extended(p, group, offset):
        edge = beside[p]
        parts = []
        for r in range(8):
            part = slice(8 * (r % 4), 8 * (r % 4) + 8)
            shift = 0 if r < 4 else 64
            tile, start = (16, 8 * (r % 4)) if group is None else (4 * group + r % 4, offset)
            parts.append(
                merged(
                    turn(planes[p, part, :], shift),
                    turn(from_side[tile], both[0] - shift - start),
                    turn(edge, both[1] - shift - 8 * (r % 4)),
                    both,
                )
            )
        return jnp.concatenate(parts, axis=0)

    mask = in_grid(0, 64, col0)
    courant = jnp.where(mask, extended(32, None, 0), 0.0)
    inside = jnp.where(mask, 1.0, 0.0)

    def work(j, special, group, offset):
        g_re, g_im = extended(2 * j, group, offset), extended(2 * j + 1, group, offset + 8)
        for i, value in enumerate(coefficients(lam, j, special, g_re, g_im, courant, inside)):
            out[j, i, 8:72, :] = value

    over_frequencies(work)


def widen(lam, planes, beside, from_side):
    return pl.pallas_call(
        widen_kernel,
        in_specs=[pl.BlockSpec(memory_space=pltpu.SMEM)] + [pl.BlockSpec(memory_space=pltpu.VMEM)] * 3,
        out_specs=pl.BlockSpec(memory_space=pltpu.VMEM),
        out_shape=jax.ShapeDtypeStruct((16, 4, 80, 128), jnp.float32),
        compiler_params=params(),
        cost_estimate=cost(2**21),
        name="widen",
    )(lam, planes, beside, from_side)


def solve_kernel(lam, middle, from_cross, from_core, out, full, solved, wide):
    core, _, _, inner, row0, col0 = place()[3:]
    both = bases(inner)
    low = lanes(32) < 64
    matrix = side_matrix()

    def halo(index):
        one, two = from_core[index], from_cross[index]
        return jnp.where(core == 1, one, two), jnp.where(core == 1, two, one)

    def extended(pair, odd, group, offset, in_slot=0):
        centre, corners = halo(pair), halo(17 + group)
        return jnp.concatenate(
            [
                merged(
                    half_turn(centre[i]) if odd else centre[i],
                    turn(corners[i], both[0] - offset - (0 if i else 64 + in_slot)),
                    turn(corners[i], both[1] - offset - (64 if i else 0)),
                    both,
                )
                for i in range(2)
            ],
            axis=0,
        )

    mask = jnp.concatenate([in_grid(row0 - 8, 8, col0), in_grid(row0 + 64, 8, col0)], axis=0)
    courant = jnp.where(mask, extended(16, False, 4, 0, 24), 0.0)
    inside = jnp.where(mask, 1.0, 0.0)

    def work(j, special, group, offset):
        g_re, g_im = extended(j, False, group, offset), extended(j, True, group, offset + 8)
        for i, value in enumerate(coefficients(lam, j, special, g_re, g_im, courant, inside)):
            full[j, i, 0:8, :] = value[:8]
            full[j, i, 72:80, :] = value[8:]

    over_frequencies(work)

    def keep(p, slot, field):
        for v in range(10):
            wide[slot, pl.ds(v, 8, stride=10), :] = field[v]
        solved[p] = jnp.where(low, wide[slot, 8:40, :], half_turn(wide[slot, 40:72, :]))

    def swept(special, start_re, start_im, gain_re, gain_im, re, im):
        all_re = around(re, sides_by_rotation(re))
        all_im = around(im, sides_by_matrix(im, matrix))
        if special:
            return (
                [start_re[v] + gain_re[v] * all_re[v] for v in range(10)],
                [start_im[v] + gain_im[v] * all_im[v] for v in range(10)],
            )
        return (
            [start_re[v] + (gain_re[v] * all_re[v] - gain_im[v] * all_im[v]) for v in range(10)],
            [start_im[v] + (gain_re[v] * all_im[v] + gain_im[v] * all_re[v]) for v in range(10)],
        )

    def batch(k, has_special):
        sets, fields = [], []
        for i in range(BATCH):
            j = k * BATCH + i
            parts = [[full[j, a, pl.ds(v, 8, stride=10), :] for v in range(10)] for a in range(4)]
            sets.append((has_special and i == 0, *parts))
            fields.append((parts[0], parts[1]))
        for _ in range(SWEEPS - 1):
            fields = [swept(*sets[i], *fields[i]) for i in range(BATCH)]
        for i in range(BATCH):
            j = k * BATCH + i
            keep(2 * j, 2 * i, fields[i][0])
            keep(2 * j + 1, 2 * i + 1, fields[i][1])

    def later(k, carry):
        batch(k, False)
        return carry

    batch(0, True)
    lax.fori_loop(1, 16 // BATCH, later, 0)

    for r in range(4):
        part = slice(8 * r, 8 * r + 8)
        steps = backward([solved[p, part, :] for p in range(32)])
        for n in range(32):
            value = steps[n] * np.float32(math.exp(-n * DECAY) / STEPS)
            t, k = n // 4, n % 4
            out[t, 32 * k + 32 + 8 * r : 32 * k + 40 + 8 * r, :] = value
            if k == 3:
                out[(t + 1) % 8, part, :] = value * np.float32(ALPHA) if n == 31 else value


def solve(lam, middle, from_cross, from_core):
    return pl.pallas_call(
        solve_kernel,
        in_specs=[pl.BlockSpec(memory_space=pltpu.SMEM)] + [pl.BlockSpec(memory_space=pltpu.VMEM)] * 3,
        out_specs=[pl.BlockSpec(memory_space=pltpu.VMEM)] * 2,
        out_shape=[
            jax.ShapeDtypeStruct((8, 160, 128), jnp.float32),
            jax.ShapeDtypeStruct((16, 4, 80, 128), jnp.float32),
        ],
        input_output_aliases={1: 1},
        scratch_shapes=[
            pltpu.VMEM((32, 32, 128), jnp.float32),
            pltpu.VMEM((2 * BATCH, 80, 128), jnp.float32),
        ],
        compiler_params=params(),
        name="solve",
    )(lam, middle, from_cross, from_core)[0]


def finish_kernel(other, units, forcing, initial, last, *refs):
    out, held, sent = refs[-3:]
    tm, odd_x, odd_y, core = place()[:4]
    low = lanes(32) < 64
    first = jnp.where(tm == 0, 1.0, 0.0).astype(jnp.float32)
    begin = 0 if other else pl.multiple_of(64 * core, 64)
    core = core ^ other
    copies = []
    for upper in range(2):
        for half in range(2):
            cols = slice(128 * half, 128 * half + 128)
            ones, twos = (
                [units[chip, pl.ds(begin + 32 * k, 32), :] for k in range(3)]
                for chip in (chip_of(half, upper, inner, odd_x, odd_y) for inner in range(2))
            )
            for part in range(2):
                rows = slice(32 * part, 32 * part + 32)
                if part == 0:
                    values = [jnp.where(low, one, half_turn(two)) for one, two in zip(ones, twos)]
                else:
                    values = [jnp.where(low, half_turn(one), two) for one, two in zip(ones, twos)]
                before, now, after = values
                start = forcing[0, 0, upper, core, rows, cols] + first * (
                    initial[0, upper, core, rows, cols] - ALPHA * last[0, upper, core, rows, cols]
                )
                held[upper, 0, 0, rows, cols] = now
                held[upper, 0, 1, rows, cols] = after
                held[upper, 1, 0, rows, cols] = now - before - start
                held[upper, 1, 1, rows, cols] = after - now - forcing[0, 1, upper, core, rows, cols]
        copies.append(pltpu.make_async_copy(held.at[upper], out.at[:, :, upper, core], sent.at[upper]))
        copies[upper].start()
    for upper in range(2):
        copies[upper].wait()


def finish(units, forcing, initial, last, result=None):
    other = result is not None
    return pl.pallas_call(
        functools.partial(finish_kernel, int(other)),
        in_specs=[pl.BlockSpec(memory_space=pltpu.VMEM)] * 4
        + [pl.BlockSpec(memory_space=pltpu.HBM)] * other,
        out_specs=pl.BlockSpec(memory_space=pltpu.HBM),
        out_shape=jax.ShapeDtypeStruct((2, 2, 2, 2, 64, 256), jnp.float32),
        scratch_shapes=[pltpu.VMEM((2, 2, 2, 64, 256), jnp.float32), pltpu.SemaphoreType.DMA((2,))],
        input_output_aliases={4: 0} if other else {},
        compiler_params=params(),
        cost_estimate=cost(2**20),
        name="finish_other" if other else "finish_own",
    )(
        units,
        forcing.reshape(2, 2, 2, 2, 64, 256),
        initial.reshape(2, 2, 2, 64, 256),
        last.reshape(2, 2, 2, 64, 256),
        *([result] if other else []),
    )


def lam_squares():
    rows = []
    for j in range(16):
        lam = 1.0 - FACTOR * complex(math.cos(angle(j)), -math.sin(angle(j)))
        square = lam * lam
        rows.append((square.real, square.imag))
    rows[0] = ((1.0 - FACTOR) ** 2, (1.0 + FACTOR) ** 2)
    return np.array(rows, np.float32)


def chips_exchange(pieces):
    return lax.all_to_all(pieces, "tm", 0, 0, axis_index_groups=CHIPS, tiled=True)


def per_device(forcing, initial, previous_last, cell_class, courant_table):
    core = lax.axis_index("tm") & 1
    lam = jnp.asarray(lam_squares())
    theirs = prepare(forcing, 1 - core, "prepare_other")
    theirs, rest = lax.optimization_barrier((theirs, forcing))
    theirs = lax.ppermute(theirs, "tm", CORES)
    merged_units, is_upper, is_lower = lax.optimization_barrier(
        (merge(prepare(rest, core, "prepare_own"), theirs), core == 0, core == 1)
    )
    received = chips_exchange(merged_units)
    fields = (courant_table, cell_class, initial, previous_last, received)
    planes, side = transform(*fields)
    from_side = lax.ppermute(side, AXES, TO_SIDE)
    beside, to_core, to_cross = strips(*fields, planes)

    rows = from_side[:16].reshape(4, 4, 8, 128)
    low = lax.broadcasted_iota(jnp.int32, (5, 8, 128), 2) < 64

    def strip(main, is_bottom):
        side = jnp.where(is_bottom, rows[:, 3], rows[:, 0])
        side = jnp.concatenate([side, from_side[16:]], axis=0)
        return jnp.concatenate([main[:17], jnp.where(low != is_bottom, side, main[17:])], axis=0)

    from_cross = lax.ppermute(strip(to_cross, is_lower), AXES, TO_CROSS)
    from_core = lax.ppermute(strip(to_core, is_upper), AXES, TO_CORE)
    middle = widen(lam, planes, beside, from_side)
    returned = chips_exchange(solve(lam, middle, from_cross, from_core))
    wanted = jnp.where(is_upper, returned[:, 64:160], returned[:, 0:96])
    other = lax.ppermute(wanted, "tm", CORES)
    result = finish(returned, forcing, initial, previous_last)
    result = finish(other, forcing, initial, previous_last, result)
    return result.reshape(2, 2, 256, 256)


def solution(mesh):
    in_specs = (
        P(None, "tm", "sx", "sy"),
        P(None, "sx", "sy"),
        P(None, "sx", "sy"),
        P("sx", "sy"),
        P(),
    )
    out_specs = P(None, "tm", "sx", "sy")
    return jax.shard_map(
        per_device, mesh=mesh, in_specs=in_specs, out_specs=out_specs, check_vma=False
    )
```

```python
import functools
import math

import jax
import jax.numpy as jnp
import numpy as np
from jax import lax
from jax.experimental import pallas as pl
from jax.experimental.pallas import tpu as pltpu
from jax.sharding import PartitionSpec as P

STEPS = 32
SWEEPS = 8
BATCH = 8
ALPHA = 0.1
DECAY = math.log(ALPHA) / STEPS
FACTOR = math.exp(DECAY)
AXES = ("tm", "sx", "sy")
VMEM = 16 * 2**20


def chip_of(half, upper, inner, odd_x, odd_y):
    half_y, upper_y = half ^ odd_y, upper ^ odd_x
    return (2 * half_y + (upper_y ^ half_y)) * 2 + (inner ^ half)


def device_of(row, col):
    row, col = row % 16, col % 16
    sx, upper, core = row // 4, row // 2 % 2, row % 2
    sy, half, inner = col // 4, col // 2 % 2, col % 2
    tm = chip_of(half, upper, inner, sx & 1, sy & 1) * 2 + core
    return (tm * 4 + sx) * 4 + sy


def pairs_of(move):
    return [
        (device_of(row, col), device_of(*move(row, col))) for row in range(16) for col in range(16)
    ]


def away(index):
    return index - 1 if index % 2 == 0 else index + 1


def side_of(row, col):
    return (row, away(col)) if 0 < col < 15 else (row ^ 1, col)


TO_SIDE = pairs_of(side_of)
TO_CORE = pairs_of(lambda row, col: (row ^ 1, col))
TO_CROSS = pairs_of(lambda row, col: (away(row), col))
CHIPS = [[chip * 2 + core for chip in range(8)] for core in range(2)]
CORES = [(tm, tm ^ 1) for tm in range(16)]


def lanes(rows):
    return lax.broadcasted_iota(jnp.int32, (rows, 128), 1)


def half_turn(value):
    return pltpu.roll(value, 64, 1)


def pack_left(value, low):
    return jnp.where(low, value[:32], half_turn(value[32:]))


def pack_right(value, low):
    return jnp.where(low, half_turn(value[:32]), value[32:])


def place():
    tm, sx, sy = (lax.axis_index(axis) for axis in AXES)
    odd_x, odd_y = sx & 1, sy & 1
    y, z, core = tm >> 2, tm >> 1 & 1, tm & 1
    half_y = y >> 1
    upper_y = (y & 1) ^ half_y
    half, upper = half_y ^ odd_y, upper_y ^ odd_x
    inner = z ^ half
    row0 = sx * 256 + upper * 128 + core * 64
    col0 = sy * 256 + half * 128 + inner * 64
    return tm, odd_x, odd_y, core, upper, half, inner, row0, col0


def params():
    return pltpu.CompilerParams(vmem_limit_bytes=VMEM)


def cost(size):
    return pl.CostEstimate(flops=size, bytes_accessed=size, transcendentals=0)


def turn(value, shift):
    if isinstance(shift, int):
        return pltpu.roll(value, shift % 128, 1) if shift % 128 else value
    return pltpu.roll(value, lax.rem(shift + 256, 128), 1)


def prepare_kernel(forcing, out):
    tm, odd_x, odd_y = place()[:3]
    low = lanes(32) < 64
    weight = jnp.float32(1.0)
    for bit in range(4):
        step = math.exp(DECAY * 2 ** (bit + 1))
        weight = weight * jnp.where((tm >> bit & 1) == 1, step, 1.0).astype(jnp.float32)
    weight_two = weight * np.float32(FACTOR)
    weight_three = weight * np.float32(-FACTOR * FACTOR)
    for upper in range(2):
        for half in range(2):
            cols = slice(128 * half, 128 * half + 128)
            first_u, second_u = forcing[0, 0, upper, :, cols], forcing[0, 1, upper, :, cols]
            first_w, second_w = forcing[1, 0, upper, :, cols], forcing[1, 1, upper, :, cols]
            units = (
                weight * (first_w + first_u),
                weight_two * (second_w + second_u - first_u),
                weight_three * second_u,
            )
            left = chip_of(half, upper, 0, odd_x, odd_y)
            right = chip_of(half, upper, 1, odd_x, odd_y)
            for k, unit in enumerate(units):
                rows = slice(32 * k, 32 * k + 32)
                out[left, rows, :] = pack_left(unit, low)
                out[right, rows, :] = pack_right(unit, low)


def prepare(forcing, core, name):
    rows = lax.dynamic_index_in_dim(forcing.reshape(2, 2, 2, 2, 64, 256), core, 3, keepdims=False)
    return pl.pallas_call(
        prepare_kernel,
        in_specs=[pl.BlockSpec(memory_space=pltpu.VMEM)],
        out_specs=pl.BlockSpec(memory_space=pltpu.VMEM),
        out_shape=jax.ShapeDtypeStruct((8, 96, 128), jnp.float32),
        compiler_params=params(),
        cost_estimate=cost(2**20),
        name=name,
    )(rows)


def merge_kernel(mine, received, out):
    _, odd_x, odd_y, core = place()[:4]
    is_first = core == 0
    lane8 = lanes(8) % 64
    for chip in range(8):
        for k in range(3):
            rows = slice(32 * k, 32 * k + 32)
            own, other = mine[chip, rows, :], received[chip, rows, :]
            early, late = jnp.where(is_first, own, other), jnp.where(is_first, other, own)
            if k < 2:
                out[chip, 32 * k : 32 * k + 32, :] = early
                kept = late if k == 0 else kept
                if k == 1:
                    out[chip, 96:128, :] = late
            else:
                out[chip, 64:96, :] = kept + early
                out[chip, 128:160, :] = late
    for chip in range(8):
        inner = (chip & 1) ^ (chip >> 2) ^ odd_y
        for tile in range(3):
            value = jnp.zeros((8, 128), jnp.float32)
            for m in range(8):
                k, r = (8 * tile + m) // 4, m % 4
                if k == 5:
                    break
                beside = out[chip ^ 1, 32 * k + 8 * r : 32 * k + 8 * r + 8, :]
                here = (lane8 >= 8 * m) & (lane8 < 8 * m + 8)
                value = jnp.where(here, turn(beside, 8 * m - 56 * inner), value)
            out[chip, 160 + 8 * tile : 168 + 8 * tile, :] = value


def merge(mine, received):
    return pl.pallas_call(
        merge_kernel,
        in_specs=[pl.BlockSpec(memory_space=pltpu.VMEM)] * 2,
        out_specs=pl.BlockSpec(memory_space=pltpu.VMEM),
        out_shape=jax.ShapeDtypeStruct((8, 184, 128), jnp.float32),
        compiler_params=params(),
        name="merge",
    )(mine, received)


def scaled(factor, value):
    if abs(factor) < 1e-12:
        return None
    if abs(factor - 1.0) < 1e-12:
        return value
    if abs(factor + 1.0) < 1e-12:
        return -value
    return np.float32(factor) * value


def total_of(terms):
    terms = [term for term in terms if term is not None]
    result = terms[0]
    for term in terms[1:]:
        result = result + term
    return result


def angle(index):
    return 2.0 * math.pi * (index % STEPS) / STEPS


def forward(steps):
    even = [steps[0]] + [steps[n] + steps[32 - n] for n in range(1, 16)] + [steps[16]]
    odd = [None] + [steps[n] - steps[32 - n] for n in range(1, 16)]
    planes = [None] * 32
    for j in range(9):
        cos_even = total_of([scaled(math.cos(angle(j * n)), even[n]) for n in range(0, 17, 2)])
        cos_odd = (
            None if j == 8 else total_of([scaled(math.cos(angle(j * n)), even[n]) for n in range(1, 17, 2)])
        )
        high, lowp = (
            (cos_even, None) if cos_odd is None else (cos_even + cos_odd, cos_even - cos_odd)
        )
        if j == 0:
            planes[0], planes[1] = high, lowp
            continue
        planes[2 * j] = high
        if j < 8:
            planes[2 * (16 - j)] = lowp
        sin_odd = total_of([scaled(math.sin(angle(j * n)), odd[n]) for n in range(1, 16, 2)])
        if j == 8:
            planes[2 * j + 1] = -sin_odd
            continue
        sin_even = total_of([scaled(math.sin(angle(j * n)), odd[n]) for n in range(2, 16, 2)])
        planes[2 * j + 1] = -(sin_even + sin_odd)
        planes[2 * (16 - j) + 1] = sin_even - sin_odd
    return planes


def backward(planes):
    real = [planes[0]] + [planes[2 * j] * 2.0 for j in range(1, 16)] + [planes[1]]
    imag = [None] + [planes[2 * j + 1] * 2.0 for j in range(1, 16)]
    steps = [None] * 32

    def put(n, cosine, sine):
        if n in (0, 16):
            steps[n] = cosine
            return
        steps[n] = cosine - sine
        steps[32 - n] = cosine + sine

    for n in range(9):
        cos_even = total_of([scaled(math.cos(angle(j * n)), real[j]) for j in range(0, 17, 2)])
        if n == 8:
            sine = total_of([scaled(math.sin(angle(j * n)), imag[j]) for j in range(1, 16, 2)])
            put(8, cos_even, sine)
            continue
        cos_odd = total_of([scaled(math.cos(angle(j * n)), real[j]) for j in range(1, 17, 2)])
        if n == 0:
            put(0, cos_even + cos_odd, None)
            put(16, cos_even - cos_odd, None)
            continue
        sin_odd = total_of([scaled(math.sin(angle(j * n)), imag[j]) for j in range(1, 16, 2)])
        sin_even = total_of([scaled(math.sin(angle(j * n)), imag[j]) for j in range(2, 16, 2)])
        put(n, cos_even + cos_odd, sin_even + sin_odd)
        put(16 - n, cos_even - cos_odd, sin_odd - sin_even)
    return steps


def slots(m):
    lane = lanes(8) % 64
    return (lane >= 8 * m) & (lane < 8 * m + 8)


def in_slots(planes, start):
    groups = []
    for g in range((len(planes) + 7) // 8):
        value = jnp.zeros((8, 128), jnp.float32)
        for m, plane in enumerate(planes[8 * g : 8 * g + 8]):
            value = jnp.where(slots(m), turn(plane, 8 * m - start), value)
        groups.append(value)
    return groups


def block_of(value, inner):
    return pack_left(jnp.where(inner == 1, half_turn(value), value), lanes(32) < 64)


def columns_in_slots(block, inner):
    result = jnp.zeros((8, 128), jnp.float32)
    for r in range(4):
        result = jnp.where(slots(r), turn(block[8 * r : 8 * r + 8], 8 * r - 56 * inner), result)
    return result


def beside_of(value, inner):
    return columns_in_slots(block_of(value, 1 - inner), inner)


def pair_fields(table, cell_class, initial, last):
    core, upper, half = place()[3:6]
    rows = pl.ds(pl.multiple_of((upper * 2 + core) * 64, 64), 64)
    cols = pl.ds(pl.multiple_of(half * 128, 128), 128)
    classes = cell_class[rows, cols]
    courant = jnp.zeros(classes.shape, jnp.float32)
    for k in range(8):
        courant = jnp.where(classes == k, table[k], courant)
    return [courant] + [initial[c, rows, cols] - ALPHA * last[c, rows, cols] for c in range(2)]


def with_start(steps, start_u, start_w):
    return [steps[0] + (start_w + start_u), steps[1] - np.float32(FACTOR) * start_u] + steps[2:]


def transform_kernel(table, cell_class, initial, last, received, planes_out, side_out):
    inner = place()[6]
    courant, start_u, start_w = (
        block_of(value, inner) for value in pair_fields(table, cell_class, initial, last)
    )
    for r in range(4):
        rows = slice(8 * r, 8 * r + 8)
        steps = []
        for t in range(8):
            part = [received[t, 32 * k + 8 * r : 32 * k + 8 * r + 8, :] for k in range(4)]
            part[0] = part[0] + received[(t + 7) % 8, 128 + 8 * r : 136 + 8 * r, :]
            steps.extend(part)
        planes = forward(with_start(steps, start_u[rows], start_w[rows]))
        for p in range(32):
            planes_out[p, rows, :] = planes[p]
        for g, value in enumerate(in_slots(planes, 56 * inner)):
            side_out[4 * g + r] = value
    planes_out[32] = courant
    side_out[16] = columns_in_slots(courant, inner)


def transform(table, cell_class, initial, last, received):
    shapes = ((33, 32, 128), (17, 8, 128))
    return pl.pallas_call(
        transform_kernel,
        in_specs=[pl.BlockSpec(memory_space=pltpu.SMEM)] + [pl.BlockSpec(memory_space=pltpu.VMEM)] * 4,
        out_specs=[pl.BlockSpec(memory_space=pltpu.VMEM)] * 2,
        out_shape=[jax.ShapeDtypeStruct(shape, jnp.float32) for shape in shapes],
        compiler_params=params(),
        name="transform",
    )(table, cell_class, initial, last, received)


def bases(inner):
    return 120 - 56 * inner, 64 + 56 * inner


def placed(value, edge, base):
    lane = lanes(8)
    return jnp.where((lane >= base) & (lane < base + 8), edge, value)


def merged(centre, side, other, bases):
    value = jnp.where(lanes(8) < 64, centre, 0.0)
    return placed(placed(value, side, bases[0]), other, bases[1])


def strips_kernel(
    table, cell_class, initial, last, received, planes, wide_out, core_out, cross_out
):
    core, _, _, inner = place()[3:7]
    low = lanes(8) < 64
    courant, start_u, start_w = (
        beside_of(value, inner) for value in pair_fields(table, cell_class, initial, last)
    )
    steps = []
    for t in range(8):
        one, two = received[t, 160:168, :], received[t, 168:176, :]
        first = one + received[(t + 7) % 8, 176:184, :]
        steps.extend([first, turn(one, -32), two, turn(two, -32)])
    beside = forward(with_start(steps, start_u, start_w)) + [courant]
    base = bases(inner)[1]
    for p in range(33):
        for r in range(8):
            shift, start = 64 * (r // 4), 8 * (r % 4)
            value = jnp.where(lanes(8) < 64, turn(planes[p, start : start + 8, :], shift), 0.0)
            wide_out[p, 8 * r : 8 * r + 8, :] = placed(value, turn(beside[p], base - shift - start), base)
    top, bottom = [], []
    for j in range(17):
        one, two = 2 * j, min(2 * j + 1, 32)
        top.append(jnp.where(low, planes[one, 0:8, :], half_turn(planes[two, 0:8, :])))
        bottom.append(jnp.where(low, half_turn(planes[one, 24:32, :]), planes[two, 24:32, :]))
    top.extend(in_slots(beside, -64))
    bottom.extend(in_slots(beside, 88))
    for i in range(22):
        core_out[i] = jnp.where(core == 0, bottom[i], top[i])
        cross_out[i] = jnp.where(core == 0, top[i], bottom[i])


def strips(table, cell_class, initial, last, received, planes):
    shapes = ((33, 64, 128), (22, 8, 128), (22, 8, 128))
    return pl.pallas_call(
        strips_kernel,
        in_specs=[pl.BlockSpec(memory_space=pltpu.SMEM)] + [pl.BlockSpec(memory_space=pltpu.VMEM)] * 5,
        out_specs=[pl.BlockSpec(memory_space=pltpu.VMEM)] * 3,
        out_shape=[jax.ShapeDtypeStruct(shape, jnp.float32) for shape in shapes],
        compiler_params=params(),
        cost_estimate=cost(2**20),
        name="strips",
    )(table, cell_class, initial, last, received, planes)


def side_matrix():
    rows = lax.broadcasted_iota(jnp.int32, (256, 128), 0) % 128
    gap = (rows - lax.broadcasted_iota(jnp.int32, (256, 128), 1)) % 128
    return jnp.where((gap == 1) | (gap == 127), 1.0, 0.0).astype(jnp.bfloat16)


def sides_by_matrix(field, matrix):
    value = jnp.concatenate(field, axis=0)
    high = value.astype(jnp.bfloat16)
    low = (value - high.astype(jnp.float32)).astype(jnp.bfloat16)
    result = jnp.dot(jnp.concatenate([high, low], axis=1), matrix, preferred_element_type=jnp.float32)
    return [result[8 * v : 8 * v + 8] for v in range(10)]


def sides_by_rotation(field):
    return [pltpu.roll(own, 1, 1) + pltpu.roll(own, 127, 1) for own in field]


def around(field, sides):
    first = pltpu.roll(field[9], 1, 0)
    last = pltpu.roll(field[0], 7, 0)
    above = [first] + field[:9]
    below = field[1:] + [last]
    return [(up + down) + side for up, side, down in zip(above, sides, below)]


def in_grid(first_row, count, col0):
    rows = lax.broadcasted_iota(jnp.int32, (count, 128), 0) + first_row
    lane = lanes(count)
    cols = jnp.where(lane >= 120, lane - 128, lane) + col0
    used = (lane < 72) | (lane >= 120)
    return used & (rows >= 0) & (rows < 1024) & (cols >= 0) & (cols < 1024)


def coefficients(lam, j, special, g_re, g_im, courant, inside):
    if special:
        inv_re = inside / (lam[0, 0] + 4.0 * courant)
        inv_im = inside / (lam[0, 1] + 4.0 * courant)
        return g_re * inv_re, g_im * inv_im, courant * inv_re, courant * inv_im
    diag_re = lam[j, 0] + 4.0 * courant
    diag_im = lam[j, 1]
    scale = inside / (diag_re * diag_re + diag_im * diag_im)
    inv_re = diag_re * scale
    inv_im = -diag_im * scale
    return (
        g_re * inv_re - g_im * inv_im,
        g_re * inv_im + g_im * inv_re,
        courant * inv_re,
        courant * inv_im,
    )


def over_frequencies(work):
    for j in range(4):
        work(j, j == 0, 0, 16 * j)

    def group(k, carry):
        for i in range(4):
            work(4 * k + i, False, k, 16 * i)
        return carry

    lax.fori_loop(1, 4, group, 0)


def widen_kernel(lam, wide, from_side, out):
    inner, _, col0 = place()[6:]
    base = bases(inner)[0]

    def extended(p, group, offset):
        parts = []
        for r in range(8):
            shift = 64 * (r // 4)
            tile, start = (16, 8 * (r % 4)) if group is None else (4 * group + r % 4, offset)
            edge = turn(from_side[tile], base - shift - start)
            parts.append(placed(wide[p, 8 * r : 8 * r + 8, :], edge, base))
        return jnp.concatenate(parts, axis=0)

    mask = in_grid(0, 64, col0)
    courant = jnp.where(mask, extended(32, None, 0), 0.0)
    inside = jnp.where(mask, 1.0, 0.0)

    def work(j, special, group, offset):
        g_re, g_im = extended(2 * j, group, offset), extended(2 * j + 1, group, offset + 8)
        for i, value in enumerate(coefficients(lam, j, special, g_re, g_im, courant, inside)):
            out[j, i, 8:72, :] = value

    over_frequencies(work)


def widen(lam, wide, from_side):
    return pl.pallas_call(
        widen_kernel,
        in_specs=[pl.BlockSpec(memory_space=pltpu.SMEM)] + [pl.BlockSpec(memory_space=pltpu.VMEM)] * 2,
        out_specs=pl.BlockSpec(memory_space=pltpu.VMEM),
        out_shape=jax.ShapeDtypeStruct((16, 4, 80, 128), jnp.float32),
        compiler_params=params(),
        cost_estimate=cost(2**21),
        name="widen",
    )(lam, wide, from_side)


def solve_kernel(lam, middle, from_cross, from_core, out, full, solved, wide):
    core, _, _, inner, row0, col0 = place()[3:]
    both = bases(inner)
    low = lanes(32) < 64
    matrix = side_matrix()

    def halo(index):
        one, two = from_core[index], from_cross[index]
        return jnp.where(core == 1, one, two), jnp.where(core == 1, two, one)

    def extended(pair, odd, group, offset, in_slot=0):
        centre, corners = halo(pair), halo(17 + group)
        return jnp.concatenate(
            [
                merged(
                    half_turn(centre[i]) if odd else centre[i],
                    turn(corners[i], both[0] - offset - (0 if i else 64 + in_slot)),
                    turn(corners[i], both[1] - offset - (64 if i else 0)),
                    both,
                )
                for i in range(2)
            ],
            axis=0,
        )

    mask = jnp.concatenate([in_grid(row0 - 8, 8, col0), in_grid(row0 + 64, 8, col0)], axis=0)
    courant = jnp.where(mask, extended(16, False, 4, 0, 24), 0.0)
    inside = jnp.where(mask, 1.0, 0.0)

    def work(j, special, group, offset):
        g_re, g_im = extended(j, False, group, offset), extended(j, True, group, offset + 8)
        for i, value in enumerate(coefficients(lam, j, special, g_re, g_im, courant, inside)):
            full[j, i, 0:8, :] = value[:8]
            full[j, i, 72:80, :] = value[8:]

    over_frequencies(work)

    def keep(p, slot, field):
        for v in range(10):
            wide[slot, pl.ds(v, 8, stride=10), :] = field[v]
        solved[p] = jnp.where(low, wide[slot, 8:40, :], half_turn(wide[slot, 40:72, :]))

    def swept(special, start_re, start_im, gain_re, gain_im, re, im):
        all_re = around(re, sides_by_rotation(re))
        all_im = around(im, sides_by_matrix(im, matrix))
        if special:
            return (
                [start_re[v] + gain_re[v] * all_re[v] for v in range(10)],
                [start_im[v] + gain_im[v] * all_im[v] for v in range(10)],
            )
        return (
            [start_re[v] + (gain_re[v] * all_re[v] - gain_im[v] * all_im[v]) for v in range(10)],
            [start_im[v] + (gain_re[v] * all_im[v] + gain_im[v] * all_re[v]) for v in range(10)],
        )

    def batch(k, has_special):
        sets, fields = [], []
        for i in range(BATCH):
            j = k * BATCH + i
            parts = [[full[j, a, pl.ds(v, 8, stride=10), :] for v in range(10)] for a in range(4)]
            sets.append((has_special and i == 0, *parts))
            fields.append((parts[0], parts[1]))
        for _ in range(SWEEPS - 1):
            fields = [swept(*sets[i], *fields[i]) for i in range(BATCH)]
        for i in range(BATCH):
            j = k * BATCH + i
            keep(2 * j, 2 * i, fields[i][0])
            keep(2 * j + 1, 2 * i + 1, fields[i][1])

    def later(k, carry):
        batch(k, False)
        return carry

    batch(0, True)
    lax.fori_loop(1, 16 // BATCH, later, 0)

    for r in range(4):
        part = slice(8 * r, 8 * r + 8)
        steps = backward([solved[p, part, :] for p in range(32)])
        for n in range(32):
            value = steps[n] * np.float32(math.exp(-n * DECAY) / STEPS)
            t, k = n // 4, n % 4
            out[t, 32 * k + 32 + 8 * r : 32 * k + 40 + 8 * r, :] = value
            if k == 3:
                out[(t + 1) % 8, part, :] = value * np.float32(ALPHA) if n == 31 else value


def solve(lam, middle, from_cross, from_core):
    return pl.pallas_call(
        solve_kernel,
        in_specs=[pl.BlockSpec(memory_space=pltpu.SMEM)] + [pl.BlockSpec(memory_space=pltpu.VMEM)] * 3,
        out_specs=[pl.BlockSpec(memory_space=pltpu.VMEM)] * 2,
        out_shape=[
            jax.ShapeDtypeStruct((8, 160, 128), jnp.float32),
            jax.ShapeDtypeStruct((16, 4, 80, 128), jnp.float32),
        ],
        input_output_aliases={1: 1},
        scratch_shapes=[
            pltpu.VMEM((32, 32, 128), jnp.float32),
            pltpu.VMEM((2 * BATCH, 80, 128), jnp.float32),
        ],
        compiler_params=params(),
        name="solve",
    )(lam, middle, from_cross, from_core)[0]


def finish_kernel(other, units, forcing, initial, last, *refs):
    out, held, sent = refs[-3:]
    tm, odd_x, odd_y, core = place()[:4]
    low = lanes(32) < 64
    first = jnp.where(tm == 0, 1.0, 0.0).astype(jnp.float32)
    begin = 0 if other else pl.multiple_of(64 * core, 64)
    core = core ^ other
    copies = []
    for upper in range(2):
        for half in range(2):
            cols = slice(128 * half, 128 * half + 128)
            ones, twos = (
                [units[chip, pl.ds(begin + 32 * k, 32), :] for k in range(3)]
                for chip in (chip_of(half, upper, inner, odd_x, odd_y) for inner in range(2))
            )
            for part in range(2):
                rows = slice(32 * part, 32 * part + 32)
                if part == 0:
                    values = [jnp.where(low, one, half_turn(two)) for one, two in zip(ones, twos)]
                else:
                    values = [jnp.where(low, half_turn(one), two) for one, two in zip(ones, twos)]
                before, now, after = values
                start = forcing[0, 0, upper, core, rows, cols] + first * (
                    initial[0, upper, core, rows, cols] - ALPHA * last[0, upper, core, rows, cols]
                )
                held[upper, 0, 0, rows, cols] = now
                held[upper, 0, 1, rows, cols] = after
                held[upper, 1, 0, rows, cols] = now - before - start
                held[upper, 1, 1, rows, cols] = after - now - forcing[0, 1, upper, core, rows, cols]
        copies.append(pltpu.make_async_copy(held.at[upper], out.at[:, :, upper, core], sent.at[upper]))
        copies[upper].start()
    for upper in range(2):
        copies[upper].wait()


def finish(units, forcing, initial, last, result=None):
    other = result is not None
    return pl.pallas_call(
        functools.partial(finish_kernel, int(other)),
        in_specs=[pl.BlockSpec(memory_space=pltpu.VMEM)] * 4
        + [pl.BlockSpec(memory_space=pltpu.HBM)] * other,
        out_specs=pl.BlockSpec(memory_space=pltpu.HBM),
        out_shape=jax.ShapeDtypeStruct((2, 2, 2, 2, 64, 256), jnp.float32),
        scratch_shapes=[pltpu.VMEM((2, 2, 2, 64, 256), jnp.float32), pltpu.SemaphoreType.DMA((2,))],
        input_output_aliases={4: 0} if other else {},
        compiler_params=params(),
        cost_estimate=cost(2**20),
        name="finish_other" if other else "finish_own",
    )(
        units,
        forcing.reshape(2, 2, 2, 2, 64, 256),
        initial.reshape(2, 2, 2, 64, 256),
        last.reshape(2, 2, 2, 64, 256),
        *([result] if other else []),
    )


def lam_squares():
    rows = []
    for j in range(16):
        lam = 1.0 - FACTOR * complex(math.cos(angle(j)), -math.sin(angle(j)))
        square = lam * lam
        rows.append((square.real, square.imag))
    rows[0] = ((1.0 - FACTOR) ** 2, (1.0 + FACTOR) ** 2)
    return np.array(rows, np.float32)


def chips_exchange(pieces):
    return lax.all_to_all(pieces, "tm", 0, 0, axis_index_groups=CHIPS, tiled=True)


def per_device(forcing, initial, previous_last, cell_class, courant_table):
    core = lax.axis_index("tm") & 1
    lam = jnp.asarray(lam_squares())
    theirs = prepare(forcing, 1 - core, "prepare_other")
    theirs, rest = lax.optimization_barrier((theirs, forcing))
    theirs = lax.ppermute(theirs, "tm", CORES)
    merged_units, is_upper, is_lower = lax.optimization_barrier(
        (merge(prepare(rest, core, "prepare_own"), theirs), core == 0, core == 1)
    )
    received = chips_exchange(merged_units)
    fields = (courant_table, cell_class, initial, previous_last, received)
    planes, side = transform(*fields)
    from_side = lax.ppermute(side, AXES, TO_SIDE)
    wide, to_core, to_cross = strips(*fields, planes)

    rows = from_side[:16].reshape(4, 4, 8, 128)
    low = lax.broadcasted_iota(jnp.int32, (5, 8, 128), 2) < 64

    def strip(main, is_bottom):
        side = jnp.where(is_bottom, rows[:, 3], rows[:, 0])
        side = jnp.concatenate([side, from_side[16:]], axis=0)
        return jnp.concatenate([main[:17], jnp.where(low != is_bottom, side, main[17:])], axis=0)

    from_cross = lax.ppermute(strip(to_cross, is_lower), AXES, TO_CROSS)
    from_core = lax.ppermute(strip(to_core, is_upper), AXES, TO_CORE)
    middle = widen(lam, wide, from_side)
    returned = chips_exchange(solve(lam, middle, from_cross, from_core))
    wanted = jnp.where(is_upper, returned[:, 64:160], returned[:, 0:96])
    other = lax.ppermute(wanted, "tm", CORES)
    result = finish(returned, forcing, initial, previous_last)
    result = finish(other, forcing, initial, previous_last, result)
    return result.reshape(2, 2, 256, 256)


def solution(mesh):
    in_specs = (
        P(None, "tm", "sx", "sy"),
        P(None, "sx", "sy"),
        P(None, "sx", "sy"),
        P("sx", "sy"),
        P(),
    )
    out_specs = P(None, "tm", "sx", "sy")
    return jax.shard_map(
        per_device, mesh=mesh, in_specs=in_specs, out_specs=out_specs, check_vma=False
    )
```

```python
import functools
import math

import jax
import jax.numpy as jnp
import numpy as np
from jax import lax
from jax.experimental import pallas as pl
from jax.experimental.pallas import tpu as pltpu
from jax.sharding import PartitionSpec as P

STEPS = 32
SWEEPS = 8
BATCH = 8
ROOM = 96
ALPHA = 0.1
DECAY = math.log(ALPHA) / STEPS
FACTOR = math.exp(DECAY)
AXES = ("tm", "sx", "sy")
VMEM = 16 * 2**20


def chip_of(half, upper, inner, odd_x, odd_y):
    half_y, upper_y = half ^ odd_y, upper ^ odd_x
    return (2 * half_y + (upper_y ^ half_y)) * 2 + (inner ^ half)


def device_of(row, col):
    row, col = row % 16, col % 16
    sx, upper, core = row // 4, row // 2 % 2, row % 2
    sy, half, inner = col // 4, col // 2 % 2, col % 2
    tm = chip_of(half, upper, inner, sx & 1, sy & 1) * 2 + core
    return (tm * 4 + sx) * 4 + sy


def pairs_of(move):
    return [
        (device_of(row, col), device_of(*move(row, col))) for row in range(16) for col in range(16)
    ]


def away(index):
    return index - 1 if index % 2 == 0 else index + 1


def side_of(row, col):
    return (row, away(col)) if 0 < col < 15 else (row ^ 1, col)


TO_SIDE = pairs_of(side_of)
TO_CORE = pairs_of(lambda row, col: (row ^ 1, col))
TO_CROSS = pairs_of(lambda row, col: (away(row), col))
CHIPS = [[chip * 2 + core for chip in range(8)] for core in range(2)]
CORES = [(tm, tm ^ 1) for tm in range(16)]


def lanes(rows):
    return lax.broadcasted_iota(jnp.int32, (rows, 128), 1)


def half_turn(value):
    return pltpu.roll(value, 64, 1)


def pack_left(value, low):
    return jnp.where(low, value[:32], half_turn(value[32:]))


def pack_right(value, low):
    return jnp.where(low, half_turn(value[:32]), value[32:])


def place():
    tm, sx, sy = (lax.axis_index(axis) for axis in AXES)
    odd_x, odd_y = sx & 1, sy & 1
    y, z, core = tm >> 2, tm >> 1 & 1, tm & 1
    half_y = y >> 1
    upper_y = (y & 1) ^ half_y
    half, upper = half_y ^ odd_y, upper_y ^ odd_x
    inner = z ^ half
    row0 = sx * 256 + upper * 128 + core * 64
    col0 = sy * 256 + half * 128 + inner * 64
    return tm, odd_x, odd_y, core, upper, half, inner, row0, col0


def params():
    return pltpu.CompilerParams(vmem_limit_bytes=VMEM)


def cost(size):
    return pl.CostEstimate(flops=size, bytes_accessed=size, transcendentals=0)


def turn(value, shift):
    if isinstance(shift, int):
        return pltpu.roll(value, shift % 128, 1) if shift % 128 else value
    return pltpu.roll(value, lax.rem(shift + 256, 128), 1)


def prepare_kernel(forcing, out):
    tm, odd_x, odd_y = place()[:3]
    low = lanes(32) < 64
    weight = jnp.float32(1.0)
    for bit in range(4):
        step = math.exp(DECAY * 2 ** (bit + 1))
        weight = weight * jnp.where((tm >> bit & 1) == 1, step, 1.0).astype(jnp.float32)
    weight_two = weight * np.float32(FACTOR)
    weight_three = weight * np.float32(-FACTOR * FACTOR)
    for upper in range(2):
        for half in range(2):
            cols = slice(128 * half, 128 * half + 128)
            first_u, second_u = forcing[0, 0, upper, :, cols], forcing[0, 1, upper, :, cols]
            first_w, second_w = forcing[1, 0, upper, :, cols], forcing[1, 1, upper, :, cols]
            units = (
                weight * (first_w + first_u),
                weight_two * (second_w + second_u - first_u),
                weight_three * second_u,
            )
            left = chip_of(half, upper, 0, odd_x, odd_y)
            right = chip_of(half, upper, 1, odd_x, odd_y)
            for k, unit in enumerate(units):
                rows = slice(32 * k, 32 * k + 32)
                out[left, rows, :] = pack_left(unit, low)
                out[right, rows, :] = pack_right(unit, low)


def prepare(forcing, core, name):
    rows = lax.dynamic_index_in_dim(forcing.reshape(2, 2, 2, 2, 64, 256), core, 3, keepdims=False)
    return pl.pallas_call(
        prepare_kernel,
        in_specs=[pl.BlockSpec(memory_space=pltpu.VMEM)],
        out_specs=pl.BlockSpec(memory_space=pltpu.VMEM),
        out_shape=jax.ShapeDtypeStruct((8, 96, 128), jnp.float32),
        compiler_params=params(),
        cost_estimate=cost(2**20),
        name=name,
    )(rows)


def merge_kernel(mine, received, out):
    _, odd_x, odd_y, core = place()[:4]
    is_first = core == 0
    lane8 = lanes(8) % 64
    for chip in range(8):
        for k in range(3):
            rows = slice(32 * k, 32 * k + 32)
            own, other = mine[chip, rows, :], received[chip, rows, :]
            early, late = jnp.where(is_first, own, other), jnp.where(is_first, other, own)
            if k < 2:
                out[chip, 32 * k : 32 * k + 32, :] = early
                kept = late if k == 0 else kept
                if k == 1:
                    out[chip, 96:128, :] = late
            else:
                out[chip, 64:96, :] = kept + early
                out[chip, 128:160, :] = late
    for chip in range(8):
        inner = (chip & 1) ^ (chip >> 2) ^ odd_y
        for tile in range(3):
            value = jnp.zeros((8, 128), jnp.float32)
            for m in range(8):
                k, r = (8 * tile + m) // 4, m % 4
                if k == 5:
                    break
                beside = out[chip ^ 1, 32 * k + 8 * r : 32 * k + 8 * r + 8, :]
                here = (lane8 >= 8 * m) & (lane8 < 8 * m + 8)
                value = jnp.where(here, turn(beside, 8 * m - 56 * inner), value)
            out[chip, 160 + 8 * tile : 168 + 8 * tile, :] = value


def merge(mine, received):
    return pl.pallas_call(
        merge_kernel,
        in_specs=[pl.BlockSpec(memory_space=pltpu.VMEM)] * 2,
        out_specs=pl.BlockSpec(memory_space=pltpu.VMEM),
        out_shape=jax.ShapeDtypeStruct((8, 184, 128), jnp.float32),
        compiler_params=params(),
        name="merge",
    )(mine, received)


def scaled(factor, value):
    if abs(factor) < 1e-12:
        return None
    if abs(factor - 1.0) < 1e-12:
        return value
    if abs(factor + 1.0) < 1e-12:
        return -value
    return np.float32(factor) * value


def total_of(terms):
    terms = [term for term in terms if term is not None]
    result = terms[0]
    for term in terms[1:]:
        result = result + term
    return result


def angle(index):
    return 2.0 * math.pi * (index % STEPS) / STEPS


def forward(steps):
    even = [steps[0]] + [steps[n] + steps[32 - n] for n in range(1, 16)] + [steps[16]]
    odd = [None] + [steps[n] - steps[32 - n] for n in range(1, 16)]
    planes = [None] * 32
    for j in range(9):
        cos_even = total_of([scaled(math.cos(angle(j * n)), even[n]) for n in range(0, 17, 2)])
        cos_odd = (
            None if j == 8 else total_of([scaled(math.cos(angle(j * n)), even[n]) for n in range(1, 17, 2)])
        )
        high, lowp = (
            (cos_even, None) if cos_odd is None else (cos_even + cos_odd, cos_even - cos_odd)
        )
        if j == 0:
            planes[0], planes[1] = high, lowp
            continue
        planes[2 * j] = high
        if j < 8:
            planes[2 * (16 - j)] = lowp
        sin_odd = total_of([scaled(math.sin(angle(j * n)), odd[n]) for n in range(1, 16, 2)])
        if j == 8:
            planes[2 * j + 1] = -sin_odd
            continue
        sin_even = total_of([scaled(math.sin(angle(j * n)), odd[n]) for n in range(2, 16, 2)])
        planes[2 * j + 1] = -(sin_even + sin_odd)
        planes[2 * (16 - j) + 1] = sin_even - sin_odd
    return planes


def backward(planes):
    real = [planes[0]] + [planes[2 * j] * 2.0 for j in range(1, 16)] + [planes[1]]
    imag = [None] + [planes[2 * j + 1] * 2.0 for j in range(1, 16)]
    steps = [None] * 32

    def put(n, cosine, sine):
        if n in (0, 16):
            steps[n] = cosine
            return
        steps[n] = cosine - sine
        steps[32 - n] = cosine + sine

    for n in range(9):
        cos_even = total_of([scaled(math.cos(angle(j * n)), real[j]) for j in range(0, 17, 2)])
        if n == 8:
            sine = total_of([scaled(math.sin(angle(j * n)), imag[j]) for j in range(1, 16, 2)])
            put(8, cos_even, sine)
            continue
        cos_odd = total_of([scaled(math.cos(angle(j * n)), real[j]) for j in range(1, 17, 2)])
        if n == 0:
            put(0, cos_even + cos_odd, None)
            put(16, cos_even - cos_odd, None)
            continue
        sin_odd = total_of([scaled(math.sin(angle(j * n)), imag[j]) for j in range(1, 16, 2)])
        sin_even = total_of([scaled(math.sin(angle(j * n)), imag[j]) for j in range(2, 16, 2)])
        put(n, cos_even + cos_odd, sin_even + sin_odd)
        put(16 - n, cos_even - cos_odd, sin_odd - sin_even)
    return steps


def slots(m):
    lane = lanes(8) % 64
    return (lane >= 8 * m) & (lane < 8 * m + 8)


def in_slots(planes, start):
    groups = []
    for g in range((len(planes) + 7) // 8):
        value = jnp.zeros((8, 128), jnp.float32)
        for m, plane in enumerate(planes[8 * g : 8 * g + 8]):
            value = jnp.where(slots(m), turn(plane, 8 * m - start), value)
        groups.append(value)
    return groups


def block_of(value, inner):
    return pack_left(jnp.where(inner == 1, half_turn(value), value), lanes(32) < 64)


def columns_in_slots(block, inner):
    result = jnp.zeros((8, 128), jnp.float32)
    for r in range(4):
        result = jnp.where(slots(r), turn(block[8 * r : 8 * r + 8], 8 * r - 56 * inner), result)
    return result


def beside_of(value, inner):
    return columns_in_slots(block_of(value, 1 - inner), inner)


def pair_fields(table, cell_class, initial, last):
    core, upper, half = place()[3:6]
    rows = pl.ds(pl.multiple_of((upper * 2 + core) * 64, 64), 64)
    cols = pl.ds(pl.multiple_of(half * 128, 128), 128)
    classes = cell_class[rows, cols]
    courant = jnp.zeros(classes.shape, jnp.float32)
    for k in range(8):
        courant = jnp.where(classes == k, table[k], courant)
    return [courant] + [initial[c, rows, cols] - ALPHA * last[c, rows, cols] for c in range(2)]


def with_start(steps, start_u, start_w):
    return [steps[0] + (start_w + start_u), steps[1] - np.float32(FACTOR) * start_u] + steps[2:]


def transform_kernel(table, cell_class, initial, last, received, planes_out, side_out):
    inner = place()[6]
    courant, start_u, start_w = (
        block_of(value, inner) for value in pair_fields(table, cell_class, initial, last)
    )
    for r in range(4):
        rows = slice(8 * r, 8 * r + 8)
        steps = []
        for t in range(8):
            part = [received[t, 32 * k + 8 * r : 32 * k + 8 * r + 8, :] for k in range(4)]
            part[0] = part[0] + received[(t + 7) % 8, 128 + 8 * r : 136 + 8 * r, :]
            steps.extend(part)
        planes = forward(with_start(steps, start_u[rows], start_w[rows]))
        for p in range(32):
            planes_out[p, rows, :] = planes[p]
        for g, value in enumerate(in_slots(planes, 56 * inner)):
            side_out[4 * g + r] = value
    planes_out[32] = courant
    side_out[16] = columns_in_slots(courant, inner)


def transform(table, cell_class, initial, last, received):
    shapes = ((33, 32, 128), (17, 8, 128))
    return pl.pallas_call(
        transform_kernel,
        in_specs=[pl.BlockSpec(memory_space=pltpu.SMEM)] + [pl.BlockSpec(memory_space=pltpu.VMEM)] * 4,
        out_specs=[pl.BlockSpec(memory_space=pltpu.VMEM)] * 2,
        out_shape=[jax.ShapeDtypeStruct(shape, jnp.float32) for shape in shapes],
        compiler_params=params(),
        name="transform",
    )(table, cell_class, initial, last, received)


def bases(inner):
    return 120 - 56 * inner, 64 + 56 * inner


def placed(value, edge, base):
    lane = lanes(8)
    return jnp.where((lane >= base) & (lane < base + 8), edge, value)


def merged(centre, side, other, bases):
    value = jnp.where(lanes(8) < 64, centre, 0.0)
    return placed(placed(value, side, bases[0]), other, bases[1])


def strips_kernel(
    table, cell_class, initial, last, received, planes, wide_out, core_out, cross_out
):
    core, _, _, inner = place()[3:7]
    low = lanes(8) < 64
    courant, start_u, start_w = (
        beside_of(value, inner) for value in pair_fields(table, cell_class, initial, last)
    )
    steps = []
    for t in range(8):
        one, two = received[t, 160:168, :], received[t, 168:176, :]
        first = one + received[(t + 7) % 8, 176:184, :]
        steps.extend([first, turn(one, -32), two, turn(two, -32)])
    beside = forward(with_start(steps, start_u, start_w)) + [courant]
    base = bases(inner)[1]
    for p in range(33):
        for r in range(8):
            shift, start = 64 * (r // 4), 8 * (r % 4)
            value = jnp.where(lanes(8) < 64, turn(planes[p, start : start + 8, :], shift), 0.0)
            wide_out[p, 8 * r : 8 * r + 8, :] = placed(value, turn(beside[p], base - shift - start), base)
    top, bottom = [], []
    for j in range(17):
        one, two = 2 * j, min(2 * j + 1, 32)
        top.append(jnp.where(low, planes[one, 0:8, :], half_turn(planes[two, 0:8, :])))
        bottom.append(jnp.where(low, half_turn(planes[one, 24:32, :]), planes[two, 24:32, :]))
    top.extend(in_slots(beside, -64))
    bottom.extend(in_slots(beside, 88))
    for i in range(22):
        core_out[i] = jnp.where(core == 0, bottom[i], top[i])
        cross_out[i] = jnp.where(core == 0, top[i], bottom[i])


def strips(table, cell_class, initial, last, received, planes):
    shapes = ((33, 64, 128), (22, 8, 128), (22, 8, 128))
    return pl.pallas_call(
        strips_kernel,
        in_specs=[pl.BlockSpec(memory_space=pltpu.SMEM)] + [pl.BlockSpec(memory_space=pltpu.VMEM)] * 5,
        out_specs=[pl.BlockSpec(memory_space=pltpu.VMEM)] * 3,
        out_shape=[jax.ShapeDtypeStruct(shape, jnp.float32) for shape in shapes],
        compiler_params=params(),
        cost_estimate=cost(2**20),
        name="strips",
    )(table, cell_class, initial, last, received, planes)


def side_matrix():
    rows = lax.broadcasted_iota(jnp.int32, (256, 128), 0) % 128
    gap = (rows - lax.broadcasted_iota(jnp.int32, (256, 128), 1)) % 128
    return jnp.where((gap == 1) | (gap == 127), 1.0, 0.0).astype(jnp.bfloat16)


def sides_by_matrix(field, matrix):
    value = jnp.concatenate(field, axis=0)
    high = value.astype(jnp.bfloat16)
    low = (value - high.astype(jnp.float32)).astype(jnp.bfloat16)
    result = jnp.dot(jnp.concatenate([high, low], axis=1), matrix, preferred_element_type=jnp.float32)
    return [result[8 * v : 8 * v + 8] for v in range(10)]


def sides_by_rotation(field):
    return [pltpu.roll(own, 1, 1) + pltpu.roll(own, 127, 1) for own in field]


def around(field, sides):
    first = pltpu.roll(field[9], 1, 0)
    last = pltpu.roll(field[0], 7, 0)
    above = [first] + field[:9]
    below = field[1:] + [last]
    return [(up + down) + side for up, side, down in zip(above, sides, below)]


def in_grid(first_row, count, col0):
    rows = lax.broadcasted_iota(jnp.int32, (count, 128), 0) + first_row
    lane = lanes(count)
    cols = jnp.where(lane >= 120, lane - 128, lane) + col0
    used = (lane < 72) | (lane >= 120)
    return used & (rows >= 0) & (rows < 1024) & (cols >= 0) & (cols < 1024)


def coefficients(lam, j, special, g_re, g_im, courant, inside):
    if special:
        inv_re = inside / (lam[0, 0] + 4.0 * courant)
        inv_im = inside / (lam[0, 1] + 4.0 * courant)
        return g_re * inv_re, g_im * inv_im, courant * inv_re, courant * inv_im
    diag_re = lam[j, 0] + 4.0 * courant
    diag_im = lam[j, 1]
    scale = inside / (diag_re * diag_re + diag_im * diag_im)
    inv_re = diag_re * scale
    inv_im = -diag_im * scale
    return (
        g_re * inv_re - g_im * inv_im,
        g_re * inv_im + g_im * inv_re,
        courant * inv_re,
        courant * inv_im,
    )


def over_frequencies(work):
    for j in range(4):
        work(j, j == 0, 0, 16 * j)

    def group(k, carry):
        for i in range(4):
            work(4 * k + i, False, k, 16 * i)
        return carry

    lax.fori_loop(1, 4, group, 0)


def widen_kernel(lam, wide, from_side, out):
    inner, _, col0 = place()[6:]
    base = bases(inner)[0]

    def extended(p, group, offset):
        parts = []
        for r in range(8):
            shift = 64 * (r // 4)
            tile, start = (16, 8 * (r % 4)) if group is None else (4 * group + r % 4, offset)
            edge = turn(from_side[tile], base - shift - start)
            parts.append(placed(wide[p, 8 * r : 8 * r + 8, :], edge, base))
        return jnp.concatenate(parts, axis=0)

    mask = in_grid(0, 64, col0)
    courant = jnp.where(mask, extended(32, None, 0), 0.0)
    inside = jnp.where(mask, 1.0, 0.0)

    def work(j, special, group, offset):
        g_re, g_im = extended(2 * j, group, offset), extended(2 * j + 1, group, offset + 8)
        for i, value in enumerate(coefficients(lam, j, special, g_re, g_im, courant, inside)):
            out[j, i, 8:72, :] = value

    over_frequencies(work)


def widen(lam, wide, from_side):
    return pl.pallas_call(
        widen_kernel,
        in_specs=[pl.BlockSpec(memory_space=pltpu.SMEM)] + [pl.BlockSpec(memory_space=pltpu.VMEM)] * 2,
        out_specs=pl.BlockSpec(memory_space=pltpu.VMEM),
        out_shape=jax.ShapeDtypeStruct((16, 4, ROOM, 128), jnp.float32),
        compiler_params=params(),
        cost_estimate=cost(2**21),
        name="widen",
    )(lam, wide, from_side)


def solve_kernel(lam, middle, from_cross, from_core, out, full, solved, wide):
    core, _, _, inner, row0, col0 = place()[3:]
    both = bases(inner)
    low = lanes(32) < 64
    matrix = side_matrix()

    def halo(index):
        one, two = from_core[index], from_cross[index]
        return jnp.where(core == 1, one, two), jnp.where(core == 1, two, one)

    def extended(pair, odd, group, offset, in_slot=0):
        centre, corners = halo(pair), halo(17 + group)
        return jnp.concatenate(
            [
                merged(
                    half_turn(centre[i]) if odd else centre[i],
                    turn(corners[i], both[0] - offset - (0 if i else 64 + in_slot)),
                    turn(corners[i], both[1] - offset - (64 if i else 0)),
                    both,
                )
                for i in range(2)
            ],
            axis=0,
        )

    mask = jnp.concatenate([in_grid(row0 - 8, 8, col0), in_grid(row0 + 64, 8, col0)], axis=0)
    courant = jnp.where(mask, extended(16, False, 4, 0, 24), 0.0)
    inside = jnp.where(mask, 1.0, 0.0)

    def work(j, special, group, offset):
        g_re, g_im = extended(j, False, group, offset), extended(j, True, group, offset + 8)
        for i, value in enumerate(coefficients(lam, j, special, g_re, g_im, courant, inside)):
            full[j, i, 0:8, :] = value[:8]
            full[j, i, 72:80, :] = value[8:]

    over_frequencies(work)

    def keep(p, slot, field):
        for v in range(10):
            wide[slot, pl.ds(v, 8, stride=10), :] = field[v]
        solved[p] = jnp.where(low, wide[slot, 8:40, :], half_turn(wide[slot, 40:72, :]))

    def swept(special, start_re, start_im, gain_re, gain_im, re, im):
        all_re = around(re, sides_by_rotation(re))
        all_im = around(im, sides_by_matrix(im, matrix))
        if special:
            return (
                [start_re[v] + gain_re[v] * all_re[v] for v in range(10)],
                [start_im[v] + gain_im[v] * all_im[v] for v in range(10)],
            )
        return (
            [start_re[v] + (gain_re[v] * all_re[v] - gain_im[v] * all_im[v]) for v in range(10)],
            [start_im[v] + (gain_re[v] * all_im[v] + gain_im[v] * all_re[v]) for v in range(10)],
        )

    def batch(k, has_special):
        sets, fields = [], []
        for i in range(BATCH):
            j = k * BATCH + i
            parts = [[full[j, a, pl.ds(v, 8, stride=10), :] for v in range(10)] for a in range(4)]
            sets.append((has_special and i == 0, *parts))
            fields.append((parts[0], parts[1]))
        for _ in range(SWEEPS - 1):
            fields = [swept(*sets[i], *fields[i]) for i in range(BATCH)]
        for i in range(BATCH):
            j = k * BATCH + i
            keep(2 * j, 2 * i, fields[i][0])
            keep(2 * j + 1, 2 * i + 1, fields[i][1])

    def later(k, carry):
        batch(k, False)
        return carry

    batch(0, True)
    lax.fori_loop(1, 16 // BATCH, later, 0)

    for r in range(4):
        part = slice(8 * r, 8 * r + 8)
        steps = backward([solved[p, part, :] for p in range(32)])
        for n in range(32):
            value = steps[n] * np.float32(math.exp(-n * DECAY) / STEPS)
            t, k = n // 4, n % 4
            out[t, 32 * k + 32 + 8 * r : 32 * k + 40 + 8 * r, :] = value
            if k == 3:
                out[(t + 1) % 8, part, :] = value * np.float32(ALPHA) if n == 31 else value


def solve(lam, middle, from_cross, from_core):
    return pl.pallas_call(
        solve_kernel,
        in_specs=[pl.BlockSpec(memory_space=pltpu.SMEM)] + [pl.BlockSpec(memory_space=pltpu.VMEM)] * 3,
        out_specs=[pl.BlockSpec(memory_space=pltpu.VMEM)] * 2,
        out_shape=[
            jax.ShapeDtypeStruct((8, 160, 128), jnp.float32),
            jax.ShapeDtypeStruct((16, 4, ROOM, 128), jnp.float32),
        ],
        input_output_aliases={1: 1},
        scratch_shapes=[
            pltpu.VMEM((32, 32, 128), jnp.float32),
            pltpu.VMEM((2 * BATCH, ROOM, 128), jnp.float32),
        ],
        compiler_params=params(),
        name="solve",
    )(lam, middle, from_cross, from_core)[0]


def finish_kernel(other, units, forcing, initial, last, *refs):
    out, held, sent = refs[-3:]
    tm, odd_x, odd_y, core = place()[:4]
    low = lanes(32) < 64
    first = jnp.where(tm == 0, 1.0, 0.0).astype(jnp.float32)
    begin = 0 if other else pl.multiple_of(64 * core, 64)
    core = core ^ other
    copies = []
    for upper in range(2):
        for half in range(2):
            cols = slice(128 * half, 128 * half + 128)
            ones, twos = (
                [units[chip, pl.ds(begin + 32 * k, 32), :] for k in range(3)]
                for chip in (chip_of(half, upper, inner, odd_x, odd_y) for inner in range(2))
            )
            for part in range(2):
                rows = slice(32 * part, 32 * part + 32)
                if part == 0:
                    values = [jnp.where(low, one, half_turn(two)) for one, two in zip(ones, twos)]
                else:
                    values = [jnp.where(low, half_turn(one), two) for one, two in zip(ones, twos)]
                before, now, after = values
                start = forcing[0, 0, upper, core, rows, cols] + first * (
                    initial[0, upper, core, rows, cols] - ALPHA * last[0, upper, core, rows, cols]
                )
                held[upper, 0, 0, rows, cols] = now
                held[upper, 0, 1, rows, cols] = after
                held[upper, 1, 0, rows, cols] = now - before - start
                held[upper, 1, 1, rows, cols] = after - now - forcing[0, 1, upper, core, rows, cols]
        copies.append(pltpu.make_async_copy(held.at[upper], out.at[:, :, upper, core], sent.at[upper]))
        copies[upper].start()
    for upper in range(2):
        copies[upper].wait()


def finish(units, forcing, initial, last, result=None):
    other = result is not None
    return pl.pallas_call(
        functools.partial(finish_kernel, int(other)),
        in_specs=[pl.BlockSpec(memory_space=pltpu.VMEM)] * 4
        + [pl.BlockSpec(memory_space=pltpu.HBM)] * other,
        out_specs=pl.BlockSpec(memory_space=pltpu.HBM),
        out_shape=jax.ShapeDtypeStruct((2, 2, 2, 2, 64, 256), jnp.float32),
        scratch_shapes=[pltpu.VMEM((2, 2, 2, 64, 256), jnp.float32), pltpu.SemaphoreType.DMA((2,))],
        input_output_aliases={4: 0} if other else {},
        compiler_params=params(),
        cost_estimate=cost(2**20),
        name="finish_other" if other else "finish_own",
    )(
        units,
        forcing.reshape(2, 2, 2, 2, 64, 256),
        initial.reshape(2, 2, 2, 64, 256),
        last.reshape(2, 2, 2, 64, 256),
        *([result] if other else []),
    )


def lam_squares():
    rows = []
    for j in range(16):
        lam = 1.0 - FACTOR * complex(math.cos(angle(j)), -math.sin(angle(j)))
        square = lam * lam
        rows.append((square.real, square.imag))
    rows[0] = ((1.0 - FACTOR) ** 2, (1.0 + FACTOR) ** 2)
    return np.array(rows, np.float32)


def chips_exchange(pieces):
    return lax.all_to_all(pieces, "tm", 0, 0, axis_index_groups=CHIPS, tiled=True)


def per_device(forcing, initial, previous_last, cell_class, courant_table):
    core = lax.axis_index("tm") & 1
    lam = jnp.asarray(lam_squares())
    theirs = prepare(forcing, 1 - core, "prepare_other")
    theirs, rest = lax.optimization_barrier((theirs, forcing))
    theirs = lax.ppermute(theirs, "tm", CORES)
    merged_units, is_upper, is_lower = lax.optimization_barrier(
        (merge(prepare(rest, core, "prepare_own"), theirs), core == 0, core == 1)
    )
    received = chips_exchange(merged_units)
    fields = (courant_table, cell_class, initial, previous_last, received)
    planes, side = transform(*fields)
    from_side = lax.ppermute(side, AXES, TO_SIDE)
    wide, to_core, to_cross = strips(*fields, planes)

    rows = from_side[:16].reshape(4, 4, 8, 128)
    low = lax.broadcasted_iota(jnp.int32, (5, 8, 128), 2) < 64

    def strip(main, is_bottom):
        side = jnp.where(is_bottom, rows[:, 3], rows[:, 0])
        side = jnp.concatenate([side, from_side[16:]], axis=0)
        return jnp.concatenate([main[:17], jnp.where(low != is_bottom, side, main[17:])], axis=0)

    from_cross = lax.ppermute(strip(to_cross, is_lower), AXES, TO_CROSS)
    from_core = lax.ppermute(strip(to_core, is_upper), AXES, TO_CORE)
    middle = widen(lam, wide, from_side)
    returned = chips_exchange(solve(lam, middle, from_cross, from_core))
    wanted = jnp.where(is_upper, returned[:, 64:160], returned[:, 0:96])
    other = lax.ppermute(wanted, "tm", CORES)
    result = finish(returned, forcing, initial, previous_last)
    result = finish(other, forcing, initial, previous_last, result)
    return result.reshape(2, 2, 256, 256)


def solution(mesh):
    in_specs = (
        P(None, "tm", "sx", "sy"),
        P(None, "sx", "sy"),
        P(None, "sx", "sy"),
        P("sx", "sy"),
        P(),
    )
    out_specs = P(None, "tm", "sx", "sy")
    return jax.shard_map(
        per_device, mesh=mesh, in_specs=in_specs, out_specs=out_specs, check_vma=False
    )
```

```python
import functools
import math

import jax
import jax.numpy as jnp
import numpy as np
from jax import lax
from jax.experimental import pallas as pl
from jax.experimental.pallas import tpu as pltpu
from jax.sharding import PartitionSpec as P

STEPS = 32
SWEEPS = 8
BATCH = 8
ROOM = 96
ALPHA = 0.1
DECAY = math.log(ALPHA) / STEPS
FACTOR = math.exp(DECAY)
AXES = ("tm", "sx", "sy")
VMEM = 16 * 2**20


def chip_of(half, upper, inner, odd_x, odd_y):
    half_y, upper_y = half ^ odd_y, upper ^ odd_x
    return (2 * half_y + (upper_y ^ half_y)) * 2 + (inner ^ half)


def device_of(row, col):
    row, col = row % 16, col % 16
    sx, upper, core = row // 4, row // 2 % 2, row % 2
    sy, half, inner = col // 4, col // 2 % 2, col % 2
    tm = chip_of(half, upper, inner, sx & 1, sy & 1) * 2 + core
    return (tm * 4 + sx) * 4 + sy


def pairs_of(move):
    return [
        (device_of(row, col), device_of(*move(row, col))) for row in range(16) for col in range(16)
    ]


def away(index):
    return index - 1 if index % 2 == 0 else index + 1


def side_of(row, col):
    return (row, away(col)) if 0 < col < 15 else (row ^ 1, col)


TO_SIDE = pairs_of(side_of)
TO_CORE = pairs_of(lambda row, col: (row ^ 1, col))
TO_CROSS = pairs_of(lambda row, col: (away(row), col))
CHIPS = [[chip * 2 + core for chip in range(8)] for core in range(2)]
CORES = [(tm, tm ^ 1) for tm in range(16)]


def lanes(rows):
    return lax.broadcasted_iota(jnp.int32, (rows, 128), 1)


def half_turn(value):
    return pltpu.roll(value, 64, 1)


def pack_left(value, low):
    return jnp.where(low, value[:32], half_turn(value[32:]))


def pack_right(value, low):
    return jnp.where(low, half_turn(value[:32]), value[32:])


def place():
    tm, sx, sy = (lax.axis_index(axis) for axis in AXES)
    odd_x, odd_y = sx & 1, sy & 1
    y, z, core = tm >> 2, tm >> 1 & 1, tm & 1
    half_y = y >> 1
    upper_y = (y & 1) ^ half_y
    half, upper = half_y ^ odd_y, upper_y ^ odd_x
    inner = z ^ half
    row0 = sx * 256 + upper * 128 + core * 64
    col0 = sy * 256 + half * 128 + inner * 64
    return tm, odd_x, odd_y, core, upper, half, inner, row0, col0


def params():
    return pltpu.CompilerParams(vmem_limit_bytes=VMEM)


def cost(size):
    return pl.CostEstimate(flops=size, bytes_accessed=size, transcendentals=0)


def turn(value, shift):
    if isinstance(shift, int):
        return pltpu.roll(value, shift % 128, 1) if shift % 128 else value
    return pltpu.roll(value, lax.rem(shift + 256, 128), 1)


def prepare_kernel(forcing, out):
    tm, odd_x, odd_y = place()[:3]
    low = lanes(32) < 64
    weight = jnp.float32(1.0)
    for bit in range(4):
        step = math.exp(DECAY * 2 ** (bit + 1))
        weight = weight * jnp.where((tm >> bit & 1) == 1, step, 1.0).astype(jnp.float32)
    weight_two = weight * np.float32(FACTOR)
    weight_three = weight * np.float32(-FACTOR * FACTOR)
    for upper in range(2):
        for half in range(2):
            cols = slice(128 * half, 128 * half + 128)
            first_u, second_u = forcing[0, 0, upper, :, cols], forcing[0, 1, upper, :, cols]
            first_w, second_w = forcing[1, 0, upper, :, cols], forcing[1, 1, upper, :, cols]
            units = (
                weight * (first_w + first_u),
                weight_two * (second_w + second_u - first_u),
                weight_three * second_u,
            )
            left = chip_of(half, upper, 0, odd_x, odd_y)
            right = chip_of(half, upper, 1, odd_x, odd_y)
            for k, unit in enumerate(units):
                rows = slice(32 * k, 32 * k + 32)
                out[left, rows, :] = pack_left(unit, low)
                out[right, rows, :] = pack_right(unit, low)


def prepare(forcing, core, name):
    rows = lax.dynamic_index_in_dim(forcing.reshape(2, 2, 2, 2, 64, 256), core, 3, keepdims=False)
    return pl.pallas_call(
        prepare_kernel,
        in_specs=[pl.BlockSpec(memory_space=pltpu.VMEM)],
        out_specs=pl.BlockSpec(memory_space=pltpu.VMEM),
        out_shape=jax.ShapeDtypeStruct((8, 96, 128), jnp.float32),
        compiler_params=params(),
        cost_estimate=cost(2**20),
        name=name,
    )(rows)


def merge_kernel(mine, received, out):
    _, odd_x, odd_y, core = place()[:4]
    is_first = core == 0
    lane8 = lanes(8) % 64
    for chip in range(8):
        for k in range(3):
            rows = slice(32 * k, 32 * k + 32)
            own, other = mine[chip, rows, :], received[chip, rows, :]
            early, late = jnp.where(is_first, own, other), jnp.where(is_first, other, own)
            if k < 2:
                out[chip, 32 * k : 32 * k + 32, :] = early
                kept = late if k == 0 else kept
                if k == 1:
                    out[chip, 96:128, :] = late
            else:
                out[chip, 64:96, :] = kept + early
                out[chip, 128:160, :] = late
    for chip in range(8):
        inner = (chip & 1) ^ (chip >> 2) ^ odd_y
        for tile in range(3):
            value = jnp.zeros((8, 128), jnp.float32)
            for m in range(8):
                k, r = (8 * tile + m) // 4, m % 4
                if k == 5:
                    break
                beside = out[chip ^ 1, 32 * k + 8 * r : 32 * k + 8 * r + 8, :]
                here = (lane8 >= 8 * m) & (lane8 < 8 * m + 8)
                value = jnp.where(here, turn(beside, 8 * m - 56 * inner), value)
            out[chip, 160 + 8 * tile : 168 + 8 * tile, :] = value


def merge(mine, received):
    return pl.pallas_call(
        merge_kernel,
        in_specs=[pl.BlockSpec(memory_space=pltpu.VMEM)] * 2,
        out_specs=pl.BlockSpec(memory_space=pltpu.VMEM),
        out_shape=jax.ShapeDtypeStruct((8, 184, 128), jnp.float32),
        compiler_params=params(),
        name="merge",
    )(mine, received)


def scaled(factor, value):
    if abs(factor) < 1e-12:
        return None
    if abs(factor - 1.0) < 1e-12:
        return value
    if abs(factor + 1.0) < 1e-12:
        return -value
    return np.float32(factor) * value


def total_of(terms):
    terms = [term for term in terms if term is not None]
    result = terms[0]
    for term in terms[1:]:
        result = result + term
    return result


def angle(index):
    return 2.0 * math.pi * (index % STEPS) / STEPS


def forward(steps):
    even = [steps[0]] + [steps[n] + steps[32 - n] for n in range(1, 16)] + [steps[16]]
    odd = [None] + [steps[n] - steps[32 - n] for n in range(1, 16)]
    planes = [None] * 32
    for j in range(9):
        cos_even = total_of([scaled(math.cos(angle(j * n)), even[n]) for n in range(0, 17, 2)])
        cos_odd = (
            None if j == 8 else total_of([scaled(math.cos(angle(j * n)), even[n]) for n in range(1, 17, 2)])
        )
        high, lowp = (
            (cos_even, None) if cos_odd is None else (cos_even + cos_odd, cos_even - cos_odd)
        )
        if j == 0:
            planes[0], planes[1] = high, lowp
            continue
        planes[2 * j] = high
        if j < 8:
            planes[2 * (16 - j)] = lowp
        sin_odd = total_of([scaled(math.sin(angle(j * n)), odd[n]) for n in range(1, 16, 2)])
        if j == 8:
            planes[2 * j + 1] = -sin_odd
            continue
        sin_even = total_of([scaled(math.sin(angle(j * n)), odd[n]) for n in range(2, 16, 2)])
        planes[2 * j + 1] = -(sin_even + sin_odd)
        planes[2 * (16 - j) + 1] = sin_even - sin_odd
    return planes


def backward(planes):
    real = [planes[0]] + [planes[2 * j] * 2.0 for j in range(1, 16)] + [planes[1]]
    imag = [None] + [planes[2 * j + 1] * 2.0 for j in range(1, 16)]
    steps = [None] * 32

    def put(n, cosine, sine):
        if n in (0, 16):
            steps[n] = cosine
            return
        steps[n] = cosine - sine
        steps[32 - n] = cosine + sine

    for n in range(9):
        cos_even = total_of([scaled(math.cos(angle(j * n)), real[j]) for j in range(0, 17, 2)])
        if n == 8:
            sine = total_of([scaled(math.sin(angle(j * n)), imag[j]) for j in range(1, 16, 2)])
            put(8, cos_even, sine)
            continue
        cos_odd = total_of([scaled(math.cos(angle(j * n)), real[j]) for j in range(1, 17, 2)])
        if n == 0:
            put(0, cos_even + cos_odd, None)
            put(16, cos_even - cos_odd, None)
            continue
        sin_odd = total_of([scaled(math.sin(angle(j * n)), imag[j]) for j in range(1, 16, 2)])
        sin_even = total_of([scaled(math.sin(angle(j * n)), imag[j]) for j in range(2, 16, 2)])
        put(n, cos_even + cos_odd, sin_even + sin_odd)
        put(16 - n, cos_even - cos_odd, sin_odd - sin_even)
    return steps


def slots(m):
    lane = lanes(8) % 64
    return (lane >= 8 * m) & (lane < 8 * m + 8)


def in_slots(planes, start):
    groups = []
    for g in range((len(planes) + 7) // 8):
        value = jnp.zeros((8, 128), jnp.float32)
        for m, plane in enumerate(planes[8 * g : 8 * g + 8]):
            value = jnp.where(slots(m), turn(plane, 8 * m - start), value)
        groups.append(value)
    return groups


def block_of(value, inner):
    return pack_left(jnp.where(inner == 1, half_turn(value), value), lanes(32) < 64)


def columns_in_slots(block, inner):
    result = jnp.zeros((8, 128), jnp.float32)
    for r in range(4):
        result = jnp.where(slots(r), turn(block[8 * r : 8 * r + 8], 8 * r - 56 * inner), result)
    return result


def beside_of(value, inner):
    return columns_in_slots(block_of(value, 1 - inner), inner)


def pair_fields(table, cell_class, initial, last):
    core, upper, half = place()[3:6]
    rows = pl.ds(pl.multiple_of((upper * 2 + core) * 64, 64), 64)
    cols = pl.ds(pl.multiple_of(half * 128, 128), 128)
    classes = cell_class[rows, cols]
    courant = jnp.zeros(classes.shape, jnp.float32)
    for k in range(8):
        courant = jnp.where(classes == k, table[k], courant)
    return [courant] + [initial[c, rows, cols] - ALPHA * last[c, rows, cols] for c in range(2)]


def with_start(steps, start_u, start_w):
    return [steps[0] + (start_w + start_u), steps[1] - np.float32(FACTOR) * start_u] + steps[2:]


def transform_kernel(table, cell_class, initial, last, received, planes_out, side_out):
    inner = place()[6]
    courant, start_u, start_w = (
        block_of(value, inner) for value in pair_fields(table, cell_class, initial, last)
    )
    for r in range(4):
        rows = slice(8 * r, 8 * r + 8)
        steps = []
        for t in range(8):
            part = [received[t, 32 * k + 8 * r : 32 * k + 8 * r + 8, :] for k in range(4)]
            part[0] = part[0] + received[(t + 7) % 8, 128 + 8 * r : 136 + 8 * r, :]
            steps.extend(part)
        planes = forward(with_start(steps, start_u[rows], start_w[rows]))
        for p in range(32):
            planes_out[p, rows, :] = planes[p]
        for g, value in enumerate(in_slots(planes, 56 * inner)):
            side_out[4 * g + r] = value
    planes_out[32] = courant
    side_out[16] = columns_in_slots(courant, inner)


def transform(table, cell_class, initial, last, received):
    shapes = ((33, 32, 128), (17, 8, 128))
    return pl.pallas_call(
        transform_kernel,
        in_specs=[pl.BlockSpec(memory_space=pltpu.SMEM)] + [pl.BlockSpec(memory_space=pltpu.VMEM)] * 4,
        out_specs=[pl.BlockSpec(memory_space=pltpu.VMEM)] * 2,
        out_shape=[jax.ShapeDtypeStruct(shape, jnp.float32) for shape in shapes],
        compiler_params=params(),
        name="transform",
    )(table, cell_class, initial, last, received)


def bases(inner):
    return 120 - 56 * inner, 64 + 56 * inner


def placed(value, edge, base):
    lane = lanes(8)
    return jnp.where((lane >= base) & (lane < base + 8), edge, value)


def merged(centre, side, other, bases):
    value = jnp.where(lanes(8) < 64, centre, 0.0)
    return placed(placed(value, side, bases[0]), other, bases[1])


def strips_kernel(
    table, cell_class, initial, last, received, planes, wide_out, core_out, cross_out
):
    core, _, _, inner = place()[3:7]
    low = lanes(8) < 64
    courant, start_u, start_w = (
        beside_of(value, inner) for value in pair_fields(table, cell_class, initial, last)
    )
    steps = []
    for t in range(8):
        one, two = received[t, 160:168, :], received[t, 168:176, :]
        first = one + received[(t + 7) % 8, 176:184, :]
        steps.extend([first, turn(one, -32), two, turn(two, -32)])
    beside = forward(with_start(steps, start_u, start_w)) + [courant]
    base = bases(inner)[1]
    for p in range(33):
        for r in range(8):
            shift, start = 64 * (r // 4), 8 * (r % 4)
            value = jnp.where(lanes(8) < 64, turn(planes[p, start : start + 8, :], shift), 0.0)
            wide_out[p, 8 * r : 8 * r + 8, :] = placed(value, turn(beside[p], base - shift - start), base)
    top, bottom = [], []
    for j in range(17):
        one, two = 2 * j, min(2 * j + 1, 32)
        top.append(jnp.where(low, planes[one, 0:8, :], half_turn(planes[two, 0:8, :])))
        bottom.append(jnp.where(low, half_turn(planes[one, 24:32, :]), planes[two, 24:32, :]))
    top.extend(in_slots(beside, -64))
    bottom.extend(in_slots(beside, 88))
    for i in range(22):
        core_out[i] = jnp.where(core == 0, bottom[i], top[i])
        cross_out[i] = jnp.where(core == 0, top[i], bottom[i])


def strips(table, cell_class, initial, last, received, planes):
    shapes = ((33, 64, 128), (22, 8, 128), (22, 8, 128))
    return pl.pallas_call(
        strips_kernel,
        in_specs=[pl.BlockSpec(memory_space=pltpu.SMEM)] + [pl.BlockSpec(memory_space=pltpu.VMEM)] * 5,
        out_specs=[pl.BlockSpec(memory_space=pltpu.VMEM)] * 3,
        out_shape=[jax.ShapeDtypeStruct(shape, jnp.float32) for shape in shapes],
        compiler_params=params(),
        cost_estimate=cost(2**20),
        name="strips",
    )(table, cell_class, initial, last, received, planes)


def side_matrix():
    rows = lax.broadcasted_iota(jnp.int32, (256, 128), 0) % 128
    gap = (rows - lax.broadcasted_iota(jnp.int32, (256, 128), 1)) % 128
    return jnp.where((gap == 1) | (gap == 127), 1.0, 0.0).astype(jnp.bfloat16)


def sides_by_matrix(field, matrix):
    value = jnp.concatenate(field, axis=0)
    high = value.astype(jnp.bfloat16)
    low = (value - high.astype(jnp.float32)).astype(jnp.bfloat16)
    result = jnp.dot(jnp.concatenate([high, low], axis=1), matrix, preferred_element_type=jnp.float32)
    return [result[8 * v : 8 * v + 8] for v in range(10)]


def sides_by_rotation(field):
    return [pltpu.roll(own, 1, 1) + pltpu.roll(own, 127, 1) for own in field]


def around(field, sides):
    first = pltpu.roll(field[9], 1, 0)
    last = pltpu.roll(field[0], 7, 0)
    above = [first] + field[:9]
    below = field[1:] + [last]
    return [(up + down) + side for up, side, down in zip(above, sides, below)]


def in_grid(first_row, count, col0):
    rows = lax.broadcasted_iota(jnp.int32, (count, 128), 0) + first_row
    lane = lanes(count)
    cols = jnp.where(lane >= 120, lane - 128, lane) + col0
    used = (lane < 72) | (lane >= 120)
    return used & (rows >= 0) & (rows < 1024) & (cols >= 0) & (cols < 1024)


def coefficients(lam, j, special, g_re, g_im, courant, inside):
    if special:
        inv_re = inside / (lam[0, 0] + 4.0 * courant)
        inv_im = inside / (lam[0, 1] + 4.0 * courant)
        return g_re * inv_re, g_im * inv_im, courant * inv_re, courant * inv_im
    diag_re = lam[j, 0] + 4.0 * courant
    diag_im = lam[j, 1]
    scale = inside / (diag_re * diag_re + diag_im * diag_im)
    inv_re = diag_re * scale
    inv_im = -diag_im * scale
    return (
        g_re * inv_re - g_im * inv_im,
        g_re * inv_im + g_im * inv_re,
        courant * inv_re,
        courant * inv_im,
    )


def over_frequencies(work):
    for j in range(4):
        work(j, j == 0, 0, 16 * j)

    def group(k, carry):
        for i in range(4):
            work(4 * k + i, False, k, 16 * i)
        return carry

    lax.fori_loop(1, 4, group, 0)


def widen_kernel(lam, wide, from_side, out):
    inner, _, col0 = place()[6:]
    base = bases(inner)[0]

    def extended(p, group, offset):
        parts = []
        for r in range(8):
            shift = 64 * (r // 4)
            tile, start = (16, 8 * (r % 4)) if group is None else (4 * group + r % 4, offset)
            edge = turn(from_side[tile], base - shift - start)
            parts.append(placed(wide[p, 8 * r : 8 * r + 8, :], edge, base))
        return jnp.concatenate(parts, axis=0)

    mask = in_grid(0, 64, col0)
    courant = jnp.where(mask, extended(32, None, 0), 0.0)
    inside = jnp.where(mask, 1.0, 0.0)

    def work(j, special, group, offset):
        g_re, g_im = extended(2 * j, group, offset), extended(2 * j + 1, group, offset + 8)
        for i, value in enumerate(coefficients(lam, j, special, g_re, g_im, courant, inside)):
            out[j, i, 8:72, :] = value

    over_frequencies(work)


def widen(lam, wide, from_side):
    return pl.pallas_call(
        widen_kernel,
        in_specs=[pl.BlockSpec(memory_space=pltpu.SMEM)] + [pl.BlockSpec(memory_space=pltpu.VMEM)] * 2,
        out_specs=pl.BlockSpec(memory_space=pltpu.VMEM),
        out_shape=jax.ShapeDtypeStruct((16, 4, ROOM, 128), jnp.float32),
        compiler_params=params(),
        cost_estimate=cost(2**21),
        name="widen",
    )(lam, wide, from_side)


def solve_kernel(lam, middle, from_cross, from_core, out, full, solved, wide):
    core, _, _, inner, row0, col0 = place()[3:]
    both = bases(inner)
    low = lanes(32) < 64
    matrix = side_matrix()

    def halo(index):
        one, two = from_core[index], from_cross[index]
        return jnp.where(core == 1, one, two), jnp.where(core == 1, two, one)

    def extended(pair, odd, group, offset, in_slot=0):
        centre, corners = halo(pair), halo(17 + group)
        return jnp.concatenate(
            [
                merged(
                    half_turn(centre[i]) if odd else centre[i],
                    turn(corners[i], both[0] - offset - (0 if i else 64 + in_slot)),
                    turn(corners[i], both[1] - offset - (64 if i else 0)),
                    both,
                )
                for i in range(2)
            ],
            axis=0,
        )

    mask = jnp.concatenate([in_grid(row0 - 8, 8, col0), in_grid(row0 + 64, 8, col0)], axis=0)
    courant = jnp.where(mask, extended(16, False, 4, 0, 24), 0.0)
    inside = jnp.where(mask, 1.0, 0.0)

    def work(j, special, group, offset):
        g_re, g_im = extended(j, False, group, offset), extended(j, True, group, offset + 8)
        for i, value in enumerate(coefficients(lam, j, special, g_re, g_im, courant, inside)):
            full[j, i, 0:8, :] = value[:8]
            full[j, i, 72:80, :] = value[8:]

    over_frequencies(work)

    def keep(p, slot, field):
        for v in range(10):
            wide[slot, pl.ds(v, 8, stride=10), :] = field[v]
        solved[p] = jnp.where(low, wide[slot, 8:40, :], half_turn(wide[slot, 40:72, :]))

    def swept(special, start_re, start_im, gain_re, gain_im, re, im):
        all_re = around(re, sides_by_rotation(re))
        all_im = around(im, sides_by_matrix(im, matrix))
        if special:
            return (
                [start_re[v] + gain_re[v] * all_re[v] for v in range(10)],
                [start_im[v] + gain_im[v] * all_im[v] for v in range(10)],
            )
        return (
            [start_re[v] + (gain_re[v] * all_re[v] - gain_im[v] * all_im[v]) for v in range(10)],
            [start_im[v] + (gain_re[v] * all_im[v] + gain_im[v] * all_re[v]) for v in range(10)],
        )

    def batch(k, has_special):
        sets, fields = [], []
        for i in range(BATCH):
            j = k * BATCH + i
            parts = [[full[j, a, pl.ds(v, 8, stride=10), :] for v in range(10)] for a in range(4)]
            sets.append((has_special and i == 0, *parts))
            fields.append((parts[0], parts[1]))
        for _ in range(SWEEPS - 1):
            fields = [swept(*sets[i], *fields[i]) for i in range(BATCH)]
        for i in range(BATCH):
            j = k * BATCH + i
            keep(2 * j, 2 * i, fields[i][0])
            keep(2 * j + 1, 2 * i + 1, fields[i][1])

    def later(k, carry):
        batch(k, False)
        return carry

    batch(0, True)
    lax.fori_loop(1, 16 // BATCH, later, 0)

    for r in range(4):
        part = slice(8 * r, 8 * r + 8)
        steps = backward([solved[p, part, :] for p in range(32)])
        for n in range(32):
            value = steps[n] * np.float32(math.exp(-n * DECAY) / STEPS)
            t, k = n // 4, n % 4
            out[t, 32 * k + 32 + 8 * r : 32 * k + 40 + 8 * r, :] = value
            if k == 3:
                out[(t + 1) % 8, part, :] = value * np.float32(ALPHA) if n == 31 else value


def solve(lam, middle, from_cross, from_core):
    return pl.pallas_call(
        solve_kernel,
        in_specs=[pl.BlockSpec(memory_space=pltpu.SMEM)] + [pl.BlockSpec(memory_space=pltpu.VMEM)] * 3,
        out_specs=[pl.BlockSpec(memory_space=pltpu.VMEM)] * 2,
        out_shape=[
            jax.ShapeDtypeStruct((8, 160, 128), jnp.float32),
            jax.ShapeDtypeStruct((16, 4, ROOM, 128), jnp.float32),
        ],
        input_output_aliases={1: 1},
        scratch_shapes=[
            pltpu.VMEM((32, 32, 128), jnp.float32),
            pltpu.VMEM((2 * BATCH, ROOM, 128), jnp.float32),
        ],
        compiler_params=params(),
        name="solve",
    )(lam, middle, from_cross, from_core)[0]


def finish_kernel(other, units, forcing, initial, last, *refs):
    out, held, sent = refs[-3:]
    tm, odd_x, odd_y, core = place()[:4]
    low = lanes(32) < 64
    first = jnp.where(tm == 0, 1.0, 0.0).astype(jnp.float32)
    begin = 0 if other else pl.multiple_of(64 * core, 64)
    core = core ^ other
    copies = []
    for upper in range(2):
        for half in range(2):
            cols = slice(128 * half, 128 * half + 128)
            ones, twos = (
                [units[chip, pl.ds(begin + 32 * k, 32), :] for k in range(3)]
                for chip in (chip_of(half, upper, inner, odd_x, odd_y) for inner in range(2))
            )
            for part in range(2):
                rows = slice(32 * part, 32 * part + 32)
                if part == 0:
                    values = [jnp.where(low, one, half_turn(two)) for one, two in zip(ones, twos)]
                else:
                    values = [jnp.where(low, half_turn(one), two) for one, two in zip(ones, twos)]
                before, now, after = values
                start = forcing[0, 0, upper, core, rows, cols] + first * (
                    initial[0, upper, core, rows, cols] - ALPHA * last[0, upper, core, rows, cols]
                )
                held[upper, 0, 0, rows, cols] = now
                held[upper, 0, 1, rows, cols] = after
                held[upper, 1, 0, rows, cols] = now - before - start
                held[upper, 1, 1, rows, cols] = after - now - forcing[0, 1, upper, core, rows, cols]
            piece = 2 * upper + half
            copies.append(
                pltpu.make_async_copy(
                    held.at[upper, :, :, :, cols], out.at[:, :, upper, core, :, cols], sent.at[piece]
                )
            )
            copies[piece].start()
    for copy in copies:
        copy.wait()


def finish(units, forcing, initial, last, result=None):
    other = result is not None
    return pl.pallas_call(
        functools.partial(finish_kernel, int(other)),
        in_specs=[pl.BlockSpec(memory_space=pltpu.VMEM)] * 4
        + [pl.BlockSpec(memory_space=pltpu.HBM)] * other,
        out_specs=pl.BlockSpec(memory_space=pltpu.HBM),
        out_shape=jax.ShapeDtypeStruct((2, 2, 2, 2, 64, 256), jnp.float32),
        scratch_shapes=[pltpu.VMEM((2, 2, 2, 64, 256), jnp.float32), pltpu.SemaphoreType.DMA((4,))],
        input_output_aliases={4: 0} if other else {},
        compiler_params=params(),
        cost_estimate=cost(2**20),
        name="finish_other" if other else "finish_own",
    )(
        units,
        forcing.reshape(2, 2, 2, 2, 64, 256),
        initial.reshape(2, 2, 2, 64, 256),
        last.reshape(2, 2, 2, 64, 256),
        *([result] if other else []),
    )


def lam_squares():
    rows = []
    for j in range(16):
        lam = 1.0 - FACTOR * complex(math.cos(angle(j)), -math.sin(angle(j)))
        square = lam * lam
        rows.append((square.real, square.imag))
    rows[0] = ((1.0 - FACTOR) ** 2, (1.0 + FACTOR) ** 2)
    return np.array(rows, np.float32)


def chips_exchange(pieces):
    return lax.all_to_all(pieces, "tm", 0, 0, axis_index_groups=CHIPS, tiled=True)


def per_device(forcing, initial, previous_last, cell_class, courant_table):
    core = lax.axis_index("tm") & 1
    lam = jnp.asarray(lam_squares())
    theirs = prepare(forcing, 1 - core, "prepare_other")
    theirs, rest = lax.optimization_barrier((theirs, forcing))
    theirs = lax.ppermute(theirs, "tm", CORES)
    merged_units, is_upper, is_lower = lax.optimization_barrier(
        (merge(prepare(rest, core, "prepare_own"), theirs), core == 0, core == 1)
    )
    received = chips_exchange(merged_units)
    fields = (courant_table, cell_class, initial, previous_last, received)
    planes, side = transform(*fields)
    from_side = lax.ppermute(side, AXES, TO_SIDE)
    wide, to_core, to_cross = strips(*fields, planes)

    rows = from_side[:16].reshape(4, 4, 8, 128)
    low = lax.broadcasted_iota(jnp.int32, (5, 8, 128), 2) < 64

    def strip(main, is_bottom):
        side = jnp.where(is_bottom, rows[:, 3], rows[:, 0])
        side = jnp.concatenate([side, from_side[16:]], axis=0)
        return jnp.concatenate([main[:17], jnp.where(low != is_bottom, side, main[17:])], axis=0)

    from_cross = lax.ppermute(strip(to_cross, is_lower), AXES, TO_CROSS)
    from_core = lax.ppermute(strip(to_core, is_upper), AXES, TO_CORE)
    middle = widen(lam, wide, from_side)
    returned = chips_exchange(solve(lam, middle, from_cross, from_core))
    wanted = jnp.where(is_upper, returned[:, 64:160], returned[:, 0:96])
    other = lax.ppermute(wanted, "tm", CORES)
    result = finish(returned, forcing, initial, previous_last)
    result = finish(other, forcing, initial, previous_last, result)
    return result.reshape(2, 2, 256, 256)


def solution(mesh):
    in_specs = (
        P(None, "tm", "sx", "sy"),
        P(None, "sx", "sy"),
        P(None, "sx", "sy"),
        P("sx", "sy"),
        P(),
    )
    out_specs = P(None, "tm", "sx", "sy")
    return jax.shard_map(
        per_device, mesh=mesh, in_specs=in_specs, out_specs=out_specs, check_vma=False
    )
```
